256 devices in a mesh: vid: 16 (over x, z_lo), aud: 8 (over y, z_hi), pair: 2 (over core).
Axes of the slice: x: 4, y: 4, z: 8 (z_hi: 2, z_lo: 4; z = z_hi * 4 + z_lo), core: 2. Of those that a mesh axis runs over, the one named last changes fastest.
Arguments:
- video_q: bfloat16 [2, 2048, 3072], P('pair', 'vid', 'aud'), may hold values from -200 to 200
- video_k: bfloat16 [2, 2048, 3072], P('pair', 'vid', 'aud'), may hold values from -7 to 7
- video_v: bfloat16 [2, 2048, 3072], P('pair', 'vid', 'aud'), may hold values from -6 to 6
- audio_q: bfloat16 [2, 1024, 3072], P('pair', 'aud'), may hold values from -200 to 200
- audio_k: bfloat16 [2, 1024, 3072], P('pair', 'aud'), may hold values from -7 to 7
- audio_v: bfloat16 [2, 1024, 3072], P('pair', 'aud'), may hold values from -6 to 6
- video_gate: float32 [3072], P('aud'), may hold values from 0.3 to 1.7
- audio_gate: float32 [3072], P('aud'), may hold values from 0.3 to 1.7
- audio_len: int32 [2], P('pair'), may hold values from 256 to 1024, as said below
- d_video_out: bfloat16 [2, 2048, 3072], P('pair', 'vid', 'aud'), may hold values from -6 to 6
- d_audio_out: bfloat16 [2, 1024, 3072], P('pair', 'vid', 'aud'), may hold values from -6 to 6
Outputs:
- video_out: bfloat16 [2, 2048, 3072], P('pair', 'vid', 'aud')
- audio_out: bfloat16 [2, 1024, 3072], P('pair', 'vid', 'aud')
- grad_video_q: bfloat16 [2, 2048, 3072], P('pair', 'vid', 'aud')
- grad_video_k: bfloat16 [2, 2048, 3072], P('pair', 'vid', 'aud')
- grad_video_v: bfloat16 [2, 2048, 3072], P('pair', 'vid', 'aud')
- grad_audio_q: bfloat16 [2, 1024, 3072], P('pair', 'vid', 'aud')
- grad_audio_k: bfloat16 [2, 1024, 3072], P('pair', 'vid', 'aud')
- grad_audio_v: bfloat16 [2, 1024, 3072], P('pair', 'vid', 'aud')
- grad_video_gate: float32 [3072], P('aud')
- grad_audio_gate: float32 [3072], P('aud')
The draws below stay inside these ranges and needn't reach their ends.
Inputs may be any that keep to these rules, and one draw needn't show every extreme that they name: `audio_len`: at least one member's audio has all 1024 tokens unpadded.
All inputs are finite; a program needn't handle non-finite values.
Results may differ from the reference program's by a relative error of at most 0.04.
Values may be sent and summed in bfloat16 or wider, within the bound.
No kernel may reach another device: no remote copies, remote signals or barrier semaphores. Data moves between devices by JAX's collectives and lax.ppermute only.
A program may use at most 128 MiB of HBM per device.

```python
import jax
import jax.numpy as jnp
from jax import lax

HEADS = 24
HEAD_DIM = 128
WIDTH = 3072
PAIRS = 2
VTOK = 2048
ATOK = 1024


def shared_keys(key, rows, salt):
    base = jnp.clip(jax.random.normal(jax.random.fold_in(key, salt), (PAIRS, rows, WIDTH), jnp.float32), -6.0, 6.0)
    twin = (jnp.arange(rows) % 16 == 1)[None, :, None]
    return jnp.where(twin, base, base)


def draw_video_k(key, part):
    result = shared_keys(key, VTOK, 11)
    return result.astype(jnp.bfloat16)


def draw_audio_k(key, part):
    result = shared_keys(key, ATOK, 12)
    return result.astype(jnp.bfloat16)


def draw_video_q(key, part):
    key = jax.random.fold_in(key, 3)
    base = jnp.clip(jax.random.normal(key, (PAIRS, VTOK, WIDTH), jnp.float32), -6.0, 6.0)
    result = base
    return result.astype(jnp.bfloat16)


def draw_audio_q(key, part):
    key = jax.random.fold_in(key, 4)
    base = jnp.clip(jax.random.normal(key, (PAIRS, ATOK, WIDTH), jnp.float32), -6.0, 6.0)
    result = base
    return result.astype(jnp.bfloat16)


def draw_audio_len(key, part):
    key = jax.random.fold_in(key, 21)
    lengths = jax.random.randint(key, (PAIRS,), ATOK // 4, ATOK + 1)
    full_member = jax.random.randint(jax.random.fold_in(key, 7), (), 0, PAIRS)
    return jnp.where(jnp.arange(PAIRS) == full_member, ATOK, lengths).astype(jnp.int32)


def shard_levels(key, extent, shards, low, high):
    loudness = 1.0
    for axis_at, blocks in shards:
        steps = jax.random.uniform(jax.random.fold_in(jax.random.fold_in(key, 6), axis_at), (blocks,), jnp.float32, low / len(shards), high / len(shards))
        loudness = loudness * jnp.repeat(jnp.exp(steps), extent[axis_at] // blocks).reshape((-1,) + (1,) * (len(extent) - 1 - axis_at))
    return loudness


def bell_draw(rng, shape, deviation, most, split=(), kind=jnp.bfloat16):
    array = jax.random.normal(rng, shape, jnp.float32) * deviation
    if len(split) > 0:
        array = shard_levels(rng, shape, split, -0.22, 0.18) * array
    return jnp.clip(array, min=-most, max=most).astype(kind)


def setup_inputs(seed: int = 0) -> dict:
    streams_of = jax.random.split(jax.random.key(seed), 12)
    return {
        "video_q": draw_video_q(jax.random.fold_in(streams_of[11], 71), 0),
        "video_k": draw_video_k(jax.random.fold_in(streams_of[11], 71), 0),
        "video_v": bell_draw(streams_of[2], (PAIRS, VTOK, WIDTH), 1.0, 6.0, ((0, 2), (1, 16), (2, 8))),
        "audio_q": draw_audio_q(jax.random.fold_in(streams_of[11], 71), 0),
        "audio_k": draw_audio_k(jax.random.fold_in(streams_of[11], 71), 0),
        "audio_v": bell_draw(streams_of[5], (PAIRS, ATOK, WIDTH), 1.0, 6.0, ((0, 2), (1, 8))),
        "video_gate": jnp.clip(0.3 + 1.40000004 * jax.random.uniform(streams_of[6], (WIDTH,), jnp.float32) ** shard_levels(streams_of[6], (WIDTH,), ((0, 8),), -0.2, 0.2), 0.3, 1.7),
        "audio_gate": jnp.clip(0.3 + 1.40000004 * jax.random.uniform(streams_of[7], (WIDTH,), jnp.float32) ** shard_levels(streams_of[7], (WIDTH,), ((0, 8),), -0.2, 0.2), 0.3, 1.7),
        "audio_len": draw_audio_len(jax.random.fold_in(streams_of[11], 71), 0),
        "d_video_out": bell_draw(streams_of[9], (PAIRS, VTOK, WIDTH), 1.0, 6.0, ((0, 2), (1, 16), (2, 8))),
        "d_audio_out": bell_draw(streams_of[10], (PAIRS, ATOK, WIDTH), 1.0, 6.0, ((0, 2), (1, 16), (2, 8))),
    }


def split_heads(matrix):
    members, rows = matrix.shape[0], matrix.shape[1]
    return matrix.reshape(members, rows, HEADS, HEAD_DIM).transpose(0, 2, 1, 3).reshape(members * HEADS, rows, HEAD_DIM)


def join_heads(stacked):
    rows = stacked.shape[1]
    return stacked.reshape(PAIRS, HEADS, rows, HEAD_DIM).transpose(0, 2, 1, 3).reshape(PAIRS, rows, HEADS * HEAD_DIM)


def logits(queries, keys, allowed):
    raw = jnp.dot(queries.astype(jnp.float32), keys.astype(jnp.float32).T, preferred_element_type=jnp.float32) * HEAD_DIM ** -0.5
    return jnp.where(allowed[None, :], raw, -1e30)


def head_forward(items):
    queries, keys, values, allowed = items
    scored = logits(queries, keys, allowed)
    peak = jnp.max(scored, axis=-1)
    expon = jnp.exp(scored - peak[:, None])
    total = jnp.sum(expon, axis=-1)
    weights = (expon / total[:, None]).astype(jnp.bfloat16)
    output = jnp.dot(weights.astype(jnp.float32), values.astype(jnp.float32), preferred_element_type=jnp.float32)
    return output, peak + jnp.log(total)


def head_backward(items):
    queries, keys, values, allowed, upstream, delta, log_total = items
    scored = logits(queries, keys, allowed)
    probs = jnp.exp(scored - log_total[:, None])
    up_wide = upstream.astype(jnp.float32)
    grad_values = jnp.dot(probs.astype(jnp.bfloat16).astype(jnp.float32).T, up_wide, preferred_element_type=jnp.float32)
    grad_probs = jnp.dot(up_wide, values.astype(jnp.float32).T, preferred_element_type=jnp.float32)
    grad_scores = (probs * (grad_probs - delta[:, None])).astype(jnp.bfloat16).astype(jnp.float32)
    scale = HEAD_DIM ** -0.5
    grad_queries = jnp.dot(grad_scores, keys.astype(jnp.float32), preferred_element_type=jnp.float32) * scale
    grad_keys = jnp.dot(grad_scores.T, queries.astype(jnp.float32), preferred_element_type=jnp.float32) * scale
    return grad_queries, grad_keys, grad_values


def run_pass(queries, keys, values, allowed, upstream):
    split_q, split_k, split_v = split_heads(queries), split_heads(keys), split_heads(values)
    output, log_total = lax.map(head_forward, (split_q, split_k, split_v, allowed))
    split_up = split_heads(upstream)
    delta = jnp.sum(split_up.astype(jnp.float32) * output, axis=-1)
    grads = lax.map(head_backward, (split_q, split_k, split_v, allowed, split_up, delta, log_total))
    return join_heads(output), join_heads(grads[0]), join_heads(grads[1]), join_heads(grads[2])


def reference(video_q, video_k, video_v, audio_q, audio_k, audio_v, video_gate, audio_gate, audio_len, d_video_out, d_audio_out):
    vid_rows = video_k.shape[1]
    aud_rows = audio_k.shape[1]
    vid_allowed = jnp.ones((PAIRS * HEADS, vid_rows), dtype=bool)
    positions = jnp.arange(aud_rows, dtype=jnp.int32)
    aud_allowed = jnp.repeat(positions[None, :] < audio_len[:, None], HEADS, axis=0)
    up_vc = (video_gate * d_video_out.astype(jnp.float32)).astype(jnp.bfloat16)
    up_ac = (audio_gate * d_audio_out.astype(jnp.float32)).astype(jnp.bfloat16)
    out_vs, gq_vs, gk_vs, gv_vs = run_pass(video_q, video_k, video_v, vid_allowed, d_video_out)
    out_vc, gq_vc, gk_vc, gv_vc = run_pass(video_q, audio_k, audio_v, aud_allowed, up_vc)
    out_as, gq_as, gk_as, gv_as = run_pass(audio_q, audio_k, audio_v, aud_allowed, d_audio_out)
    out_ac, gq_ac, gk_ac, gv_ac = run_pass(audio_q, video_k, video_v, vid_allowed, up_ac)
    video_out = (out_vs + video_gate * out_vc).astype(jnp.bfloat16)
    audio_out = (out_as + audio_gate * out_ac).astype(jnp.bfloat16)
    grad_video_q = (gq_vs + gq_vc).astype(jnp.bfloat16)
    grad_audio_q = (gq_as + gq_ac).astype(jnp.bfloat16)
    grad_video_k = (gk_vs + gk_ac).astype(jnp.bfloat16)
    grad_video_v = (gv_vs + gv_ac).astype(jnp.bfloat16)
    grad_audio_k = (gk_vc + gk_as).astype(jnp.bfloat16)
    grad_audio_v = (gv_vc + gv_as).astype(jnp.bfloat16)
    grad_video_gate = jnp.sum(d_video_out.astype(jnp.float32) * out_vc, axis=(0, 1))
    grad_audio_gate = jnp.sum(d_audio_out.astype(jnp.float32) * out_ac, axis=(0, 1))
    return (video_out, audio_out, grad_video_q, grad_video_k, grad_video_v, grad_audio_q, grad_audio_k, grad_audio_v, grad_video_gate, grad_audio_gate)
```

```python
import jax
import jax.numpy as jnp
from jax import lax
from jax.experimental import pallas as pl
from jax.experimental.pallas import tpu as pltpu
from jax.sharding import PartitionSpec as P

HEAD_DIM = 128
SCALE = HEAD_DIM ** (-0.5)
SIDE = 4
F32 = jnp.float32
BF16 = jnp.bfloat16

ALONG_X = [[x * SIDE + z for x in range(SIDE)] for z in range(SIDE)]
ALONG_Z = [[x * SIDE + z for z in range(SIDE)] for x in range(SIDE)]


def rows_of(ref, part, video_rows):
    block = ref[:, part]
    count, rows, width = block.shape
    video = block[:, :video_rows].reshape(count * video_rows, width)
    audio = block[:, video_rows:].reshape(count * (rows - video_rows), width)
    return video, audio


def gated(rows, gate_row):
    return (gate_row * rows.astype(F32)).astype(BF16)


def nt(a, b):
    return lax.dot_general(a, b, (((1,), (1,)), ((), ())), preferred_element_type=F32)


def nn(a, b):
    return lax.dot_general(a, b, (((1,), (0,)), ((), ())), preferred_element_type=F32)


def upstreams(q_ref, gates_ref, video_rows):
    up_video, up_audio = rows_of(q_ref, 1, video_rows)
    on_video_keys = jnp.concatenate([up_video, gated(up_audio, gates_ref[1:2, :])], axis=0)
    on_audio_keys = jnp.concatenate([gated(up_video, gates_ref[0:1, :]), up_audio], axis=0)
    return on_video_keys, on_audio_keys


def forward_kernel(video_rows, limit_ref, q_ref, k_ref, gates_ref, e_ref, o_ref, stats_ref):
    queries = jnp.concatenate(rows_of(q_ref, 0, video_rows), axis=0)
    keys = rows_of(k_ref, 0, video_rows)
    values = rows_of(k_ref, 1, video_rows)
    ups = upstreams(q_ref, gates_ref, video_rows)
    split = keys[0].shape[0]
    stats = []
    for part in (0, 1):
        raw = nt(keys[part], queries)
        if part == 1:
            position = lax.broadcasted_iota(jnp.int32, raw.shape, 0)
            raw = jnp.where(position < limit_ref[0], raw, -1e30)
        peak = jnp.max(raw, axis=0, keepdims=True)
        expon = jnp.exp((raw - peak) * SCALE)
        total = jnp.sum(expon, axis=0, keepdims=True)
        expon = expon.astype(BF16)
        if part == 0:
            e_ref[0, :split] = expon
        else:
            e_ref[0, split:] = expon
        output = nn(values[part].T, expon)
        o_ref[0, part] = output
        weighted = jnp.sum(ups[part].astype(F32).T * output, axis=0, keepdims=True)
        stats.append((peak, total, weighted))
    stats_ref[0] = jnp.concatenate(
        [stats[0][0], stats[1][0], stats[0][1], stats[1][1], stats[0][2], stats[1][2], stats[0][0], stats[1][0]],
        axis=0,
    )


def backward_kernel(
    video_rows, q_ref, k_ref, gates_ref, columns_ref, e_ref, o_ref, own_ref, all_ref, qside_ref, kside_ref, gate_ref
):
    queries = jnp.concatenate(rows_of(q_ref, 0, video_rows), axis=0)
    keys = rows_of(k_ref, 0, video_rows)
    values = rows_of(k_ref, 1, video_rows)
    ups = upstreams(q_ref, gates_ref, video_rows)
    split = keys[0].shape[0]
    count = q_ref.shape[0]
    video_q = count * video_rows
    peers = all_ref.shape[0]
    grad_queries = None
    outputs = []
    for part in (0, 1):
        peak = all_ref[0, 0, part : part + 1]
        for peer in range(1, peers):
            peak = jnp.maximum(peak, all_ref[peer, 0, part : part + 1])
        total = jnp.zeros_like(peak)
        weighted = jnp.zeros_like(peak)
        for peer in range(peers):
            weight = jnp.exp((all_ref[peer, 0, part : part + 1] - peak) * SCALE)
            total += weight * all_ref[peer, 0, part + 2 : part + 3]
            weighted += weight * all_ref[peer, 0, part + 4 : part + 5]
        delta = weighted / total
        factor = jnp.exp((own_ref[0, part : part + 1] - peak) * SCALE) / total
        expon = e_ref[0, :split] if part == 0 else e_ref[0, split:]
        probs = expon.astype(F32) * factor
        grad_values = nn(probs.astype(BF16), ups[part])
        grad_probs = nt(values[part], ups[part])
        grad_scores = (probs * (grad_probs - delta)).astype(BF16)
        grad_keys = nn(grad_scores, queries) * SCALE
        term = nn(keys[part].T, grad_scores)
        grad_queries = term if grad_queries is None else grad_queries + term
        outputs.append(o_ref[0, part] * factor)
        lo, hi = (0, video_rows) if part == 0 else (video_rows, kside_ref.shape[2])
        kside_ref[:, 0, lo:hi] = grad_keys.astype(BF16).reshape(count, hi - lo, HEAD_DIM)
        kside_ref[:, 1, lo:hi] = grad_values.astype(BF16).reshape(count, hi - lo, HEAD_DIM)
    video_gate = columns_ref[:, 0:1]
    audio_gate = columns_ref[:, 1:2]
    cross_video = outputs[1][:, :video_q]
    cross_audio = outputs[0][:, video_q:]
    merged = jnp.concatenate(
        [outputs[0][:, :video_q] + video_gate * cross_video, outputs[1][:, video_q:] + audio_gate * cross_audio], axis=1
    )
    up_video, up_audio = rows_of(q_ref, 1, video_rows)
    video_sum = jnp.sum(up_video.astype(F32).T * cross_video, axis=1, keepdims=True)
    audio_sum = jnp.sum(up_audio.astype(F32).T * cross_audio, axis=1, keepdims=True)
    sums = jnp.concatenate(
        [jnp.broadcast_to(video_sum, (HEAD_DIM, 8)), jnp.broadcast_to(audio_sum, (HEAD_DIM, HEAD_DIM - 8))], axis=1
    )
    gate_ref[...] = sums.T[0:16]
    merged = merged.T.astype(BF16)
    grad_queries = (grad_queries.T * SCALE).astype(BF16)
    for index, array in ((0, merged), (1, grad_queries)):
        qside_ref[:, index, :video_rows] = array[:video_q].reshape(count, video_rows, HEAD_DIM)
        qside_ref[:, index, video_rows:] = array[video_q:].reshape(count, -1, HEAD_DIM)


def attention_forward(limit, qside, kside, gates, video_rows):
    count, _, rows, width = qside.shape
    heads = width // HEAD_DIM
    total = count * rows
    block = pl.BlockSpec((count, 2, rows, HEAD_DIM), lambda h: (0, 0, 0, h))
    return pl.pallas_call(
        lambda *refs: forward_kernel(video_rows, *refs),
        grid=(heads,),
        in_specs=[
            pl.BlockSpec(memory_space=pltpu.SMEM),
            block,
            block,
            pl.BlockSpec((2, HEAD_DIM), lambda h: (0, h)),
        ],
        out_specs=[
            pl.BlockSpec((1, total, total), lambda h: (h, 0, 0)),
            pl.BlockSpec((1, 2, HEAD_DIM, total), lambda h: (h, 0, 0, 0)),
            pl.BlockSpec((1, 8, total), lambda h: (h, 0, 0)),
        ],
        out_shape=[
            jax.ShapeDtypeStruct((heads, total, total), BF16),
            jax.ShapeDtypeStruct((heads, 2, HEAD_DIM, total), F32),
            jax.ShapeDtypeStruct((heads, 8, total), F32),
        ],
        compiler_params=pltpu.CompilerParams(vmem_limit_bytes=48 * 2**20),
        name="attention_forward",
    )(limit, qside, kside, gates)


def attention_backward(qside, kside, gates, expon, outputs, stats, stats_all, video_rows):
    count, _, rows, width = qside.shape
    heads = width // HEAD_DIM
    total = count * rows
    block = pl.BlockSpec((count, 2, rows, HEAD_DIM), lambda h: (0, 0, 0, h))
    return pl.pallas_call(
        lambda *refs: backward_kernel(video_rows, *refs),
        grid=(heads,),
        in_specs=[
            block,
            block,
            pl.BlockSpec((2, HEAD_DIM), lambda h: (0, h)),
            pl.BlockSpec((HEAD_DIM, 2), lambda h: (h, 0)),
            pl.BlockSpec((1, total, total), lambda h: (h, 0, 0)),
            pl.BlockSpec((1, 2, HEAD_DIM, total), lambda h: (h, 0, 0, 0)),
            pl.BlockSpec((1, 8, total), lambda h: (h, 0, 0)),
            pl.BlockSpec((stats_all.shape[0], 1, 8, total), lambda h: (0, h, 0, 0)),
        ],
        out_specs=[block, block, pl.BlockSpec((16, HEAD_DIM), lambda h: (0, h))],
        out_shape=[
            jax.ShapeDtypeStruct(qside.shape, BF16),
            jax.ShapeDtypeStruct(kside.shape, BF16),
            jax.ShapeDtypeStruct((16, width), F32),
        ],
        compiler_params=pltpu.CompilerParams(vmem_limit_bytes=56 * 2**20),
        name="attention_backward",
    )(qside, kside, gates, gates.T, expon, outputs, stats, stats_all)


def own_audio(audio, vid, aud, columns, rows):
    count = lax.axis_size("aud")
    sends = [
        lax.dynamic_slice(array[0], ((vid % 2) * rows, (vid // 2) * columns), (rows, columns)) for array in audio
    ]
    pairs = [
        (v * count + a, (2 * a + v % 2) * count + v // 2) for v in range(lax.axis_size("vid")) for a in range(count)
    ]
    return lax.ppermute(jnp.stack(sends), ("vid", "aud"), pairs)


def shards(
    video_q, video_k, video_v, audio_q, audio_k, audio_v, video_gate, audio_gate, audio_len, d_video_out, d_audio_out
):
    vid = lax.axis_index("vid")
    aud = lax.axis_index("aud")
    video_rows, columns = video_q.shape[1:]
    audio_rows = d_audio_out.shape[1]
    aud_q, aud_k, aud_v = own_audio((audio_q, audio_k, audio_v), vid, aud, columns, audio_rows)
    qside = jnp.stack(
        [jnp.concatenate([video_q[0], aud_q], axis=0), jnp.concatenate([d_video_out[0], d_audio_out[0]], axis=0)]
    )
    kside = jnp.stack(
        [jnp.concatenate([video_k[0], aud_k], axis=0), jnp.concatenate([video_v[0], aud_v], axis=0)]
    )
    qside = lax.all_gather(qside, "vid", axis=0, axis_index_groups=ALONG_X)
    kside = lax.all_gather(kside, "vid", axis=0, axis_index_groups=ALONG_Z)
    gates = jnp.stack([video_gate, audio_gate])
    limit = audio_len - (vid // SIDE) * (SIDE * audio_rows)
    expon, outputs, stats = attention_forward(limit, qside, kside, gates, video_rows)
    stats_all = lax.all_gather(stats, "vid", axis=0, axis_index_groups=ALONG_X)
    qside, kside, gate_part = attention_backward(
        qside, kside, gates, expon, outputs, stats, stats_all, video_rows
    )
    gate_all = lax.all_gather(gate_part[7:9], ("vid", "pair"), axis=0)
    gate_grad = jnp.sum(gate_all, axis=0)
    qside = lax.all_to_all(qside, "vid", 0, 0, axis_index_groups=ALONG_X, tiled=True)
    kside = lax.all_to_all(kside, "vid", 0, 0, axis_index_groups=ALONG_Z, tiled=True)
    qside = jnp.sum(qside.astype(F32), axis=0).astype(BF16)
    kside = jnp.sum(kside.astype(F32), axis=0).astype(BF16)
    return (
        qside[0:1, :video_rows],
        qside[0:1, video_rows:],
        qside[1:2, :video_rows],
        kside[0:1, :video_rows],
        kside[1:2, :video_rows],
        qside[1:2, video_rows:],
        kside[0:1, video_rows:],
        kside[1:2, video_rows:],
        gate_grad[0],
        gate_grad[1],
    )


def solution(mesh):
    split = P("pair", "vid", "aud")
    rows = P("pair", "aud", None)
    return jax.shard_map(
        shards,
        mesh=mesh,
        in_specs=(split, split, split, rows, rows, rows, P("aud"), P("aud"), P("pair"), split, split),
        out_specs=(split,) * 8 + (P("aud"), P("aud")),
        check_vma=False,
    )
```

```python
import functools

import jax
import jax.numpy as jnp
from jax import lax
from jax.experimental import pallas as pl
from jax.experimental.pallas import tpu as pltpu
from jax.sharding import PartitionSpec as P

HEAD_DIM = 128
SCALE = HEAD_DIM ** (-0.5)
SIDE = 4
F32 = jnp.float32
BF16 = jnp.bfloat16
VIDEO, AUDIO = 0, 1


def along_x(array, shift):
    pairs = [(x * SIDE + z, (x + shift) % SIDE * SIDE + z) for x in range(SIDE) for z in range(SIDE)]
    return lax.ppermute(array, "vid", pairs)


def along_z(array, shift):
    pairs = [(x * SIDE + z, x * SIDE + (z + shift) % SIDE) for x in range(SIDE) for z in range(SIDE)]
    return lax.ppermute(array, "vid", pairs)


def gathered(array, along):
    return [array] + [along(array, shift) for shift in range(1, SIDE)]


def returned(parts, along):
    return [parts[0]] + [along(parts[place], SIDE - place) for place in range(1, SIDE)]


def nt(a, b):
    return lax.dot_general(a, b, (((1,), (1,)), ((), ())), preferred_element_type=F32)


def nn(a, b):
    return lax.dot_general(a, b, (((1,), (0,)), ((), ())), preferred_element_type=F32)


def joined(refs, index):
    return jnp.concatenate([ref[index] for ref in refs], axis=0)


def gated(rows, gate_row):
    return (gate_row * rows.astype(F32)).astype(BF16)


def upstreams(q_refs, gates_ref):
    up_video, up_audio = joined(q_refs[VIDEO], 1), joined(q_refs[AUDIO], 1)
    return (
        jnp.concatenate([up_video, gated(up_audio, gates_ref[1:2, :])], axis=0),
        jnp.concatenate([gated(up_video, gates_ref[0:1, :]), up_audio], axis=0),
    )


def sides(refs):
    return (refs[0:4], refs[4:8]), (refs[8:12], refs[12:16])


def forward_kernel(*refs):
    (q_refs, k_refs), (limit_ref, gates_ref, e_ref, o_ref, video_ref, audio_ref) = sides(refs[:16]), refs[16:]
    queries = jnp.concatenate([joined(q_refs[VIDEO], 0), joined(q_refs[AUDIO], 0)], axis=0)
    ups = upstreams(q_refs, gates_ref)
    split = sum(ref.shape[1] for ref in k_refs[VIDEO])
    video_q = sum(ref.shape[1] for ref in q_refs[VIDEO])
    stats = []
    for part in (VIDEO, AUDIO):
        raw = nt(joined(k_refs[part], 0), queries)
        if part == AUDIO:
            rows = k_refs[AUDIO][0].shape[1]
            position = lax.broadcasted_iota(jnp.int32, (rows, raw.shape[1]), 0)
            raw = jnp.concatenate(
                [
                    jnp.where(position < limit_ref[place], raw[place * rows : (place + 1) * rows], -1e30)
                    for place in range(SIDE)
                ],
                axis=0,
            )
        peak = jnp.max(raw, axis=0, keepdims=True)
        expon = jnp.exp((raw - peak) * SCALE)
        total = jnp.sum(expon, axis=0, keepdims=True)
        expon = expon.astype(BF16)
        if part == VIDEO:
            e_ref[0, :split] = expon
        else:
            e_ref[0, split:] = expon
        output = nn(joined(k_refs[part], 1).T, expon)
        o_ref[0, part] = output
        weighted = jnp.sum(ups[part].astype(F32).T * output, axis=0, keepdims=True)
        stats.append((peak, total, weighted))
    rows = [stats[part][kind] for kind in range(3) for part in (VIDEO, AUDIO)]
    stats = jnp.concatenate(rows + rows[:2], axis=0)
    video_ref[0] = stats[:, :video_q]
    audio_ref[0] = stats[:, video_q:]


def backward_kernel(*refs):
    q_refs, k_refs = sides(refs[:16])
    gates_ref, columns_ref, e_ref, o_ref = refs[16:20]
    video_stats, audio_stats = refs[20:24], refs[24:28]
    q_outs, k_outs, gate_ref = refs[28:32], refs[32:36], refs[36]
    queries = jnp.concatenate([joined(q_refs[VIDEO], 0), joined(q_refs[AUDIO], 0)], axis=0)
    ups = upstreams(q_refs, gates_ref)
    split = sum(ref.shape[1] for ref in k_refs[VIDEO])
    video_q = sum(ref.shape[1] for ref in q_refs[VIDEO])
    video_rows, audio_rows = q_refs[VIDEO][0].shape[1], q_refs[AUDIO][0].shape[1]
    stats = []
    for shift in range(SIDE):
        video, audio = video_stats[shift][0], audio_stats[shift][0]
        if shift:
            video = pltpu.roll(video, shift * video_rows, 1)
            audio = pltpu.roll(audio, shift * audio_rows, 1)
        stats.append(jnp.concatenate([video, audio], axis=1))
    grad_queries = None
    outputs = []
    for part in (VIDEO, AUDIO):
        peaks = [array[part : part + 1] for array in stats]
        peak = functools.reduce(jnp.maximum, peaks)
        weights = [jnp.exp((local - peak) * SCALE) for local in peaks]
        total = sum(weight * array[part + 2 : part + 3] for weight, array in zip(weights, stats))
        delta = sum(weight * array[part + 4 : part + 5] for weight, array in zip(weights, stats)) / total
        factor = weights[0] / total
        expon = e_ref[0, :split] if part == VIDEO else e_ref[0, split:]
        probs = expon.astype(F32) * factor
        grad_values = nn(probs.astype(BF16), ups[part]).astype(BF16)
        grad_probs = nt(joined(k_refs[part], 1), ups[part])
        grad_scores = (probs * (grad_probs - delta)).astype(BF16)
        grad_keys = (nn(grad_scores, queries) * SCALE).astype(BF16)
        term = nn(joined(k_refs[part], 0).T, grad_scores)
        grad_queries = term if grad_queries is None else grad_queries + term
        outputs.append(o_ref[0, part] * factor)
        rows, first = (video_rows, 0) if part == VIDEO else (audio_rows, video_rows)
        for place in range(SIDE):
            taken = slice(place * rows, (place + 1) * rows)
            k_outs[place][0, first : first + rows] = grad_keys[taken]
            k_outs[place][1, first : first + rows] = grad_values[taken]
    cross_video = outputs[AUDIO][:, :video_q]
    cross_audio = outputs[VIDEO][:, video_q:]
    merged = jnp.concatenate(
        [
            outputs[VIDEO][:, :video_q] + columns_ref[:, 0:1] * cross_video,
            outputs[AUDIO][:, video_q:] + columns_ref[:, 1:2] * cross_audio,
        ],
        axis=1,
    )
    video_sum = jnp.sum(joined(q_refs[VIDEO], 1).astype(F32).T * cross_video, axis=1, keepdims=True)
    audio_sum = jnp.sum(joined(q_refs[AUDIO], 1).astype(F32).T * cross_audio, axis=1, keepdims=True)
    sums = jnp.concatenate(
        [jnp.broadcast_to(video_sum, (HEAD_DIM, 4)), jnp.broadcast_to(audio_sum, (HEAD_DIM, HEAD_DIM - 4))], axis=1
    )
    gate_ref[...] = sums.T[0:8]
    for index, array in ((0, merged.T.astype(BF16)), (1, (grad_queries.T * SCALE).astype(BF16))):
        for place in range(SIDE):
            q_outs[place][index, :video_rows] = array[place * video_rows : (place + 1) * video_rows]
            first = video_q + place * audio_rows
            q_outs[place][index, video_rows:] = array[first : first + audio_rows]


def chunk_spec(rows):
    return pl.BlockSpec((2, rows, HEAD_DIM), lambda h: (0, 0, h))


def head_spec(*shape):
    return pl.BlockSpec((1, *shape), lambda h: (h,) + (0,) * len(shape))


def attention_forward(sides_in, limits, gates):
    video_rows, audio_rows = sides_in[0].shape[1], sides_in[4].shape[1]
    heads = gates.shape[1] // HEAD_DIM
    video, audio = SIDE * video_rows, SIDE * audio_rows
    total = video + audio
    shapes = [((total, total), BF16), ((2, HEAD_DIM, total), F32), ((8, video), F32), ((8, audio), F32)]
    return pl.pallas_call(
        forward_kernel,
        grid=(heads,),
        in_specs=[chunk_spec(array.shape[1]) for array in sides_in]
        + [pl.BlockSpec(memory_space=pltpu.SMEM), pl.BlockSpec((2, HEAD_DIM), lambda h: (0, h))],
        out_specs=[head_spec(*shape) for shape, _ in shapes],
        out_shape=[jax.ShapeDtypeStruct((heads, *shape), kind) for shape, kind in shapes],
        compiler_params=pltpu.CompilerParams(vmem_limit_bytes=48 * 2**20),
        name="attention_forward",
    )(*sides_in, limits, gates)


def attention_backward(sides_in, gates, expon, outputs, video_stats, audio_stats):
    video_rows, audio_rows = sides_in[0].shape[1], sides_in[4].shape[1]
    width = gates.shape[1]
    rows = video_rows + audio_rows
    given = [expon, outputs, *video_stats, *audio_stats]
    outs = pl.pallas_call(
        backward_kernel,
        grid=(width // HEAD_DIM,),
        in_specs=[chunk_spec(array.shape[1]) for array in sides_in]
        + [pl.BlockSpec((2, HEAD_DIM), lambda h: (0, h)), pl.BlockSpec((HEAD_DIM, 2), lambda h: (h, 0))]
        + [head_spec(*array.shape[1:]) for array in given],
        out_specs=[chunk_spec(rows)] * 8 + [pl.BlockSpec((8, HEAD_DIM), lambda h: (0, h))],
        out_shape=[jax.ShapeDtypeStruct((2, rows, width), BF16)] * 8 + [jax.ShapeDtypeStruct((8, width), F32)],
        compiler_params=pltpu.CompilerParams(vmem_limit_bytes=56 * 2**20),
        name="attention_backward",
    )(*sides_in, gates, gates.T, *given)
    return outs[0:4], outs[4:8], outs[8]


def own_audio(audio, vid, columns, rows):
    count = lax.axis_size("aud")
    sends = [
        lax.dynamic_slice(array[0], ((vid % 2) * rows, (vid // 2) * columns), (rows, columns)) for array in audio
    ]
    pairs = [
        (v * count + a, (2 * a + v % 2) * count + v // 2) for v in range(lax.axis_size("vid")) for a in range(count)
    ]
    return lax.ppermute(jnp.stack(sends), ("vid", "aud"), pairs)


def summed(parts):
    return sum(part.astype(F32) for part in parts)


def shards(
    video_q, video_k, video_v, audio_q, audio_k, audio_v, video_gate, audio_gate, audio_len, d_video_out, d_audio_out
):
    vid = lax.axis_index("vid")
    video_rows, columns = video_q.shape[1:]
    audio_rows = d_audio_out.shape[1]
    aud_q, aud_k, aud_v = own_audio((audio_q, audio_k, audio_v), vid, columns, audio_rows)
    video_queries = gathered(jnp.concatenate([video_q, d_video_out]), along_x)
    video_keys = gathered(jnp.concatenate([video_k, video_v]), along_z)
    audio_queries = gathered(jnp.stack([aud_q, d_audio_out[0]]), along_x)
    audio_keys = gathered(jnp.stack([aud_k, aud_v]), along_z)
    sides_in = (*video_queries, *audio_queries, *video_keys, *audio_keys)
    gates = jnp.stack([video_gate, audio_gate])
    column, row = vid // SIDE, vid % SIDE
    limits = jnp.stack(
        [audio_len[0] - (column * SIDE + (row - place) % SIDE) * audio_rows for place in range(SIDE)]
    )
    expon, outputs, video_stats, audio_stats = attention_forward(sides_in, limits, gates)
    video_stats = gathered(video_stats, along_x)
    audio_stats = gathered(audio_stats, along_x)
    q_parts, k_parts, gate = attention_backward(sides_in, gates, expon, outputs, video_stats, audio_stats)
    k_side = summed(returned(k_parts, along_z)).astype(BF16)
    q_side = summed(returned(q_parts, along_x)).astype(BF16)
    gate = sum(gathered(gate, along_x))
    gate = sum(gathered(gate, along_z))
    gate = gate + lax.ppermute(gate, "pair", [(0, 1), (1, 0)])
    return (
        q_side[0:1, :video_rows],
        q_side[0:1, video_rows:],
        q_side[1:2, :video_rows],
        k_side[0:1, :video_rows],
        k_side[1:2, :video_rows],
        q_side[1:2, video_rows:],
        k_side[0:1, video_rows:],
        k_side[1:2, video_rows:],
        gate[0],
        gate[7],
    )


def solution(mesh):
    split = P("pair", "vid", "aud")
    rows = P("pair", "aud", None)
    return jax.shard_map(
        shards,
        mesh=mesh,
        in_specs=(split, split, split, rows, rows, rows, P("aud"), P("aud"), P("pair"), split, split),
        out_specs=(split,) * 8 + (P("aud"), P("aud")),
        check_vma=False,
    )
```

```python
import functools

import jax
import jax.numpy as jnp
from jax import lax
from jax.experimental import pallas as pl
from jax.experimental.pallas import tpu as pltpu
from jax.sharding import PartitionSpec as P

HEAD_DIM = 128
SCALE = HEAD_DIM ** (-0.5)
SIDE = 4
F32 = jnp.float32
BF16 = jnp.bfloat16
VIDEO, AUDIO = 0, 1
GATE_ROWS = 16


def along_x(array, shift):
    pairs = [(x * SIDE + z, (x + shift) % SIDE * SIDE + z) for x in range(SIDE) for z in range(SIDE)]
    return lax.ppermute(array, "vid", pairs)


def along_z(array, shift):
    pairs = [(x * SIDE + z, x * SIDE + (z + shift) % SIDE) for x in range(SIDE) for z in range(SIDE)]
    return lax.ppermute(array, "vid", pairs)


def beside_z(array, distance):
    pairs = [(x * SIDE + z, x * SIDE + (z ^ distance)) for x in range(SIDE) for z in range(SIDE)]
    return lax.ppermute(array, "vid", pairs)


def gathered(array, along):
    return [array] + [along(array, shift) for shift in range(1, SIDE)]


def returned(parts, along):
    return [parts[0]] + [along(parts[place], SIDE - place) for place in range(1, SIDE)]


def nt(a, b):
    return lax.dot_general(a, b, (((1,), (1,)), ((), ())), preferred_element_type=F32)


def nn(a, b):
    return lax.dot_general(a, b, (((1,), (0,)), ((), ())), preferred_element_type=F32)


def joined(refs, index):
    return jnp.concatenate([ref[index] for ref in refs], axis=0)


def gated(rows, gate_row):
    return (gate_row * rows.astype(F32)).astype(BF16)


def query_rows(refs, index, video_rows):
    video = [ref[index, :video_rows] for ref in refs]
    audio = [ref[index, video_rows:] for ref in refs]
    return jnp.concatenate(video, axis=0), jnp.concatenate(audio, axis=0)


def upstream(refs, gates_ref, video_rows, part):
    video, audio = query_rows(refs, 1, video_rows)
    if part == VIDEO:
        audio = gated(audio, gates_ref[1:2, :])
    else:
        video = gated(video, gates_ref[0:1, :])
    return jnp.concatenate([video, audio], axis=0)


def prepare_kernel(place_ref, aq_ref, ak_ref, av_ref, vq_ref, vk_ref, vv_ref, dv_ref, da_ref, *outs):
    audio, video_kv, queries = outs
    rows = vq_ref.shape[1]
    audio[0] = aq_ref[0]
    audio[1] = ak_ref[0]
    audio[2] = av_ref[0]
    video_kv[0] = vk_ref[0]
    video_kv[1] = vv_ref[0]
    queries[0, :rows] = vq_ref[0]
    queries[0, rows:] = jnp.zeros_like(da_ref[0])
    queries[1, :rows] = dv_ref[0]
    queries[1, rows:] = da_ref[0]


def prepare(place, audio_q, audio_k, audio_v, video_q, video_k, video_v, d_video, d_audio):
    _, video_rows, width = video_q.shape
    audio_rows = d_audio.shape[1]
    cut = pl.BlockSpec((1, audio_rows, width), lambda i, place: (0, place[0], place[1]))
    whole = lambda *shape: pl.BlockSpec(shape, lambda i, place: (0,) * len(shape))
    shapes = [
        (3, audio_rows, width),
        (2, video_rows, width),
        (2, video_rows + audio_rows, width),
    ]
    return pl.pallas_call(
        prepare_kernel,
        grid_spec=pltpu.PrefetchScalarGridSpec(
            num_scalar_prefetch=1,
            grid=(1,),
            in_specs=[cut] * 3 + [whole(*video_q.shape)] * 4 + [whole(*d_audio.shape)],
            out_specs=[whole(*shape) for shape in shapes],
        ),
        out_shape=[jax.ShapeDtypeStruct(shape, BF16) for shape in shapes],
        compiler_params=pltpu.CompilerParams(vmem_limit_bytes=56 * 2**20),
        name="prepare",
    )(place, audio_q, audio_k, audio_v, video_q, video_k, video_v, d_video, d_audio)


def forward_kernel(part, video_rows, *refs):
    q_refs, k_refs, limit_ref, gates_ref = refs[:4], refs[4:8], refs[8], refs[9]
    e_ref, o_ref, stats_ref = refs[-3:]
    queries = jnp.concatenate(query_rows(q_refs, 0, video_rows), axis=0)
    raw = nt(joined(k_refs, 0), queries)
    if part == AUDIO:
        rows = k_refs[0].shape[1]
        position = lax.broadcasted_iota(jnp.int32, (rows, raw.shape[1]), 0)
        pieces = [raw[place * rows : (place + 1) * rows] for place in range(SIDE)]
        pieces = [jnp.where(position < limit_ref[place], pieces[place], -1e30) for place in range(SIDE)]
        raw = jnp.concatenate(pieces, axis=0)
    peak = jnp.max(raw, axis=0, keepdims=True)
    expon = jnp.exp((raw - peak) * SCALE)
    total = jnp.sum(expon, axis=0, keepdims=True)
    expon = expon.astype(BF16)
    e_ref[0] = expon
    output = nn(joined(k_refs, 1).T, expon)
    o_ref[0] = output
    up = upstream(q_refs, gates_ref, video_rows, part)
    weighted = jnp.sum(up.astype(F32).T * output, axis=0, keepdims=True)
    if part == VIDEO:
        stats_ref[0] = jnp.concatenate([peak, total, weighted, jnp.broadcast_to(peak, (5, peak.shape[1]))], axis=0)
    else:
        stats_ref[0] = jnp.concatenate([refs[10][0, 0:3], peak, total, weighted, peak, peak], axis=0)


def rolled_stats(refs, video_rows, audio_rows):
    video = SIDE * video_rows
    stats = [refs[0][0]]
    for shift in range(1, SIDE):
        array = refs[shift][0]
        stats.append(
            jnp.concatenate(
                [
                    pltpu.roll(array[:, :video], shift * video_rows, 1),
                    pltpu.roll(array[:, video:], shift * audio_rows, 1),
                ],
                axis=1,
            )
        )
    return stats


def merged_stats(stats, part):
    peaks = [array[3 * part : 3 * part + 1] for array in stats]
    peak = functools.reduce(jnp.maximum, peaks)
    weights = [jnp.exp((local - peak) * SCALE) for local in peaks]
    total = sum(weight * array[3 * part + 1 : 3 * part + 2] for weight, array in zip(weights, stats))
    delta = sum(weight * array[3 * part + 2 : 3 * part + 3] for weight, array in zip(weights, stats)) / total
    return weights[0] / total, delta


def backward_keys(part, queries, up, stats, k_refs, e_ref, k_outs, first):
    factor, delta = merged_stats(stats, part)
    probs = e_ref[0].astype(F32) * factor
    grad_values = nn(probs.astype(BF16), up).astype(BF16)
    grad_probs = nt(joined(k_refs, 1), up)
    grad_scores = (probs * (grad_probs - delta)).astype(BF16)
    grad_keys = (nn(grad_scores, queries) * SCALE).astype(BF16)
    rows = k_refs[0].shape[1]
    for place in range(SIDE):
        k_outs[place][0, first : first + rows] = grad_keys[place * rows : (place + 1) * rows]
        k_outs[place][1, first : first + rows] = grad_values[place * rows : (place + 1) * rows]
    return nn(joined(k_refs, 0).T, grad_scores), factor


def backward_kernel(video_rows, *refs):
    q_refs, k_video, k_audio, stats_refs = refs[:4], refs[4:8], refs[8:12], refs[12:16]
    gates_ref, columns_ref, e_video, e_audio, o_video, o_audio = refs[16:22]
    k_outs, q_outs = refs[22:26], refs[26:30]
    rows = q_refs[0].shape[1]
    audio_rows = rows - video_rows
    video = SIDE * video_rows
    queries = jnp.concatenate(query_rows(q_refs, 0, video_rows), axis=0)
    stats = rolled_stats(stats_refs, video_rows, audio_rows)
    up = upstream(q_refs, gates_ref, video_rows, VIDEO)
    term_video, factor = backward_keys(VIDEO, queries, up, stats, k_video, e_video, k_outs, 0)
    on_video = o_video[0] * factor
    up = upstream(q_refs, gates_ref, video_rows, AUDIO)
    term_audio, factor = backward_keys(AUDIO, queries, up, stats, k_audio, e_audio, k_outs, video_rows)
    on_audio = o_audio[0] * factor
    grad_queries = term_video + term_audio
    cross_video, cross_audio = on_audio[:, :video], on_video[:, video:]
    merged = jnp.concatenate(
        [
            on_video[:, :video] + columns_ref[:, 0:1] * cross_video,
            on_audio[:, video:] + columns_ref[:, 1:2] * cross_audio,
        ],
        axis=1,
    )
    up_video, up_audio = query_rows(q_refs, 1, video_rows)
    video_sum = jnp.sum(up_video.astype(F32).T * cross_video, axis=1, keepdims=True)
    audio_sum = jnp.sum(up_audio.astype(F32).T * cross_audio, axis=1, keepdims=True)
    sums = jnp.concatenate(
        [jnp.broadcast_to(video_sum, (HEAD_DIM, 4)), jnp.broadcast_to(audio_sum, (HEAD_DIM, HEAD_DIM - 4))], axis=1
    ).T[0:GATE_ROWS]
    high = sums.astype(BF16)
    low = (sums - high.astype(F32)).astype(BF16)
    even = lax.broadcasted_iota(jnp.int32, sums.shape, 0) % 2 == 0
    sums = jnp.where(even, high.astype(F32), low.astype(F32)).astype(BF16)
    merged = merged.T.astype(BF16)
    grad_queries = (grad_queries.T * SCALE).astype(BF16)
    for place in range(SIDE):
        for index, array in ((0, merged), (1, grad_queries)):
            first = index * rows
            q_outs[place][first : first + video_rows] = array[place * video_rows : (place + 1) * video_rows]
            start = video + place * audio_rows
            q_outs[place][first + video_rows : first + rows] = array[start : start + audio_rows]
        q_outs[place][2 * rows :] = sums


def chunk_spec(array):
    shape = array.shape[:-1]
    return pl.BlockSpec((*shape, HEAD_DIM), lambda h: (0,) * len(shape) + (h,))


def head_spec(array):
    shape = array.shape[1:]
    return pl.BlockSpec((1, *shape), lambda h: (h,) + (0,) * len(shape))


def like(*shape, kind=BF16):
    return jax.ShapeDtypeStruct(shape, kind)


def cost(keys, queries, heads, products):
    return pl.CostEstimate(
        flops=2 * products * heads * keys * queries * HEAD_DIM,
        bytes_accessed=4 * heads * keys * queries,
        transcendentals=heads * keys * queries,
    )


def attention_forward(part, q_chunks, k_chunks, limits, gates, earlier, video_rows):
    heads = gates.shape[1] // HEAD_DIM
    keys, queries = SIDE * k_chunks[0].shape[1], SIDE * q_chunks[0].shape[1]
    outs = [
        like(heads, keys, queries),
        like(heads, HEAD_DIM, queries, kind=F32),
        like(heads, 8, queries, kind=F32),
    ]
    return pl.pallas_call(
        functools.partial(forward_kernel, part, video_rows),
        grid=(heads,),
        in_specs=[chunk_spec(array) for array in (*q_chunks, *k_chunks)]
        + [pl.BlockSpec(memory_space=pltpu.SMEM), chunk_spec(gates)]
        + [head_spec(array) for array in earlier],
        out_specs=[head_spec(array) for array in outs],
        out_shape=outs,
        cost_estimate=cost(keys, queries, heads, 2),
        compiler_params=pltpu.CompilerParams(vmem_limit_bytes=24 * 2**20),
        name=("forward_video", "forward_audio")[part],
    )(*q_chunks, *k_chunks, limits, gates, *earlier)


def attention_backward(q_chunks, video_keys, audio_keys, stats, gates, by_head, video_rows):
    width = gates.shape[1]
    heads = width // HEAD_DIM
    rows, q_rows = video_keys[0].shape[1] + audio_keys[0].shape[1], q_chunks[0].shape[1]
    outs = [like(2, rows, width)] * SIDE + [like(2 * q_rows + GATE_ROWS, width)] * SIDE
    chunks = [*q_chunks, *video_keys, *audio_keys]
    outs = pl.pallas_call(
        functools.partial(backward_kernel, video_rows),
        grid=(heads,),
        in_specs=[chunk_spec(array) for array in chunks]
        + [head_spec(array) for array in stats]
        + [chunk_spec(gates), pl.BlockSpec((HEAD_DIM, 2), lambda h: (h, 0))]
        + [head_spec(array) for array in by_head],
        out_specs=[chunk_spec(array) for array in outs],
        out_shape=outs,
        cost_estimate=cost(SIDE * rows, SIDE * q_rows, heads, 4),
        compiler_params=pltpu.CompilerParams(vmem_limit_bytes=32 * 2**20),
        name="backward",
    )(*chunks, *stats, gates, gates.T, *by_head)
    return outs[:SIDE], outs[SIDE:]


def total_of(refs, *index):
    return sum(ref[index].astype(F32) for ref in refs)


def finish_queries_kernel(*refs):
    parts, (video_out, audio_out, video_q, audio_q, gate_ref) = refs[:SIDE], refs[SIDE:]
    video_rows, audio_rows = video_out.shape[1], audio_out.shape[1]
    rows = video_rows + audio_rows
    for index, video, audio in ((0, video_out, audio_out), (1, video_q, audio_q)):
        first = index * rows
        video[0] = total_of(parts, slice(first, first + video_rows)).astype(BF16)
        audio[0] = total_of(parts, slice(first + video_rows, first + rows)).astype(BF16)
    gates = total_of(parts, slice(2 * rows, None))
    video_gate = gates[0:1] + gates[1:2]
    audio_gate = gates[4:5] + gates[5:6]
    gate_ref[...] = jnp.concatenate([jnp.broadcast_to(video_gate, (4, gates.shape[1])), jnp.broadcast_to(audio_gate, (4, gates.shape[1]))], axis=0)


def finish_queries(parts, video_rows, audio_rows):
    width = parts[0].shape[1]
    video, audio = like(1, video_rows, width), like(1, audio_rows, width)
    return pl.pallas_call(
        finish_queries_kernel,
        out_shape=[video, audio, video, audio, like(8, width, kind=F32)],
        name="finish_queries",
    )(*parts)


def finish_keys_kernel(*refs):
    parts, (video_k, video_v, audio_k, audio_v) = refs[:SIDE], refs[SIDE:]
    rows = video_k.shape[1]
    for index, video, audio in ((0, video_k, audio_k), (1, video_v, audio_v)):
        video[0] = total_of(parts, index, slice(0, rows)).astype(BF16)
        audio[0] = total_of(parts, index, slice(rows, None)).astype(BF16)


def finish_keys(parts, video_rows, audio_rows):
    width = parts[0].shape[2]
    video, audio = like(1, video_rows, width), like(1, audio_rows, width)
    return pl.pallas_call(finish_keys_kernel, out_shape=[video, video, audio, audio], name="finish_keys")(*parts)


def own_audio(array, vid_size, aud_size):
    pairs = [
        (v * aud_size + a, (2 * a + v % 2) * aud_size + v // 2) for v in range(vid_size) for a in range(aud_size)
    ]
    return lax.ppermute(array, ("vid", "aud"), pairs)


def fenced(holds, function, *arrays):
    outs = jax.eval_shape(function, *arrays)
    return lax.cond(
        holds, function, lambda *_: jax.tree.map(lambda out: jnp.zeros(out.shape, out.dtype), outs), *arrays
    )


def shards(
    video_q, video_k, video_v, audio_q, audio_k, audio_v, video_gate, audio_gate, audio_len, d_video_out, d_audio_out
):
    vid = lax.axis_index("vid")
    sizes = lax.axis_size("vid"), lax.axis_size("aud")
    video_rows, audio_rows = video_q.shape[1], d_audio_out.shape[1]
    holds = audio_len[0] > 0
    place = jnp.stack([vid % 2, vid // 2]).astype(jnp.int32)
    send_audio, video_kv, queries = prepare(
        place, audio_q, audio_k, audio_v, video_q, video_k, video_v, d_video_out, d_audio_out
    )

    def first_chunks(send_audio, video_kv):
        return own_audio(send_audio, *sizes), along_z(video_kv, 1), along_z(video_kv, SIDE - 1)

    audio, before, behind = fenced(holds, first_chunks, send_audio, video_kv)
    audio_kv = audio[1:]
    q_chunks = gathered(lax.dynamic_update_slice(queries, audio[0:1], (0, video_rows, 0)), along_x)
    video_keys = [video_kv, before, along_z(video_kv, 2), behind]
    audio_keys = gathered(audio_kv, along_z)
    gates = jnp.stack([video_gate, audio_gate])
    column, row = vid // SIDE, vid % SIDE
    limits = jnp.stack([audio_len[0] - (column * SIDE + (row - p) % SIDE) * audio_rows for p in range(SIDE)])
    e_video, o_video, stats = attention_forward(VIDEO, q_chunks, video_keys, limits, gates, (), video_rows)
    e_audio, o_audio, stats = attention_forward(AUDIO, q_chunks, audio_keys, limits, gates, (stats,), video_rows)
    stats = gathered(stats, along_x)
    key_parts, query_parts = attention_backward(
        q_chunks, video_keys, audio_keys, stats, gates, (e_video, e_audio, o_video, o_audio), video_rows
    )

    def query_results(*parts):
        *results, gate = finish_queries(parts, video_rows, audio_rows)
        for distance in (1, 2):
            gate = gate + beside_z(gate, distance)
        return (*results, gate + lax.ppermute(gate, "pair", [(0, 1), (1, 0)]))

    query_parts = fenced(holds, lambda *parts: tuple(returned(parts, along_x)), *query_parts)
    video_out, audio_out, grad_video_q, grad_audio_q, gate = fenced(holds, query_results, *query_parts)
    key_parts = returned(key_parts, along_z)
    grad_video_k, grad_video_v, grad_audio_k, grad_audio_v = finish_keys(key_parts, video_rows, audio_rows)
    return (
        video_out,
        audio_out,
        grad_video_q,
        grad_video_k,
        grad_video_v,
        grad_audio_q,
        grad_audio_k,
        grad_audio_v,
        gate[0],
        gate[7],
    )


def solution(mesh):
    split = P("pair", "vid", "aud")
    rows = P("pair", "aud", None)
    return jax.shard_map(
        shards,
        mesh=mesh,
        in_specs=(split, split, split, rows, rows, rows, P("aud"), P("aud"), P("pair"), split, split),
        out_specs=(split,) * 8 + (P("aud"), P("aud")),
        check_vma=False,
    )
```

```python
import functools

import jax
import jax.numpy as jnp
from jax import lax
from jax.experimental import pallas as pl
from jax.experimental.pallas import tpu as pltpu
from jax.sharding import PartitionSpec as P

HEAD_DIM = 128
SCALE = HEAD_DIM ** (-0.5)
SIDE = 4
F32 = jnp.float32
BF16 = jnp.bfloat16
VIDEO, AUDIO = 0, 1
GATE_ROWS = 16
VMEM = 60 * 2**20

ALONG_X = [[x * SIDE + z for x in range(SIDE)] for z in range(SIDE)]


def along_x(array, shift):
    pairs = [(x * SIDE + z, (x + shift) % SIDE * SIDE + z) for x in range(SIDE) for z in range(SIDE)]
    return lax.ppermute(array, "vid", pairs)


def along_z(array, shift):
    pairs = [(x * SIDE + z, x * SIDE + (z + shift) % SIDE) for x in range(SIDE) for z in range(SIDE)]
    return lax.ppermute(array, "vid", pairs)


def beside_z(array, distance):
    pairs = [(x * SIDE + z, x * SIDE + (z ^ distance)) for x in range(SIDE) for z in range(SIDE)]
    return lax.ppermute(array, "vid", pairs)


def all_along_x(array):
    return lax.all_gather(array, "vid", axis=0, axis_index_groups=ALONG_X)


def gathered(array, along):
    return [array] + [along(array, shift) for shift in range(1, SIDE)]


def returned(parts, along):
    return [parts[0]] + [along(parts[place], SIDE - place) for place in range(1, SIDE)]


def nt(a, b):
    return lax.dot_general(a, b, (((1,), (1,)), ((), ())), preferred_element_type=F32)


def nn(a, b):
    return lax.dot_general(a, b, (((1,), (0,)), ((), ())), preferred_element_type=F32)


def joined(refs, index):
    return jnp.concatenate([ref[index] for ref in refs], axis=0)


def gated(rows, gate_row):
    return (gate_row * rows.astype(F32)).astype(BF16)


def query_rows(refs, index):
    blocks = [ref[:, index] for ref in refs]
    return tuple(block.reshape(-1, block.shape[-1]) for block in blocks)


def upstream(refs, gates_ref, part):
    video, audio = query_rows(refs, 1)
    if part == VIDEO:
        audio = gated(audio, gates_ref[1:2, :])
    else:
        video = gated(video, gates_ref[0:1, :])
    return jnp.concatenate([video, audio], axis=0)


def prepare_kernel(place_ref, aq_ref, ak_ref, av_ref, vq_ref, vk_ref, vv_ref, dv_ref, *outs):
    audio_q, audio_kv, video_kv, queries = outs
    audio_q[...] = aq_ref[0]
    audio_kv[0] = ak_ref[0]
    audio_kv[1] = av_ref[0]
    video_kv[0] = vk_ref[0]
    video_kv[1] = vv_ref[0]
    queries[0] = vq_ref[0]
    queries[1] = dv_ref[0]


def prepare(place, audio_rows, audio_q, audio_k, audio_v, video_q, video_k, video_v, d_video):
    _, video_rows, width = video_q.shape
    cut = pl.BlockSpec((1, audio_rows, width), lambda i, place: (0, place[0], place[1]))
    whole = lambda *shape: pl.BlockSpec(shape, lambda i, place: (0,) * len(shape))
    shapes = [(audio_rows, width), (2, audio_rows, width), (2, video_rows, width), (2, video_rows, width)]
    return pl.pallas_call(
        prepare_kernel,
        grid_spec=pltpu.PrefetchScalarGridSpec(
            num_scalar_prefetch=1,
            grid=(1,),
            in_specs=[cut] * 3 + [whole(*video_q.shape)] * 4,
            out_specs=[whole(*shape) for shape in shapes],
        ),
        out_shape=[jax.ShapeDtypeStruct(shape, BF16) for shape in shapes],
        compiler_params=pltpu.CompilerParams(vmem_limit_bytes=VMEM),
        name="prepare",
    )(place, audio_q, audio_k, audio_v, video_q, video_k, video_v, d_video)


def forward_kernel(part, *refs):
    q_refs, k_refs, limit_ref, gates_ref = refs[:2], refs[2:6], refs[6], refs[7]
    e_ref, o_ref, stats_ref = refs[-3:]
    queries = jnp.concatenate(query_rows(q_refs, 0), axis=0)
    raw = nt(joined(k_refs, 0), queries)
    if part == AUDIO:
        rows = k_refs[0].shape[1]
        position = lax.broadcasted_iota(jnp.int32, (rows, raw.shape[1]), 0)
        pieces = [raw[place * rows : (place + 1) * rows] for place in range(SIDE)]
        pieces = [jnp.where(position < limit_ref[place], pieces[place], -1e30) for place in range(SIDE)]
        raw = jnp.concatenate(pieces, axis=0)
    peak = jnp.max(raw, axis=0, keepdims=True)
    expon = jnp.exp((raw - peak) * SCALE)
    total = jnp.sum(expon, axis=0, keepdims=True)
    expon = (expon * (1.0 / total)).astype(BF16)
    e_ref[0] = expon
    output = nn(joined(k_refs, 1).T, expon)
    o_ref[0] = output
    up = upstream(q_refs, gates_ref, part)
    delta = jnp.sum(up.astype(F32).T * output, axis=0, keepdims=True)
    log_total = peak * SCALE + jnp.log(total)
    if part == VIDEO:
        stats_ref[0] = jnp.concatenate([log_total, delta, log_total, delta], axis=0)
    else:
        stats_ref[0] = jnp.concatenate([refs[8][0, 0:2], log_total, delta], axis=0)


def merged_stats(refs, part):
    logs = [ref[0, 2 * part : 2 * part + 1] for ref in refs]
    peak = functools.reduce(jnp.maximum, logs)
    weights = [jnp.exp(local - peak) for local in logs]
    scale = 1.0 / sum(weights)
    delta = sum(weight * ref[0, 2 * part + 1 : 2 * part + 2] for weight, ref in zip(weights, refs)) * scale
    return weights[0] * scale, delta


def backward_keys(part, queries, up, stats_refs, k_refs, e_ref, k_outs, first):
    factor, delta = merged_stats(stats_refs, part)
    probs = e_ref[0].astype(F32) * factor
    grad_values = nn(probs.astype(BF16), up).astype(BF16)
    grad_probs = nt(joined(k_refs, 1), up)
    grad_scores = (probs * (grad_probs - delta)).astype(BF16)
    grad_keys = (nn(grad_scores, queries) * SCALE).astype(BF16)
    rows = k_refs[0].shape[1]
    for place in range(SIDE):
        k_outs[place][0, first : first + rows] = grad_keys[place * rows : (place + 1) * rows]
        k_outs[place][1, first : first + rows] = grad_values[place * rows : (place + 1) * rows]
    return nn(joined(k_refs, 0).T, grad_scores), factor


def backward_kernel(*refs):
    q_refs, k_video, k_audio, stats_refs = refs[:2], refs[2:6], refs[6:10], refs[10:14]
    gates_ref, columns_ref, e_video, e_audio, o_video, o_audio = refs[14:20]
    k_outs, q_out = refs[20:24], refs[24]
    video_rows, audio_rows = (ref.shape[2] for ref in q_refs)
    rows = video_rows + audio_rows
    video = SIDE * video_rows
    queries = jnp.concatenate(query_rows(q_refs, 0), axis=0)
    up = upstream(q_refs, gates_ref, VIDEO)
    term_video, factor = backward_keys(VIDEO, queries, up, stats_refs, k_video, e_video, k_outs, 0)
    on_video = o_video[0] * factor
    up = upstream(q_refs, gates_ref, AUDIO)
    term_audio, factor = backward_keys(AUDIO, queries, up, stats_refs, k_audio, e_audio, k_outs, video_rows)
    on_audio = o_audio[0] * factor
    grad_queries = term_video + term_audio
    cross_video, cross_audio = on_audio[:, :video], on_video[:, video:]
    merged = jnp.concatenate(
        [
            on_video[:, :video] + columns_ref[:, 0:1] * cross_video,
            on_audio[:, video:] + columns_ref[:, 1:2] * cross_audio,
        ],
        axis=1,
    )
    up_video, up_audio = query_rows(q_refs, 1)
    video_sum = jnp.sum(up_video.astype(F32).T * cross_video, axis=1, keepdims=True)
    audio_sum = jnp.sum(up_audio.astype(F32).T * cross_audio, axis=1, keepdims=True)
    sums = jnp.concatenate(
        [jnp.broadcast_to(video_sum, (HEAD_DIM, 4)), jnp.broadcast_to(audio_sum, (HEAD_DIM, HEAD_DIM - 4))], axis=1
    ).T[0:GATE_ROWS]
    high = sums.astype(BF16)
    low = (sums - high.astype(F32)).astype(BF16)
    even = lax.broadcasted_iota(jnp.int32, sums.shape, 0) % 2 == 0
    sums = jnp.where(even, high.astype(F32), low.astype(F32)).astype(BF16)
    merged = merged.T.astype(BF16)
    grad_queries = (grad_queries.T * SCALE).astype(BF16)
    for index, array in ((0, merged), (1, grad_queries)):
        first = index * rows
        q_out[:, first : first + video_rows] = array[:video].reshape(SIDE, video_rows, HEAD_DIM)
        q_out[:, first + video_rows : first + rows] = array[video:].reshape(SIDE, audio_rows, HEAD_DIM)
    q_out[:, 2 * rows :] = jnp.broadcast_to(sums, (SIDE, *sums.shape))


def chunk_spec(array):
    shape = array.shape[:-1]
    return pl.BlockSpec((*shape, HEAD_DIM), lambda h: (0,) * len(shape) + (h,))


def head_spec(array):
    shape = array.shape[1:]
    return pl.BlockSpec((1, *shape), lambda h: (h,) + (0,) * len(shape))


def like(*shape, kind=BF16):
    return jax.ShapeDtypeStruct(shape, kind)


def cost(keys, queries, heads, products):
    return pl.CostEstimate(
        flops=2 * products * heads * keys * queries * HEAD_DIM,
        bytes_accessed=4 * heads * keys * queries,
        transcendentals=heads * keys * queries,
    )


def attention_forward(part, q_chunks, k_chunks, limits, gates, earlier):
    heads = gates.shape[1] // HEAD_DIM
    keys, queries = SIDE * k_chunks[0].shape[1], sum(SIDE * array.shape[2] for array in q_chunks)
    outs = [
        like(heads, keys, queries),
        like(heads, HEAD_DIM, queries, kind=F32),
        like(heads, 4, queries, kind=F32),
    ]
    return pl.pallas_call(
        functools.partial(forward_kernel, part),
        grid=(heads,),
        in_specs=[chunk_spec(array) for array in (*q_chunks, *k_chunks)]
        + [pl.BlockSpec(memory_space=pltpu.SMEM), chunk_spec(gates)]
        + [head_spec(array) for array in earlier],
        out_specs=[head_spec(array) for array in outs],
        out_shape=outs,
        cost_estimate=cost(keys, queries, heads, 2),
        compiler_params=pltpu.CompilerParams(vmem_limit_bytes=VMEM),
        name=("forward_video", "forward_audio")[part],
    )(*q_chunks, *k_chunks, limits, gates, *earlier)


def attention_backward(q_chunks, video_keys, audio_keys, stats, gates, by_head):
    width = gates.shape[1]
    heads = width // HEAD_DIM
    rows, q_rows = video_keys[0].shape[1] + audio_keys[0].shape[1], sum(array.shape[2] for array in q_chunks)
    outs = [like(2, rows, width)] * SIDE + [like(SIDE, 2 * q_rows + GATE_ROWS, width)]
    chunks = [*q_chunks, *video_keys, *audio_keys]
    *key_parts, query_parts = pl.pallas_call(
        backward_kernel,
        grid=(heads,),
        in_specs=[chunk_spec(array) for array in chunks]
        + [head_spec(array) for array in stats]
        + [chunk_spec(gates), pl.BlockSpec((HEAD_DIM, 2), lambda h: (h, 0))]
        + [head_spec(array) for array in by_head],
        out_specs=[chunk_spec(array) for array in outs],
        out_shape=outs,
        cost_estimate=cost(SIDE * rows, SIDE * q_rows, heads, 4),
        compiler_params=pltpu.CompilerParams(vmem_limit_bytes=VMEM),
        name="backward",
    )(*chunks, *stats, gates, gates.T, *by_head)
    return key_parts, query_parts


def total_of(refs, *index):
    return sum(ref[index].astype(F32) for ref in refs)


def finish_queries_kernel(parts_ref, video_out, audio_out, video_q, audio_q, gate_ref):
    video_rows, audio_rows = video_out.shape[1], audio_out.shape[1]
    rows = video_rows + audio_rows
    parts = [parts_ref.at[place] for place in range(SIDE)]
    for index, video, audio in ((0, video_out, audio_out), (1, video_q, audio_q)):
        first = index * rows
        video[0] = total_of(parts, slice(first, first + video_rows)).astype(BF16)
        audio[0] = total_of(parts, slice(first + video_rows, first + rows)).astype(BF16)
    gates = total_of(parts, slice(2 * rows, None))
    width = gates.shape[1]
    video_gate = jnp.broadcast_to(gates[0:1] + gates[1:2], (4, width))
    audio_gate = jnp.broadcast_to(gates[4:5] + gates[5:6], (4, width))
    gate_ref[...] = jnp.concatenate([video_gate, audio_gate], axis=0)


def finish_queries(parts, video_rows, audio_rows):
    width = parts.shape[2]
    video, audio = like(1, video_rows, width), like(1, audio_rows, width)
    return pl.pallas_call(
        finish_queries_kernel,
        out_shape=[video, audio, video, audio, like(8, width, kind=F32)],
        compiler_params=pltpu.CompilerParams(vmem_limit_bytes=8 * 2**20),
        name="finish_queries",
    )(parts)


def finish_keys_kernel(*refs):
    parts, (video_k, video_v, audio_k, audio_v) = refs[:SIDE], refs[SIDE:]
    rows = video_k.shape[1]
    for index, video, audio in ((0, video_k, audio_k), (1, video_v, audio_v)):
        video[0] = total_of(parts, index, slice(0, rows)).astype(BF16)
        audio[0] = total_of(parts, index, slice(rows, None)).astype(BF16)


def finish_keys(parts, video_rows, audio_rows):
    width = parts[0].shape[2]
    video, audio = like(1, video_rows, width), like(1, audio_rows, width)
    return pl.pallas_call(
        finish_keys_kernel,
        out_shape=[video, video, audio, audio],
        compiler_params=pltpu.CompilerParams(vmem_limit_bytes=8 * 2**20),
        name="finish_keys",
    )(*parts)


def own_audio(array, vid_size, aud_size):
    pairs = [
        (v * aud_size + a, (2 * a + v % 2) * aud_size + v // 2) for v in range(vid_size) for a in range(aud_size)
    ]
    return lax.ppermute(array, ("vid", "aud"), pairs)


def fenced(holds, function, *arrays):
    outs = jax.eval_shape(function, *arrays)
    return lax.cond(
        holds, function, lambda *_: jax.tree.map(lambda out: jnp.zeros(out.shape, out.dtype), outs), *arrays
    )


def shards(
    video_q, video_k, video_v, audio_q, audio_k, audio_v, video_gate, audio_gate, audio_len, d_video_out, d_audio_out
):
    vid = lax.axis_index("vid")
    sizes = lax.axis_size("vid"), lax.axis_size("aud")
    video_rows, audio_rows = video_q.shape[1], d_audio_out.shape[1]
    holds = audio_len[0] > 0
    place = jnp.stack([vid % 2, vid // 2]).astype(jnp.int32)
    send_q, send_kv, video_kv, video_queries = prepare(
        place, audio_rows, audio_q, audio_k, audio_v, video_q, video_k, video_v, d_video_out
    )

    def first_chunks(send_q, send_kv, video_kv, video_queries):
        audio = own_audio(send_q, *sizes), own_audio(send_kv, *sizes)
        keys = gathered(video_kv, along_z)
        return audio, tuple(keys[1:]), all_along_x(video_queries)

    (aud_q, aud_kv), video_keys, video_queries = fenced(
        holds, first_chunks, send_q, send_kv, video_kv, video_queries
    )
    video_keys = [video_kv, *video_keys]
    audio_keys = gathered(aud_kv, along_z)
    q_chunks = video_queries, all_along_x(jnp.stack([aud_q, d_audio_out[0]]))
    gates = jnp.stack([video_gate, audio_gate])
    column, row = vid // SIDE, vid % SIDE
    limits = jnp.stack([audio_len[0] - (column * SIDE + (row - p) % SIDE) * audio_rows for p in range(SIDE)])
    e_video, o_video, stats = attention_forward(VIDEO, q_chunks, video_keys, limits, gates, ())
    e_audio, o_audio, stats = attention_forward(AUDIO, q_chunks, audio_keys, limits, gates, (stats,))
    stats = gathered(stats, along_x)
    key_parts, query_parts = attention_backward(
        q_chunks, video_keys, audio_keys, stats, gates, (e_video, e_audio, o_video, o_audio)
    )

    def query_results(parts):
        parts = lax.all_to_all(parts, "vid", 0, 0, axis_index_groups=ALONG_X, tiled=True)
        *results, gate = finish_queries(parts, video_rows, audio_rows)
        for distance in (1, 2):
            gate = gate + beside_z(gate, distance)
        return (*results, gate + lax.ppermute(gate, "pair", [(0, 1), (1, 0)]))

    video_out, audio_out, grad_video_q, grad_audio_q, gate = fenced(holds, query_results, query_parts)
    key_parts = returned(key_parts, along_z)
    grad_video_k, grad_video_v, grad_audio_k, grad_audio_v = finish_keys(key_parts, video_rows, audio_rows)
    return (
        video_out,
        audio_out,
        grad_video_q,
        grad_video_k,
        grad_video_v,
        grad_audio_q,
        grad_audio_k,
        grad_audio_v,
        gate[0],
        gate[7],
    )


def solution(mesh):
    split = P("pair", "vid", "aud")
    rows = P("pair", "aud", None)
    return jax.shard_map(
        shards,
        mesh=mesh,
        in_specs=(split, split, split, rows, rows, rows, P("aud"), P("aud"), P("pair"), split, split),
        out_specs=(split,) * 8 + (P("aud"), P("aud")),
        check_vma=False,
    )
```

```python
import functools

import jax
import jax.numpy as jnp
from jax import lax
from jax.experimental import pallas as pl
from jax.experimental.pallas import tpu as pltpu
from jax.sharding import PartitionSpec as P

HEAD_DIM = 128
SCALE = HEAD_DIM ** (-0.5)
SIDE = 4
F32 = jnp.float32
BF16 = jnp.bfloat16
VIDEO, AUDIO = 0, 1
GATE_ROWS = 16
VMEM = 60 * 2**20

ALONG_X = [[x * SIDE + z for x in range(SIDE)] for z in range(SIDE)]


def along_x(array, shift):
    pairs = [(x * SIDE + z, (x + shift) % SIDE * SIDE + z) for x in range(SIDE) for z in range(SIDE)]
    return lax.ppermute(array, "vid", pairs)


def along_z(array, shift):
    pairs = [(x * SIDE + z, x * SIDE + (z + shift) % SIDE) for x in range(SIDE) for z in range(SIDE)]
    return lax.ppermute(array, "vid", pairs)


def beside_z(array, distance):
    pairs = [(x * SIDE + z, x * SIDE + (z ^ distance)) for x in range(SIDE) for z in range(SIDE)]
    return lax.ppermute(array, "vid", pairs)


def all_along_x(array):
    return lax.all_gather(array, "vid", axis=0, axis_index_groups=ALONG_X)


def gathered(array, along):
    return [array] + [along(array, shift) for shift in range(1, SIDE)]


def returned(parts, along):
    return [parts[0]] + [along(parts[place], SIDE - place) for place in range(1, SIDE)]


def nt(a, b):
    return lax.dot_general(a, b, (((1,), (1,)), ((), ())), preferred_element_type=F32)


def nn(a, b):
    return lax.dot_general(a, b, (((1,), (0,)), ((), ())), preferred_element_type=F32)


def joined(refs, index):
    return jnp.concatenate([ref[index] for ref in refs], axis=0)


def gated(rows, gate_row):
    return (gate_row * rows.astype(F32)).astype(BF16)


def flat(block):
    return block.reshape(-1, block.shape[-1])


def queries_of(gathered_ref, audio_ref, video_rows):
    return jnp.concatenate([flat(gathered_ref[:, :video_rows]), flat(audio_ref[...])], axis=0)


def upstreams_of(gathered_ref, video_rows):
    return flat(gathered_ref[:, video_rows : 2 * video_rows]), flat(gathered_ref[:, 2 * video_rows :])


def upstream(gathered_ref, gates_ref, video_rows, part):
    video, audio = upstreams_of(gathered_ref, video_rows)
    if part == VIDEO:
        audio = gated(audio, gates_ref[1:2, :])
    else:
        video = gated(video, gates_ref[0:1, :])
    return jnp.concatenate([video, audio], axis=0)


def prepare_kernel(place_ref, aq_ref, ak_ref, av_ref, vq_ref, vk_ref, vv_ref, dv_ref, da_ref, *outs):
    audio_q, audio_kv, video_kv, queries = outs
    rows = vq_ref.shape[1]
    audio_q[...] = aq_ref[0]
    audio_kv[0] = ak_ref[0]
    audio_kv[1] = av_ref[0]
    video_kv[0] = vk_ref[0]
    video_kv[1] = vv_ref[0]
    queries[:rows] = vq_ref[0]
    queries[rows : 2 * rows] = dv_ref[0]
    queries[2 * rows :] = da_ref[0]


def prepare(place, audio_q, audio_k, audio_v, video_q, video_k, video_v, d_video, d_audio):
    _, video_rows, width = video_q.shape
    audio_rows = d_audio.shape[1]
    cut = pl.BlockSpec((1, audio_rows, width), lambda i, place: (0, place[0], place[1]))
    whole = lambda *shape: pl.BlockSpec(shape, lambda i, place: (0,) * len(shape))
    shapes = [
        (audio_rows, width),
        (2, audio_rows, width),
        (2, video_rows, width),
        (2 * video_rows + audio_rows, width),
    ]
    return pl.pallas_call(
        prepare_kernel,
        grid_spec=pltpu.PrefetchScalarGridSpec(
            num_scalar_prefetch=1,
            grid=(1,),
            in_specs=[cut] * 3 + [whole(*video_q.shape)] * 4 + [whole(*d_audio.shape)],
            out_specs=[whole(*shape) for shape in shapes],
        ),
        out_shape=[jax.ShapeDtypeStruct(shape, BF16) for shape in shapes],
        compiler_params=pltpu.CompilerParams(vmem_limit_bytes=VMEM),
        name="prepare",
    )(place, audio_q, audio_k, audio_v, video_q, video_k, video_v, d_video, d_audio)


def forward_kernel(video_rows, *refs):
    gathered_ref, audio_q, k_refs, numbers_ref, gates_ref = refs[0], refs[1:5], (refs[5:9], refs[9:13]), refs[13], refs[14]
    e_refs, o_ref, stats_ref, ordered_ref = refs[15:17], refs[17], refs[18], refs[19]
    for place in range(SIDE):
        ordered_ref[lax.rem(numbers_ref[SIDE] + SIDE - place, SIDE)] = audio_q[place][...]
    queries = queries_of(gathered_ref, ordered_ref, video_rows)
    stats = []
    for part in (VIDEO, AUDIO):
        raw = nt(joined(k_refs[part], 0), queries)
        if part == AUDIO:
            rows = k_refs[part][0].shape[1]
            position = lax.broadcasted_iota(jnp.int32, (rows, raw.shape[1]), 0)
            pieces = [raw[place * rows : (place + 1) * rows] for place in range(SIDE)]
            pieces = [jnp.where(position < numbers_ref[place], pieces[place], -1e30) for place in range(SIDE)]
            raw = jnp.concatenate(pieces, axis=0)
        peak = jnp.max(raw, axis=0, keepdims=True)
        expon = jnp.exp((raw - peak) * SCALE)
        total = jnp.sum(expon, axis=0, keepdims=True)
        expon = (expon * (1.0 / total)).astype(BF16)
        e_refs[part][0] = expon
        output = nn(joined(k_refs[part], 1).T, expon)
        o_ref[0, part] = output
        up = upstream(gathered_ref, gates_ref, video_rows, part)
        stats.append(peak * SCALE + jnp.log(total))
        stats.append(jnp.sum(up.astype(F32).T * output, axis=0, keepdims=True))
    stats_ref[0] = jnp.concatenate(stats, axis=0)


def merged_stats(refs, part):
    logs = [ref[0, 2 * part : 2 * part + 1] for ref in refs]
    peak = functools.reduce(jnp.maximum, logs)
    weights = [jnp.exp(local - peak) for local in logs]
    scale = 1.0 / sum(weights)
    delta = sum(weight * ref[0, 2 * part + 1 : 2 * part + 2] for weight, ref in zip(weights, refs)) * scale
    return weights[0] * scale, delta


def backward_keys(part, queries, up, stats_refs, k_refs, e_ref, k_outs, first):
    factor, delta = merged_stats(stats_refs, part)
    probs = e_ref[0].astype(F32) * factor
    grad_values = nn(probs.astype(BF16), up).astype(BF16)
    grad_probs = nt(joined(k_refs, 1), up)
    grad_scores = (probs * (grad_probs - delta)).astype(BF16)
    grad_keys = (nn(grad_scores, queries) * SCALE).astype(BF16)
    rows = k_refs[0].shape[1]
    for place in range(SIDE):
        k_outs[place][0, first : first + rows] = grad_keys[place * rows : (place + 1) * rows]
        k_outs[place][1, first : first + rows] = grad_values[place * rows : (place + 1) * rows]
    return nn(joined(k_refs, 0).T, grad_scores), factor


def backward_kernel(video_rows, *refs):
    gathered_ref, audio_q, k_video, k_audio, stats_refs = refs[0], refs[1], refs[2:6], refs[6:10], refs[10:14]
    gates_ref, columns_ref, e_video, e_audio, o_ref = refs[14:19]
    k_outs, q_out = refs[19:23], refs[23]
    audio_rows = audio_q.shape[1]
    rows = video_rows + audio_rows
    video = SIDE * video_rows
    queries = queries_of(gathered_ref, audio_q, video_rows)
    up = upstream(gathered_ref, gates_ref, video_rows, VIDEO)
    term_video, factor = backward_keys(VIDEO, queries, up, stats_refs, k_video, e_video, k_outs, 0)
    on_video = o_ref[0, VIDEO] * factor
    up = upstream(gathered_ref, gates_ref, video_rows, AUDIO)
    term_audio, factor = backward_keys(AUDIO, queries, up, stats_refs, k_audio, e_audio, k_outs, video_rows)
    on_audio = o_ref[0, AUDIO] * factor
    grad_queries = term_video + term_audio
    cross_video, cross_audio = on_audio[:, :video], on_video[:, video:]
    merged = jnp.concatenate(
        [
            on_video[:, :video] + columns_ref[:, 0:1] * cross_video,
            on_audio[:, video:] + columns_ref[:, 1:2] * cross_audio,
        ],
        axis=1,
    )
    up_video, up_audio = upstreams_of(gathered_ref, video_rows)
    video_sum = jnp.sum(up_video.astype(F32).T * cross_video, axis=1, keepdims=True)
    audio_sum = jnp.sum(up_audio.astype(F32).T * cross_audio, axis=1, keepdims=True)
    sums = jnp.concatenate(
        [jnp.broadcast_to(video_sum, (HEAD_DIM, 4)), jnp.broadcast_to(audio_sum, (HEAD_DIM, HEAD_DIM - 4))], axis=1
    ).T[0:GATE_ROWS]
    high = sums.astype(BF16)
    low = (sums - high.astype(F32)).astype(BF16)
    even = lax.broadcasted_iota(jnp.int32, sums.shape, 0) % 2 == 0
    sums = jnp.where(even, high.astype(F32), low.astype(F32)).astype(BF16)
    merged = merged.T.astype(BF16)
    grad_queries = (grad_queries.T * SCALE).astype(BF16)
    for index, array in ((0, merged), (1, grad_queries)):
        first = index * rows
        q_out[:, first : first + video_rows] = array[:video].reshape(SIDE, video_rows, HEAD_DIM)
        q_out[:, first + video_rows : first + rows] = array[video:].reshape(SIDE, audio_rows, HEAD_DIM)
    q_out[:, 2 * rows :] = jnp.broadcast_to(sums, (SIDE, *sums.shape))


def chunk_spec(array):
    shape = array.shape[:-1]
    return pl.BlockSpec((*shape, HEAD_DIM), lambda h: (0,) * len(shape) + (h,))


def head_spec(array):
    shape = array.shape[1:]
    return pl.BlockSpec((1, *shape), lambda h: (h,) + (0,) * len(shape))


def like(*shape, kind=BF16):
    return jax.ShapeDtypeStruct(shape, kind)


def cost(keys, queries, heads, products):
    return pl.CostEstimate(
        flops=2 * products * heads * keys * queries * HEAD_DIM,
        bytes_accessed=4 * heads * keys * queries,
        transcendentals=heads * keys * queries,
    )


def attention_forward(queries, audio_q, video_keys, audio_keys, numbers, gates, video_rows):
    heads = gates.shape[1] // HEAD_DIM
    audio_rows, width = audio_q[0].shape
    video, audio = SIDE * video_rows, SIDE * audio_rows
    total = video + audio
    outs = [
        like(heads, video, total),
        like(heads, audio, total),
        like(heads, 2, HEAD_DIM, total, kind=F32),
        like(heads, 4, total, kind=F32),
    ]
    ordered = like(SIDE, audio_rows, width)
    chunks = [queries, *audio_q, *video_keys, *audio_keys]
    return pl.pallas_call(
        functools.partial(forward_kernel, video_rows),
        grid=(heads,),
        in_specs=[chunk_spec(array) for array in chunks] + [pl.BlockSpec(memory_space=pltpu.SMEM), chunk_spec(gates)],
        out_specs=[head_spec(array) for array in outs] + [chunk_spec(ordered)],
        out_shape=[*outs, ordered],
        cost_estimate=cost(total, total, heads, 2),
        compiler_params=pltpu.CompilerParams(vmem_limit_bytes=VMEM),
        name="forward",
    )(*chunks, numbers, gates)


def attention_backward(queries, audio_q, video_keys, audio_keys, stats, gates, by_head, video_rows):
    width = gates.shape[1]
    heads = width // HEAD_DIM
    rows = video_rows + audio_q.shape[1]
    outs = [like(2, rows, width)] * SIDE + [like(SIDE, 2 * rows + GATE_ROWS, width)]
    chunks = [queries, audio_q, *video_keys, *audio_keys]
    *key_parts, query_parts = pl.pallas_call(
        functools.partial(backward_kernel, video_rows),
        grid=(heads,),
        in_specs=[chunk_spec(array) for array in chunks]
        + [head_spec(array) for array in stats]
        + [chunk_spec(gates), pl.BlockSpec((HEAD_DIM, 2), lambda h: (h, 0))]
        + [head_spec(array) for array in by_head],
        out_specs=[chunk_spec(array) for array in outs],
        out_shape=outs,
        cost_estimate=cost(SIDE * rows, SIDE * rows, heads, 4),
        compiler_params=pltpu.CompilerParams(vmem_limit_bytes=VMEM),
        name="backward",
    )(*chunks, *stats, gates, gates.T, *by_head)
    return key_parts, query_parts


def total_of(refs, *index):
    return sum(ref[index].astype(F32) for ref in refs)


def finish_queries_kernel(parts_ref, video_out, audio_out, video_q, audio_q, gate_ref):
    video_rows, audio_rows = video_out.shape[1], audio_out.shape[1]
    rows = video_rows + audio_rows
    parts = [parts_ref.at[place] for place in range(SIDE)]
    for index, video, audio in ((0, video_out, audio_out), (1, video_q, audio_q)):
        first = index * rows
        video[0] = total_of(parts, slice(first, first + video_rows)).astype(BF16)
        audio[0] = total_of(parts, slice(first + video_rows, first + rows)).astype(BF16)
    gates = total_of(parts, slice(2 * rows, None))
    width = gates.shape[1]
    video_gate = jnp.broadcast_to(gates[0:1] + gates[1:2], (4, width))
    audio_gate = jnp.broadcast_to(gates[4:5] + gates[5:6], (4, width))
    gate_ref[...] = jnp.concatenate([video_gate, audio_gate], axis=0)


def finish_queries(parts, video_rows, audio_rows):
    width = parts.shape[2]
    video, audio = like(1, video_rows, width), like(1, audio_rows, width)
    return pl.pallas_call(
        finish_queries_kernel,
        out_shape=[video, audio, video, audio, like(8, width, kind=F32)],
        compiler_params=pltpu.CompilerParams(vmem_limit_bytes=8 * 2**20),
        name="finish_queries",
    )(parts)


def finish_keys_kernel(*refs):
    parts, (video_k, video_v, audio_k, audio_v) = refs[:SIDE], refs[SIDE:]
    rows = video_k.shape[1]
    for index, video, audio in ((0, video_k, audio_k), (1, video_v, audio_v)):
        video[0] = total_of(parts, index, slice(0, rows)).astype(BF16)
        audio[0] = total_of(parts, index, slice(rows, None)).astype(BF16)


def finish_keys(parts, video_rows, audio_rows):
    width = parts[0].shape[2]
    video, audio = like(1, video_rows, width), like(1, audio_rows, width)
    return pl.pallas_call(
        finish_keys_kernel,
        out_shape=[video, video, audio, audio],
        compiler_params=pltpu.CompilerParams(vmem_limit_bytes=8 * 2**20),
        name="finish_keys",
    )(*parts)


def own_audio(array, vid_size, aud_size):
    pairs = [
        (v * aud_size + a, (2 * a + v % 2) * aud_size + v // 2) for v in range(vid_size) for a in range(aud_size)
    ]
    return lax.ppermute(array, ("vid", "aud"), pairs)


def fenced(holds, function, *arrays):
    outs = jax.eval_shape(function, *arrays)
    return lax.cond(
        holds, function, lambda *_: jax.tree.map(lambda out: jnp.zeros(out.shape, out.dtype), outs), *arrays
    )


def shards(
    video_q, video_k, video_v, audio_q, audio_k, audio_v, video_gate, audio_gate, audio_len, d_video_out, d_audio_out
):
    vid = lax.axis_index("vid")
    sizes = lax.axis_size("vid"), lax.axis_size("aud")
    video_rows, audio_rows = video_q.shape[1], d_audio_out.shape[1]
    holds = audio_len[0] > 0
    place = jnp.stack([vid % 2, vid // 2]).astype(jnp.int32)
    send_q, send_kv, video_kv, queries = prepare(
        place, audio_q, audio_k, audio_v, video_q, video_k, video_v, d_video_out, d_audio_out
    )

    def video_chunks(video_kv, queries):
        return tuple(gathered(video_kv, along_z)[1:]), all_along_x(queries)

    aud_q, aud_kv = own_audio(send_q, *sizes), own_audio(send_kv, *sizes)
    video_keys, queries = fenced(holds, video_chunks, video_kv, queries)
    aud_q, aud_kv, queries = lax.optimization_barrier((aud_q, aud_kv, queries))
    video_keys = [video_kv, *video_keys]
    audio_queries = gathered(aud_q, along_x)
    audio_keys = gathered(aud_kv, along_z)
    gates = jnp.stack([video_gate, audio_gate])
    column, row = vid // SIDE, vid % SIDE
    limits = [audio_len[0] - (column * SIDE + (row - p) % SIDE) * audio_rows for p in range(SIDE)]
    numbers = jnp.stack([*limits, column])
    *by_head, stats, audio_queries = attention_forward(
        queries, audio_queries, video_keys, audio_keys, numbers, gates, video_rows
    )
    key_parts, query_parts = attention_backward(
        queries, audio_queries, video_keys, audio_keys, gathered(stats, along_x), gates, by_head, video_rows
    )

    def query_results(parts):
        parts = lax.all_to_all(parts, "vid", 0, 0, axis_index_groups=ALONG_X, tiled=True)
        *results, gate = finish_queries(parts, video_rows, audio_rows)
        for distance in (1, 2):
            gate = gate + beside_z(gate, distance)
        return (*results, gate + lax.ppermute(gate, "pair", [(0, 1), (1, 0)]))

    video_out, audio_out, grad_video_q, grad_audio_q, gate = fenced(holds, query_results, query_parts)
    key_parts = returned(key_parts, along_z)
    grad_video_k, grad_video_v, grad_audio_k, grad_audio_v = finish_keys(key_parts, video_rows, audio_rows)
    return (
        video_out,
        audio_out,
        grad_video_q,
        grad_video_k,
        grad_video_v,
        grad_audio_q,
        grad_audio_k,
        grad_audio_v,
        gate[0],
        gate[7],
    )


def solution(mesh):
    split = P("pair", "vid", "aud")
    rows = P("pair", "aud", None)
    return jax.shard_map(
        shards,
        mesh=mesh,
        in_specs=(split, split, split, rows, rows, rows, P("aud"), P("aud"), P("pair"), split, split),
        out_specs=(split,) * 8 + (P("aud"), P("aud")),
        check_vma=False,
    )
```

```python
import functools

import jax
import jax.numpy as jnp
from jax import lax
from jax.experimental import pallas as pl
from jax.experimental.pallas import tpu as pltpu
from jax.sharding import PartitionSpec as P

HEAD_DIM = 128
SCALE = HEAD_DIM ** (-0.5)
SIDE = 4
F32 = jnp.float32
BF16 = jnp.bfloat16
VIDEO, AUDIO = 0, 1
GATE_ROWS = 16
VMEM = 60 * 2**20

ALONG_X = [[x * SIDE + z for x in range(SIDE)] for z in range(SIDE)]


def along_x(array, shift):
    pairs = [(x * SIDE + z, (x + shift) % SIDE * SIDE + z) for x in range(SIDE) for z in range(SIDE)]
    return lax.ppermute(array, "vid", pairs)


def along_z(array, shift):
    pairs = [(x * SIDE + z, x * SIDE + (z + shift) % SIDE) for x in range(SIDE) for z in range(SIDE)]
    return lax.ppermute(array, "vid", pairs)


def beside_z(array, distance):
    pairs = [(x * SIDE + z, x * SIDE + (z ^ distance)) for x in range(SIDE) for z in range(SIDE)]
    return lax.ppermute(array, "vid", pairs)


def all_along_x(array):
    return lax.all_gather(array, "vid", axis=0, axis_index_groups=ALONG_X)


def gathered(array, along):
    return [array] + [along(array, shift) for shift in range(1, SIDE)]


def returned(parts, along):
    return [parts[0]] + [along(parts[place], SIDE - place) for place in range(1, SIDE)]


def nt(a, b):
    return lax.dot_general(a, b, (((1,), (1,)), ((), ())), preferred_element_type=F32)


def nn(a, b):
    return lax.dot_general(a, b, (((1,), (0,)), ((), ())), preferred_element_type=F32)


def joined(refs, index):
    return jnp.concatenate([ref[index] for ref in refs], axis=0)


def gated(rows, gate_row):
    return (gate_row * rows.astype(F32)).astype(BF16)


def flat(block):
    return block.reshape(-1, block.shape[-1])


def queries_of(gathered_ref, audio_ref, video_rows):
    return jnp.concatenate([flat(gathered_ref[:, :video_rows]), flat(audio_ref[...])], axis=0)


def upstreams_of(gathered_ref, video_rows):
    return flat(gathered_ref[:, video_rows : 2 * video_rows]), flat(gathered_ref[:, 2 * video_rows :])


def upstream(gathered_ref, gates_ref, video_rows, part):
    video, audio = upstreams_of(gathered_ref, video_rows)
    if part == VIDEO:
        audio = gated(audio, gates_ref[1:2, :])
    else:
        video = gated(video, gates_ref[0:1, :])
    return jnp.concatenate([video, audio], axis=0)


def prepare_kernel(aq_ref, ak_ref, av_ref, vq_ref, vk_ref, vv_ref, dv_ref, da_ref, audio, video_kv, queries, sems):
    vid = lax.axis_index("vid")
    rows, width = vq_ref.shape[1:]
    audio_rows = da_ref.shape[1]
    taken = pl.ds(pl.multiple_of(lax.rem(vid, 2) * audio_rows, audio_rows), audio_rows)
    columns = pl.ds(pl.multiple_of(lax.div(vid, 2) * width, HEAD_DIM), width)
    pairs = [(ref.at[0, taken, columns], audio.at[index]) for index, ref in enumerate((aq_ref, ak_ref, av_ref))]
    pairs += [(vk_ref.at[0], video_kv.at[0]), (vv_ref.at[0], video_kv.at[1])]
    pairs += [(vq_ref.at[0], queries.at[pl.ds(0, rows)]), (dv_ref.at[0], queries.at[pl.ds(rows, rows)])]
    pairs += [(da_ref.at[0], queries.at[pl.ds(2 * rows, audio_rows)])]
    copies = [pltpu.make_async_copy(source, target, sems.at[index]) for index, (source, target) in enumerate(pairs)]
    for copy in copies:
        copy.start()
    for copy in copies:
        copy.wait()


def prepare(audio_q, audio_k, audio_v, video_q, video_k, video_v, d_video, d_audio):
    _, video_rows, width = video_q.shape
    audio_rows = d_audio.shape[1]
    given = (audio_q, audio_k, audio_v, video_q, video_k, video_v, d_video, d_audio)
    shapes = [(3, audio_rows, width), (2, video_rows, width), (2 * video_rows + audio_rows, width)]
    return pl.pallas_call(
        prepare_kernel,
        in_specs=[pl.BlockSpec(memory_space=pl.ANY)] * len(given),
        out_specs=[pl.BlockSpec(memory_space=pl.ANY)] * len(shapes),
        out_shape=[like(*shape) for shape in shapes],
        scratch_shapes=[pltpu.SemaphoreType.DMA((len(given),))],
        compiler_params=pltpu.CompilerParams(vmem_limit_bytes=VMEM),
        name="prepare",
    )(*given)


def forward_kernel(video_rows, *refs):
    gathered_ref, audio_q, k_refs, numbers_ref, gates_ref = refs[0], refs[1:5], (refs[5:9], refs[9:13]), refs[13], refs[14]
    e_refs, o_ref, stats_ref, ordered_ref = refs[15:17], refs[17], refs[18], refs[19]
    for place in range(SIDE):
        ordered_ref[lax.rem(numbers_ref[SIDE] + SIDE - place, SIDE)] = audio_q[place][...]
    queries = queries_of(gathered_ref, ordered_ref, video_rows)
    stats = []
    for part in (VIDEO, AUDIO):
        raw = nt(joined(k_refs[part], 0), queries)
        if part == AUDIO:
            rows = k_refs[part][0].shape[1]
            position = lax.broadcasted_iota(jnp.int32, (rows, raw.shape[1]), 0)
            pieces = [raw[place * rows : (place + 1) * rows] for place in range(SIDE)]
            pieces = [jnp.where(position < numbers_ref[place], pieces[place], -1e30) for place in range(SIDE)]
            raw = jnp.concatenate(pieces, axis=0)
        peak = jnp.max(raw, axis=0, keepdims=True)
        expon = jnp.exp((raw - peak) * SCALE)
        total = jnp.sum(expon, axis=0, keepdims=True)
        expon = (expon * (1.0 / total)).astype(BF16)
        e_refs[part][0] = expon
        output = nn(joined(k_refs[part], 1).T, expon)
        o_ref[0, part] = output
        up = upstream(gathered_ref, gates_ref, video_rows, part)
        stats.append(peak * SCALE + jnp.log(total))
        stats.append(jnp.sum(up.astype(F32).T * output, axis=0, keepdims=True))
    stats_ref[0] = jnp.concatenate(stats, axis=0)


def merged_stats(refs, part):
    logs = [ref[0, 2 * part : 2 * part + 1] for ref in refs]
    peak = functools.reduce(jnp.maximum, logs)
    weights = [jnp.exp(local - peak) for local in logs]
    scale = 1.0 / sum(weights)
    delta = sum(weight * ref[0, 2 * part + 1 : 2 * part + 2] for weight, ref in zip(weights, refs)) * scale
    return weights[0] * scale, delta


def backward_keys(part, queries, up, stats_refs, k_refs, e_ref, k_outs, first):
    factor, delta = merged_stats(stats_refs, part)
    probs = e_ref[0].astype(F32) * factor
    grad_values = nn(probs.astype(BF16), up).astype(BF16)
    grad_probs = nt(joined(k_refs, 1), up)
    grad_scores = (probs * (grad_probs - delta)).astype(BF16)
    grad_keys = (nn(grad_scores, queries) * SCALE).astype(BF16)
    rows = k_refs[0].shape[1]
    for place in range(SIDE):
        k_outs[place][0, first : first + rows] = grad_keys[place * rows : (place + 1) * rows]
        k_outs[place][1, first : first + rows] = grad_values[place * rows : (place + 1) * rows]
    return nn(joined(k_refs, 0).T, grad_scores), factor


def backward_kernel(video_rows, *refs):
    gathered_ref, audio_q, k_video, k_audio, stats_refs = refs[0], refs[1], refs[2:6], refs[6:10], refs[10:14]
    gates_ref, columns_ref, e_video, e_audio, o_ref = refs[14:19]
    k_outs, q_out = refs[19:23], refs[23]
    audio_rows = audio_q.shape[1]
    rows = video_rows + audio_rows
    video = SIDE * video_rows
    queries = queries_of(gathered_ref, audio_q, video_rows)
    up = upstream(gathered_ref, gates_ref, video_rows, VIDEO)
    term_video, factor = backward_keys(VIDEO, queries, up, stats_refs, k_video, e_video, k_outs, 0)
    on_video = o_ref[0, VIDEO] * factor
    up = upstream(gathered_ref, gates_ref, video_rows, AUDIO)
    term_audio, factor = backward_keys(AUDIO, queries, up, stats_refs, k_audio, e_audio, k_outs, video_rows)
    on_audio = o_ref[0, AUDIO] * factor
    grad_queries = term_video + term_audio
    cross_video, cross_audio = on_audio[:, :video], on_video[:, video:]
    merged = jnp.concatenate(
        [
            on_video[:, :video] + columns_ref[:, 0:1] * cross_video,
            on_audio[:, video:] + columns_ref[:, 1:2] * cross_audio,
        ],
        axis=1,
    )
    up_video, up_audio = upstreams_of(gathered_ref, video_rows)
    video_sum = jnp.sum(up_video.astype(F32).T * cross_video, axis=1, keepdims=True)
    audio_sum = jnp.sum(up_audio.astype(F32).T * cross_audio, axis=1, keepdims=True)
    sums = jnp.concatenate(
        [jnp.broadcast_to(video_sum, (HEAD_DIM, 4)), jnp.broadcast_to(audio_sum, (HEAD_DIM, HEAD_DIM - 4))], axis=1
    ).T[0:GATE_ROWS]
    high = sums.astype(BF16)
    low = (sums - high.astype(F32)).astype(BF16)
    even = lax.broadcasted_iota(jnp.int32, sums.shape, 0) % 2 == 0
    sums = jnp.where(even, high.astype(F32), low.astype(F32)).astype(BF16)
    merged = merged.T.astype(BF16)
    grad_queries = (grad_queries.T * SCALE).astype(BF16)
    for index, array in ((0, merged), (1, grad_queries)):
        first = index * rows
        q_out[:, first : first + video_rows] = array[:video].reshape(SIDE, video_rows, HEAD_DIM)
        q_out[:, first + video_rows : first + rows] = array[video:].reshape(SIDE, audio_rows, HEAD_DIM)
    q_out[:, 2 * rows :] = jnp.broadcast_to(sums, (SIDE, *sums.shape))


def chunk_spec(array):
    shape = array.shape[:-1]
    return pl.BlockSpec((*shape, HEAD_DIM), lambda h: (0,) * len(shape) + (h,))


def head_spec(array):
    shape = array.shape[1:]
    return pl.BlockSpec((1, *shape), lambda h: (h,) + (0,) * len(shape))


def like(*shape, kind=BF16):
    return jax.ShapeDtypeStruct(shape, kind)


def cost(keys, queries, heads, products):
    return pl.CostEstimate(
        flops=2 * products * heads * keys * queries * HEAD_DIM,
        bytes_accessed=4 * heads * keys * queries,
        transcendentals=heads * keys * queries,
    )


def attention_forward(queries, audio_q, video_keys, audio_keys, numbers, gates, video_rows):
    heads = gates.shape[1] // HEAD_DIM
    audio_rows, width = audio_q[0].shape
    video, audio = SIDE * video_rows, SIDE * audio_rows
    total = video + audio
    outs = [
        like(heads, video, total),
        like(heads, audio, total),
        like(heads, 2, HEAD_DIM, total, kind=F32),
        like(heads, 4, total, kind=F32),
    ]
    ordered = like(SIDE, audio_rows, width)
    chunks = [queries, *audio_q, *video_keys, *audio_keys]
    return pl.pallas_call(
        functools.partial(forward_kernel, video_rows),
        grid=(heads,),
        in_specs=[chunk_spec(array) for array in chunks] + [pl.BlockSpec(memory_space=pltpu.SMEM), chunk_spec(gates)],
        out_specs=[head_spec(array) for array in outs] + [chunk_spec(ordered)],
        out_shape=[*outs, ordered],
        cost_estimate=cost(total, total, heads, 2),
        compiler_params=pltpu.CompilerParams(vmem_limit_bytes=VMEM),
        name="forward",
    )(*chunks, numbers, gates)


def attention_backward(queries, audio_q, video_keys, audio_keys, stats, gates, by_head, video_rows):
    width = gates.shape[1]
    heads = width // HEAD_DIM
    rows = video_rows + audio_q.shape[1]
    outs = [like(2, rows, width)] * SIDE + [like(SIDE, 2 * rows + GATE_ROWS, width)]
    chunks = [queries, audio_q, *video_keys, *audio_keys]
    *key_parts, query_parts = pl.pallas_call(
        functools.partial(backward_kernel, video_rows),
        grid=(heads,),
        in_specs=[chunk_spec(array) for array in chunks]
        + [head_spec(array) for array in stats]
        + [chunk_spec(gates), pl.BlockSpec((HEAD_DIM, 2), lambda h: (h, 0))]
        + [head_spec(array) for array in by_head],
        out_specs=[chunk_spec(array) for array in outs],
        out_shape=outs,
        cost_estimate=cost(SIDE * rows, SIDE * rows, heads, 4),
        compiler_params=pltpu.CompilerParams(vmem_limit_bytes=VMEM),
        name="backward",
    )(*chunks, *stats, gates, gates.T, *by_head)
    return key_parts, query_parts


def total_of(refs, *index):
    return sum(ref[index].astype(F32) for ref in refs)


def finish_queries_kernel(parts_ref, video_out, audio_out, video_q, audio_q, gate_ref):
    video_rows, audio_rows = video_out.shape[1], audio_out.shape[1]
    rows = video_rows + audio_rows
    parts = [parts_ref.at[place] for place in range(SIDE)]
    for index, video, audio in ((0, video_out, audio_out), (1, video_q, audio_q)):
        first = index * rows
        video[0] = total_of(parts, slice(first, first + video_rows)).astype(BF16)
        audio[0] = total_of(parts, slice(first + video_rows, first + rows)).astype(BF16)
    gates = total_of(parts, slice(2 * rows, None))
    width = gates.shape[1]
    video_gate = jnp.broadcast_to(gates[0:1] + gates[1:2], (4, width))
    audio_gate = jnp.broadcast_to(gates[4:5] + gates[5:6], (4, width))
    gate_ref[...] = jnp.concatenate([video_gate, audio_gate], axis=0)


def finish_queries(parts, video_rows, audio_rows):
    width = parts.shape[2]
    video, audio = like(1, video_rows, width), like(1, audio_rows, width)
    return pl.pallas_call(
        finish_queries_kernel,
        out_shape=[video, audio, video, audio, like(8, width, kind=F32)],
        compiler_params=pltpu.CompilerParams(vmem_limit_bytes=8 * 2**20),
        name="finish_queries",
    )(parts)


def finish_keys_kernel(*refs):
    parts, (video_k, video_v, audio_k, audio_v) = refs[:SIDE], refs[SIDE:]
    rows = video_k.shape[1]
    for index, video, audio in ((0, video_k, audio_k), (1, video_v, audio_v)):
        video[0] = total_of(parts, index, slice(0, rows)).astype(BF16)
        audio[0] = total_of(parts, index, slice(rows, None)).astype(BF16)


def finish_keys(parts, video_rows, audio_rows):
    width = parts[0].shape[2]
    video, audio = like(1, video_rows, width), like(1, audio_rows, width)
    return pl.pallas_call(
        finish_keys_kernel,
        out_shape=[video, video, audio, audio],
        compiler_params=pltpu.CompilerParams(vmem_limit_bytes=8 * 2**20),
        name="finish_keys",
    )(*parts)


def own_audio(array, vid_size, aud_size):
    pairs = [
        (v * aud_size + a, (2 * a + v % 2) * aud_size + v // 2) for v in range(vid_size) for a in range(aud_size)
    ]
    return lax.ppermute(array, ("vid", "aud"), pairs)


def fenced(holds, function, *arrays):
    outs = jax.eval_shape(function, *arrays)
    return lax.cond(
        holds, function, lambda *_: jax.tree.map(lambda out: jnp.zeros(out.shape, out.dtype), outs), *arrays
    )


def shards(
    video_q, video_k, video_v, audio_q, audio_k, audio_v, video_gate, audio_gate, audio_len, d_video_out, d_audio_out
):
    vid = lax.axis_index("vid")
    sizes = lax.axis_size("vid"), lax.axis_size("aud")
    video_rows, audio_rows = video_q.shape[1], d_audio_out.shape[1]
    holds = audio_len[0] > 0
    send_audio, video_kv, queries = prepare(
        audio_q, audio_k, audio_v, video_q, video_k, video_v, d_video_out, d_audio_out
    )

    def video_chunks(video_kv, queries):
        return tuple(gathered(video_kv, along_z)[1:]), all_along_x(queries)

    audio = own_audio(send_audio, *sizes)
    video_keys, queries = fenced(holds, video_chunks, video_kv, queries)
    audio, queries = lax.optimization_barrier((audio, queries))
    video_keys = [video_kv, *video_keys]
    audio_queries = gathered(audio[0], along_x)
    audio_keys = gathered(audio[1:], along_z)
    gates = jnp.stack([video_gate, audio_gate])
    column, row = vid // SIDE, vid % SIDE
    limits = [audio_len[0] - (column * SIDE + (row - p) % SIDE) * audio_rows for p in range(SIDE)]
    numbers = jnp.stack([*limits, column])
    *by_head, stats, audio_queries = attention_forward(
        queries, audio_queries, video_keys, audio_keys, numbers, gates, video_rows
    )
    key_parts, query_parts = attention_backward(
        queries, audio_queries, video_keys, audio_keys, gathered(stats, along_x), gates, by_head, video_rows
    )

    def query_results(parts):
        parts = lax.all_to_all(parts, "vid", 0, 0, axis_index_groups=ALONG_X, tiled=True)
        *results, gate = finish_queries(parts, video_rows, audio_rows)
        for distance in (1, 2):
            gate = gate + beside_z(gate, distance)
        return (*results, gate)

    video_out, audio_out, grad_video_q, grad_audio_q, gate = fenced(holds, query_results, query_parts)
    key_parts = returned(key_parts, along_z)
    gate = gate + lax.ppermute(gate, "pair", [(0, 1), (1, 0)])
    grad_video_k, grad_video_v, grad_audio_k, grad_audio_v = finish_keys(key_parts, video_rows, audio_rows)
    return (
        video_out,
        audio_out,
        grad_video_q,
        grad_video_k,
        grad_video_v,
        grad_audio_q,
        grad_audio_k,
        grad_audio_v,
        gate[0],
        gate[7],
    )


def solution(mesh):
    split = P("pair", "vid", "aud")
    rows = P("pair", "aud", None)
    return jax.shard_map(
        shards,
        mesh=mesh,
        in_specs=(split, split, split, rows, rows, rows, P("aud"), P("aud"), P("pair"), split, split),
        out_specs=(split,) * 8 + (P("aud"), P("aud")),
        check_vma=False,
    )
```

```python
import functools

import jax
import jax.numpy as jnp
from jax import lax
from jax.experimental import pallas as pl
from jax.experimental.pallas import tpu as pltpu
from jax.sharding import PartitionSpec as P

HEAD_DIM = 128
SCALE = HEAD_DIM ** (-0.5)
SIDE = 4
F32 = jnp.float32
BF16 = jnp.bfloat16
VIDEO, AUDIO = 0, 1
GATE_ROWS = 16
VMEM = 60 * 2**20

ALONG_X = [[x * SIDE + z for x in range(SIDE)] for z in range(SIDE)]


def along_x(array, shift):
    pairs = [(x * SIDE + z, (x + shift) % SIDE * SIDE + z) for x in range(SIDE) for z in range(SIDE)]
    return lax.ppermute(array, "vid", pairs)


def along_z(array, shift):
    pairs = [(x * SIDE + z, x * SIDE + (z + shift) % SIDE) for x in range(SIDE) for z in range(SIDE)]
    return lax.ppermute(array, "vid", pairs)


def beside_z(array, distance):
    pairs = [(x * SIDE + z, x * SIDE + (z ^ distance)) for x in range(SIDE) for z in range(SIDE)]
    return lax.ppermute(array, "vid", pairs)


def all_along_x(array):
    return lax.all_gather(array, "vid", axis=0, axis_index_groups=ALONG_X)


def gathered(array, along):
    return [array] + [along(array, shift) for shift in range(1, SIDE)]


def returned(parts, along):
    return [parts[0]] + [along(parts[place], SIDE - place) for place in range(1, SIDE)]


def nt(a, b):
    return lax.dot_general(a, b, (((1,), (1,)), ((), ())), preferred_element_type=F32)


def nn(a, b):
    return lax.dot_general(a, b, (((1,), (0,)), ((), ())), preferred_element_type=F32)


def joined(refs, index):
    return jnp.concatenate([ref[index] for ref in refs], axis=0)


def gated(rows, gate_row):
    return (gate_row * rows.astype(F32)).astype(BF16)


def flat(block):
    return block.reshape(-1, block.shape[-1])


def queries_of(gathered_ref, audio_ref, video_rows):
    return jnp.concatenate([flat(gathered_ref[:, :video_rows]), flat(audio_ref[...])], axis=0)


def upstreams_of(gathered_ref, video_rows):
    return flat(gathered_ref[:, video_rows : 2 * video_rows]), flat(gathered_ref[:, 2 * video_rows :])


def upstream(gathered_ref, gates_ref, video_rows, part):
    video, audio = upstreams_of(gathered_ref, video_rows)
    if part == VIDEO:
        audio = gated(audio, gates_ref[1:2, :])
    else:
        video = gated(video, gates_ref[0:1, :])
    return jnp.concatenate([video, audio], axis=0)


def prepare_kernel(aq_ref, ak_ref, av_ref, vq_ref, vk_ref, vv_ref, dv_ref, da_ref, audio, video_kv, queries, sems):
    vid = lax.axis_index("vid")
    rows, width = vq_ref.shape[1:]
    audio_rows = da_ref.shape[1]
    taken = pl.ds(pl.multiple_of(lax.rem(vid, 2) * audio_rows, audio_rows), audio_rows)
    columns = pl.ds(pl.multiple_of(lax.div(vid, 2) * width, HEAD_DIM), width)
    pairs = [(ref.at[0, taken, columns], audio.at[index]) for index, ref in enumerate((aq_ref, ak_ref, av_ref))]
    pairs += [(vk_ref.at[0], video_kv.at[0]), (vv_ref.at[0], video_kv.at[1])]
    pairs += [(vq_ref.at[0], queries.at[pl.ds(0, rows)]), (dv_ref.at[0], queries.at[pl.ds(rows, rows)])]
    pairs += [(da_ref.at[0], queries.at[pl.ds(2 * rows, audio_rows)])]
    copies = [pltpu.make_async_copy(source, target, sems.at[index]) for index, (source, target) in enumerate(pairs)]
    for copy in copies:
        copy.start()
    for copy in copies:
        copy.wait()


def prepare(audio_q, audio_k, audio_v, video_q, video_k, video_v, d_video, d_audio):
    _, video_rows, width = video_q.shape
    audio_rows = d_audio.shape[1]
    given = (audio_q, audio_k, audio_v, video_q, video_k, video_v, d_video, d_audio)
    shapes = [(3, audio_rows, width), (2, video_rows, width), (2 * video_rows + audio_rows, width)]
    return pl.pallas_call(
        prepare_kernel,
        in_specs=[pl.BlockSpec(memory_space=pl.ANY)] * len(given),
        out_specs=[pl.BlockSpec(memory_space=pltpu.VMEM)] * len(shapes),
        out_shape=[like(*shape) for shape in shapes],
        scratch_shapes=[pltpu.SemaphoreType.DMA((len(given),))],
        compiler_params=pltpu.CompilerParams(vmem_limit_bytes=VMEM),
        name="prepare",
    )(*given)


def forward_kernel(video_rows, *refs):
    gathered_ref, k_refs, audio_q, numbers_ref, gates_ref = refs[0], (refs[1:5], refs[5:9]), refs[9:13], refs[13], refs[14]
    e_refs, o_ref, stats_ref, ordered_ref = refs[15:17], refs[17], refs[18], refs[19]
    for place in range(SIDE):
        ordered_ref[lax.rem(numbers_ref[SIDE] + SIDE - place, SIDE)] = audio_q[place][...]
    queries = queries_of(gathered_ref, ordered_ref, video_rows)
    stats = []
    for part in (VIDEO, AUDIO):
        raw = nt(joined(k_refs[part], 0), queries)
        if part == AUDIO:
            rows = k_refs[part][0].shape[1]
            position = lax.broadcasted_iota(jnp.int32, (rows, raw.shape[1]), 0)
            pieces = [raw[place * rows : (place + 1) * rows] for place in range(SIDE)]
            pieces = [jnp.where(position < numbers_ref[place], pieces[place], -1e30) for place in range(SIDE)]
            raw = jnp.concatenate(pieces, axis=0)
        peak = jnp.max(raw, axis=0, keepdims=True)
        expon = jnp.exp((raw - peak) * SCALE)
        total = jnp.sum(expon, axis=0, keepdims=True)
        expon = (expon * (1.0 / total)).astype(BF16)
        e_refs[part][0] = expon
        output = nn(joined(k_refs[part], 1).T, expon)
        o_ref[0, part] = output
        up = upstream(gathered_ref, gates_ref, video_rows, part)
        stats.append(peak * SCALE + jnp.log(total))
        stats.append(jnp.sum(up.astype(F32).T * output, axis=0, keepdims=True))
    stats_ref[0] = jnp.concatenate(stats, axis=0)


def merged_stats(refs, part):
    logs = [ref[0, 2 * part : 2 * part + 1] for ref in refs]
    peak = functools.reduce(jnp.maximum, logs)
    weights = [jnp.exp(local - peak) for local in logs]
    scale = 1.0 / sum(weights)
    delta = sum(weight * ref[0, 2 * part + 1 : 2 * part + 2] for weight, ref in zip(weights, refs)) * scale
    return weights[0] * scale, delta


def backward_keys(part, queries, up, stats_refs, k_refs, e_ref, k_outs, first):
    factor, delta = merged_stats(stats_refs, part)
    probs = e_ref[0].astype(F32) * factor
    grad_values = nn(probs.astype(BF16), up).astype(BF16)
    grad_probs = nt(joined(k_refs, 1), up)
    grad_scores = (probs * (grad_probs - delta)).astype(BF16)
    grad_keys = (nn(grad_scores, queries) * SCALE).astype(BF16)
    rows = k_refs[0].shape[1]
    for place in range(SIDE):
        k_outs[place][0, first : first + rows] = grad_keys[place * rows : (place + 1) * rows]
        k_outs[place][1, first : first + rows] = grad_values[place * rows : (place + 1) * rows]
    return nn(joined(k_refs, 0).T, grad_scores), factor


def column_of(row):
    return jnp.broadcast_to(row, (HEAD_DIM, HEAD_DIM)).T[:, 0:1]


def backward_kernel(video_rows, *refs):
    gathered_ref, audio_q, k_video, k_audio, stats_refs = refs[0], refs[1], refs[2:6], refs[6:10], refs[10:14]
    gates_ref, e_video, e_audio, o_ref = refs[14:18]
    k_outs, q_out = refs[18:22], refs[22]
    audio_rows = audio_q.shape[1]
    rows = video_rows + audio_rows
    video = SIDE * video_rows
    queries = queries_of(gathered_ref, audio_q, video_rows)
    up = upstream(gathered_ref, gates_ref, video_rows, VIDEO)
    term_video, factor = backward_keys(VIDEO, queries, up, stats_refs, k_video, e_video, k_outs, 0)
    on_video = o_ref[0, VIDEO] * factor
    up = upstream(gathered_ref, gates_ref, video_rows, AUDIO)
    term_audio, factor = backward_keys(AUDIO, queries, up, stats_refs, k_audio, e_audio, k_outs, video_rows)
    on_audio = o_ref[0, AUDIO] * factor
    grad_queries = term_video + term_audio
    cross_video, cross_audio = on_audio[:, :video], on_video[:, video:]
    merged = jnp.concatenate(
        [
            on_video[:, :video] + column_of(gates_ref[0:1, :]) * cross_video,
            on_audio[:, video:] + column_of(gates_ref[1:2, :]) * cross_audio,
        ],
        axis=1,
    )
    up_video, up_audio = upstreams_of(gathered_ref, video_rows)
    video_sum = jnp.sum(up_video.astype(F32).T * cross_video, axis=1, keepdims=True)
    audio_sum = jnp.sum(up_audio.astype(F32).T * cross_audio, axis=1, keepdims=True)
    sums = jnp.concatenate(
        [jnp.broadcast_to(video_sum, (HEAD_DIM, 4)), jnp.broadcast_to(audio_sum, (HEAD_DIM, HEAD_DIM - 4))], axis=1
    ).T[0:GATE_ROWS]
    high = sums.astype(BF16)
    low = (sums - high.astype(F32)).astype(BF16)
    even = lax.broadcasted_iota(jnp.int32, sums.shape, 0) % 2 == 0
    sums = jnp.where(even, high.astype(F32), low.astype(F32)).astype(BF16)
    merged = merged.T.astype(BF16)
    grad_queries = (grad_queries.T * SCALE).astype(BF16)
    for index, array in ((0, merged), (1, grad_queries)):
        first = index * rows
        q_out[:, first : first + video_rows] = array[:video].reshape(SIDE, video_rows, HEAD_DIM)
        q_out[:, first + video_rows : first + rows] = array[video:].reshape(SIDE, audio_rows, HEAD_DIM)
    q_out[:, 2 * rows :] = jnp.broadcast_to(sums, (SIDE, *sums.shape))


def chunk_spec(array):
    shape = array.shape[:-1]
    return pl.BlockSpec((*shape, HEAD_DIM), lambda h: (0,) * len(shape) + (h,))


def head_spec(array):
    shape = array.shape[1:]
    return pl.BlockSpec((1, *shape), lambda h: (h,) + (0,) * len(shape))


def like(*shape, kind=BF16):
    return jax.ShapeDtypeStruct(shape, kind)


def cost(keys, queries, heads, products):
    return pl.CostEstimate(
        flops=2 * products * heads * keys * queries * HEAD_DIM,
        bytes_accessed=4 * heads * keys * queries,
        transcendentals=heads * keys * queries,
    )


def attention_forward(queries, audio_q, video_keys, audio_keys, numbers, gates, video_rows):
    heads = gates.shape[1] // HEAD_DIM
    audio_rows, width = audio_q[0].shape
    video, audio = SIDE * video_rows, SIDE * audio_rows
    total = video + audio
    outs = [
        like(heads, video, total),
        like(heads, audio, total),
        like(heads, 2, HEAD_DIM, total, kind=F32),
        like(heads, 4, total, kind=F32),
    ]
    ordered = like(SIDE, audio_rows, width)
    chunks = [queries, *video_keys, *audio_keys, *audio_q]
    return pl.pallas_call(
        functools.partial(forward_kernel, video_rows),
        grid=(heads,),
        in_specs=[chunk_spec(array) for array in chunks] + [pl.BlockSpec(memory_space=pltpu.SMEM), chunk_spec(gates)],
        out_specs=[head_spec(array) for array in outs] + [chunk_spec(ordered)],
        out_shape=[*outs, ordered],
        cost_estimate=cost(total, total, heads, 2),
        compiler_params=pltpu.CompilerParams(vmem_limit_bytes=VMEM),
        name="forward",
    )(*chunks, numbers, gates)


def attention_backward(queries, audio_q, video_keys, audio_keys, stats, gates, by_head, video_rows):
    width = gates.shape[1]
    heads = width // HEAD_DIM
    rows = video_rows + audio_q.shape[1]
    outs = [like(2, rows, width)] * SIDE + [like(SIDE, 2 * rows + GATE_ROWS, width)]
    chunks = [queries, audio_q, *video_keys, *audio_keys]
    *key_parts, query_parts = pl.pallas_call(
        functools.partial(backward_kernel, video_rows),
        grid=(heads,),
        in_specs=[chunk_spec(array) for array in chunks]
        + [head_spec(array) for array in stats]
        + [chunk_spec(gates)]
        + [head_spec(array) for array in by_head],
        out_specs=[chunk_spec(array) for array in outs],
        out_shape=outs,
        cost_estimate=cost(SIDE * rows, SIDE * rows, heads, 4),
        compiler_params=pltpu.CompilerParams(vmem_limit_bytes=VMEM),
        name="backward",
    )(*chunks, *stats, gates, *by_head)
    return key_parts, query_parts


def total_of(refs, *index):
    return sum(ref[index].astype(F32) for ref in refs)


def finish_queries_kernel(parts_ref, video_out, audio_out, video_q, audio_q, gate_ref):
    video_rows, audio_rows = video_out.shape[1], audio_out.shape[1]
    rows = video_rows + audio_rows
    parts = [parts_ref.at[place] for place in range(SIDE)]
    for index, video, audio in ((0, video_out, audio_out), (1, video_q, audio_q)):
        first = index * rows
        video[0] = total_of(parts, slice(first, first + video_rows)).astype(BF16)
        audio[0] = total_of(parts, slice(first + video_rows, first + rows)).astype(BF16)
    gates = total_of(parts, slice(2 * rows, None))
    width = gates.shape[1]
    video_gate = jnp.broadcast_to(gates[0:1] + gates[1:2], (4, width))
    audio_gate = jnp.broadcast_to(gates[4:5] + gates[5:6], (4, width))
    gate_ref[...] = jnp.concatenate([video_gate, audio_gate], axis=0)


def finish_queries(parts, video_rows, audio_rows):
    width = parts.shape[2]
    video, audio = like(1, video_rows, width), like(1, audio_rows, width)
    return pl.pallas_call(
        finish_queries_kernel,
        out_shape=[video, audio, video, audio, like(8, width, kind=F32)],
        compiler_params=pltpu.CompilerParams(vmem_limit_bytes=8 * 2**20),
        name="finish_queries",
    )(parts)


def finish_keys_kernel(*refs):
    parts, (video_k, video_v, audio_k, audio_v) = refs[:SIDE], refs[SIDE:]
    rows = video_k.shape[1]
    for index, video, audio in ((0, video_k, audio_k), (1, video_v, audio_v)):
        video[0] = total_of(parts, index, slice(0, rows)).astype(BF16)
        audio[0] = total_of(parts, index, slice(rows, None)).astype(BF16)


def finish_keys(parts, video_rows, audio_rows):
    width = parts[0].shape[2]
    video, audio = like(1, video_rows, width), like(1, audio_rows, width)
    return pl.pallas_call(
        finish_keys_kernel,
        out_shape=[video, video, audio, audio],
        compiler_params=pltpu.CompilerParams(vmem_limit_bytes=8 * 2**20),
        name="finish_keys",
    )(*parts)


def own_audio(array, vid_size, aud_size):
    pairs = [
        (v * aud_size + a, (2 * a + v % 2) * aud_size + v // 2) for v in range(vid_size) for a in range(aud_size)
    ]
    return lax.ppermute(array, ("vid", "aud"), pairs)


def fenced(holds, function, *arrays):
    outs = jax.eval_shape(function, *arrays)
    return lax.cond(
        holds, function, lambda *_: jax.tree.map(lambda out: jnp.zeros(out.shape, out.dtype), outs), *arrays
    )


def shards(
    video_q, video_k, video_v, audio_q, audio_k, audio_v, video_gate, audio_gate, audio_len, d_video_out, d_audio_out
):
    vid = lax.axis_index("vid")
    sizes = lax.axis_size("vid"), lax.axis_size("aud")
    video_rows, audio_rows = video_q.shape[1], d_audio_out.shape[1]
    holds = audio_len[0] > 0
    send_audio, video_kv, queries = prepare(
        audio_q, audio_k, audio_v, video_q, video_k, video_v, d_video_out, d_audio_out
    )

    def first_chunks(send_audio, video_kv, queries):
        return own_audio(send_audio, *sizes), tuple(gathered(video_kv, along_z)[1:]), all_along_x(queries)

    audio, video_keys, queries = fenced(holds, first_chunks, send_audio, video_kv, queries)
    video_keys = [video_kv, *video_keys]
    audio = lax.optimization_barrier(audio)
    audio_keys = gathered(audio[1:], along_z)
    audio_queries = gathered(audio[0], along_x)
    gates = jnp.stack([video_gate, audio_gate])
    column, row = vid // SIDE, vid % SIDE
    limits = [audio_len[0] - (column * SIDE + (row - p) % SIDE) * audio_rows for p in range(SIDE)]
    numbers = jnp.stack([*limits, column])
    *by_head, stats, audio_queries = attention_forward(
        queries, audio_queries, video_keys, audio_keys, numbers, gates, video_rows
    )
    key_parts, query_parts = attention_backward(
        queries, audio_queries, video_keys, audio_keys, gathered(stats, along_x), gates, by_head, video_rows
    )

    def query_results(parts):
        parts = lax.all_to_all(parts, "vid", 0, 0, axis_index_groups=ALONG_X, tiled=True)
        *results, gate = finish_queries(parts, video_rows, audio_rows)
        for distance in (1, 2):
            gate = gate + beside_z(gate, distance)
        return (*results, gate)

    video_out, audio_out, grad_video_q, grad_audio_q, gate = fenced(holds, query_results, query_parts)
    key_parts = returned(key_parts, along_z)
    gate = gate + lax.ppermute(gate, "pair", [(0, 1), (1, 0)])
    grad_video_k, grad_video_v, grad_audio_k, grad_audio_v = finish_keys(key_parts, video_rows, audio_rows)
    return (
        video_out,
        audio_out,
        grad_video_q,
        grad_video_k,
        grad_video_v,
        grad_audio_q,
        grad_audio_k,
        grad_audio_v,
        gate[0],
        gate[7],
    )


def solution(mesh):
    split = P("pair", "vid", "aud")
    rows = P("pair", "aud", None)
    return jax.shard_map(
        shards,
        mesh=mesh,
        in_specs=(split, split, split, rows, rows, rows, P("aud"), P("aud"), P("pair"), split, split),
        out_specs=(split,) * 8 + (P("aud"), P("aud")),
        check_vma=False,
    )
```

```python
import functools

import jax
import jax.numpy as jnp
from jax import lax
from jax.experimental import pallas as pl
from jax.experimental.pallas import tpu as pltpu
from jax.sharding import PartitionSpec as P

HEAD_DIM = 128
SCALE = HEAD_DIM ** (-0.5)
SIDE = 4
F32 = jnp.float32
BF16 = jnp.bfloat16
VIDEO, AUDIO = 0, 1
GATE_ROWS = 16
VMEM = 60 * 2**20

ALONG_X = [[x * SIDE + z for x in range(SIDE)] for z in range(SIDE)]


def along_x(array, shift):
    pairs = [(x * SIDE + z, (x + shift) % SIDE * SIDE + z) for x in range(SIDE) for z in range(SIDE)]
    return lax.ppermute(array, "vid", pairs)


def along_z(array, shift):
    pairs = [(x * SIDE + z, x * SIDE + (z + shift) % SIDE) for x in range(SIDE) for z in range(SIDE)]
    return lax.ppermute(array, "vid", pairs)


def beside_z(array, distance):
    pairs = [(x * SIDE + z, x * SIDE + (z ^ distance)) for x in range(SIDE) for z in range(SIDE)]
    return lax.ppermute(array, "vid", pairs)


def across_x(array):
    return lax.all_to_all(array, "vid", 0, 0, axis_index_groups=ALONG_X, tiled=True)


def gathered(array, along):
    return [array] + [along(array, shift) for shift in range(1, SIDE)]


def returned(parts, along):
    return [parts[0]] + [along(parts[place], SIDE - place) for place in range(1, SIDE)]


def nt(a, b):
    return lax.dot_general(a, b, (((1,), (1,)), ((), ())), preferred_element_type=F32)


def nn(a, b):
    return lax.dot_general(a, b, (((1,), (0,)), ((), ())), preferred_element_type=F32)


def gated(rows, gate_row):
    return (gate_row * rows.astype(F32)).astype(BF16)


def flat(block):
    return block.reshape(-1, block.shape[-1])


def queries_of(gathered_ref, video_rows):
    audio_rows = gathered_ref.shape[1] // 2 - video_rows
    return jnp.concatenate([flat(gathered_ref[:, :video_rows]), flat(gathered_ref[:, -audio_rows:])], axis=0)


def upstreams_of(gathered_ref, video_rows):
    audio_rows = gathered_ref.shape[1] // 2 - video_rows
    return flat(gathered_ref[:, video_rows : 2 * video_rows]), flat(gathered_ref[:, 2 * video_rows : -audio_rows])


def keys_of(refs, part, index, video_rows):
    own, video_1, audio_1, both_2, video_3, audio_3 = refs
    if part == VIDEO:
        pieces = [own[index, :video_rows], video_1[index], both_2[index, :video_rows], video_3[index]]
    else:
        pieces = [own[index, video_rows:], audio_1[index], both_2[index, video_rows:], audio_3[index]]
    return jnp.concatenate(pieces, axis=0)


def upstream(gathered_ref, gates_ref, video_rows, part):
    video, audio = upstreams_of(gathered_ref, video_rows)
    if part == VIDEO:
        audio = gated(audio, gates_ref[1:2, :])
    else:
        video = gated(video, gates_ref[0:1, :])
    return jnp.concatenate([video, audio], axis=0)


def prepare_kernel(
    aq_ref, ak_ref, av_ref, vq_ref, vk_ref, vv_ref, dv_ref, da_ref, audio, video_kv, keys, queries, sems
):
    vid = lax.axis_index("vid")
    rows, width = vq_ref.shape[1:]
    audio_rows = da_ref.shape[1]
    taken = pl.ds(pl.multiple_of(lax.rem(vid, 2) * audio_rows, audio_rows), audio_rows)
    columns = pl.ds(pl.multiple_of(lax.div(vid, 2) * width, HEAD_DIM), width)
    pairs = [(ref.at[0, taken, columns], audio.at[index]) for index, ref in enumerate((aq_ref, ak_ref, av_ref))]
    for index, ref in enumerate((vk_ref, vv_ref)):
        pairs += [(ref.at[0], video_kv.at[index]), (ref.at[0], keys.at[index, pl.ds(0, rows)])]
    for place in range(SIDE):
        pairs += [(vq_ref.at[0], queries.at[place, pl.ds(0, rows)])]
        pairs += [(dv_ref.at[0], queries.at[place, pl.ds(rows, rows)])]
        pairs += [(da_ref.at[0], queries.at[place, pl.ds(2 * rows, audio_rows)])]
    copies = [pltpu.make_async_copy(source, target, sems.at[index]) for index, (source, target) in enumerate(pairs)]
    for copy in copies:
        copy.start()
    for copy in copies:
        copy.wait()


def prepare(audio_q, audio_k, audio_v, video_q, video_k, video_v, d_video, d_audio):
    _, video_rows, width = video_q.shape
    audio_rows = d_audio.shape[1]
    rows = video_rows + audio_rows
    given = (audio_q, audio_k, audio_v, video_q, video_k, video_v, d_video, d_audio)
    shapes = [(3, audio_rows, width), (2, video_rows, width), (2, rows, width), (SIDE, 2 * rows, width)]
    return pl.pallas_call(
        prepare_kernel,
        in_specs=[pl.BlockSpec(memory_space=pl.ANY)] * len(given),
        out_specs=[pl.BlockSpec(memory_space=pltpu.VMEM)] * len(shapes),
        out_shape=[like(*shape) for shape in shapes],
        scratch_shapes=[pltpu.SemaphoreType.DMA((7 + 3 * SIDE,))],
        compiler_params=pltpu.CompilerParams(vmem_limit_bytes=VMEM),
        name="prepare",
    )(*given)


def forward_kernel(video_rows, *refs):
    gathered_ref, k_refs, numbers_ref, gates_ref = refs[0], refs[1:7], refs[7], refs[8]
    e_refs, o_ref, stats_ref = refs[9:11], refs[11], refs[12]
    queries = queries_of(gathered_ref, video_rows)
    stats = []
    for part in (VIDEO, AUDIO):
        raw = nt(keys_of(k_refs, part, 0, video_rows), queries)
        if part == AUDIO:
            rows = raw.shape[0] // SIDE
            position = lax.broadcasted_iota(jnp.int32, (rows, raw.shape[1]), 0)
            pieces = [raw[place * rows : (place + 1) * rows] for place in range(SIDE)]
            pieces = [jnp.where(position < numbers_ref[place], pieces[place], -1e30) for place in range(SIDE)]
            raw = jnp.concatenate(pieces, axis=0)
        peak = jnp.max(raw, axis=0, keepdims=True)
        expon = jnp.exp((raw - peak) * SCALE)
        total = jnp.sum(expon, axis=0, keepdims=True)
        expon = (expon * (1.0 / total)).astype(BF16)
        e_refs[part][0] = expon
        output = nn(keys_of(k_refs, part, 1, video_rows).T, expon)
        o_ref[0, part] = output
        up = upstream(gathered_ref, gates_ref, video_rows, part)
        stats.append(peak * SCALE + jnp.log(total))
        stats.append(jnp.sum(up.astype(F32).T * output, axis=0, keepdims=True))
    stats_ref[0] = jnp.concatenate(stats, axis=0)


def merged_stats(refs, part):
    logs = [ref[0, 2 * part : 2 * part + 1] for ref in refs]
    peak = functools.reduce(jnp.maximum, logs)
    weights = [jnp.exp(local - peak) for local in logs]
    scale = 1.0 / sum(weights)
    delta = sum(weight * ref[0, 2 * part + 1 : 2 * part + 2] for weight, ref in zip(weights, refs)) * scale
    return weights[0] * scale, delta


def backward_keys(part, queries, up, stats_refs, k_refs, e_ref, k_outs, video_rows):
    factor, delta = merged_stats(stats_refs, part)
    probs = e_ref[0].astype(F32) * factor
    grad_values = nn(probs.astype(BF16), up).astype(BF16)
    grad_probs = nt(keys_of(k_refs, part, 1, video_rows), up)
    grad_scores = (probs * (grad_probs - delta)).astype(BF16)
    grad_keys = (nn(grad_scores, queries) * SCALE).astype(BF16)
    rows, first = probs.shape[0] // SIDE, part * video_rows
    for place in range(SIDE):
        k_outs[place][0, first : first + rows] = grad_keys[place * rows : (place + 1) * rows]
        k_outs[place][1, first : first + rows] = grad_values[place * rows : (place + 1) * rows]
    return nn(keys_of(k_refs, part, 0, video_rows).T, grad_scores), factor


def column_of(row):
    return jnp.broadcast_to(row, (HEAD_DIM, HEAD_DIM)).T[:, 0:1]


def backward_kernel(video_rows, *refs):
    gathered_ref, k_refs, stats_refs = refs[0], refs[1:7], refs[7:11]
    gates_ref, e_video, e_audio, o_ref = refs[11:15]
    k_outs, q_out = refs[15:19], refs[19]
    rows = gathered_ref.shape[1] // 2
    audio_rows = rows - video_rows
    video = SIDE * video_rows
    queries = queries_of(gathered_ref, video_rows)
    up = upstream(gathered_ref, gates_ref, video_rows, VIDEO)
    term_video, factor = backward_keys(VIDEO, queries, up, stats_refs, k_refs, e_video, k_outs, video_rows)
    on_video = o_ref[0, VIDEO] * factor
    up = upstream(gathered_ref, gates_ref, video_rows, AUDIO)
    term_audio, factor = backward_keys(AUDIO, queries, up, stats_refs, k_refs, e_audio, k_outs, video_rows)
    on_audio = o_ref[0, AUDIO] * factor
    grad_queries = term_video + term_audio
    cross_video, cross_audio = on_audio[:, :video], on_video[:, video:]
    merged = jnp.concatenate(
        [
            on_video[:, :video] + column_of(gates_ref[0:1, :]) * cross_video,
            on_audio[:, video:] + column_of(gates_ref[1:2, :]) * cross_audio,
        ],
        axis=1,
    )
    up_video, up_audio = upstreams_of(gathered_ref, video_rows)
    video_sum = jnp.sum(up_video.astype(F32).T * cross_video, axis=1, keepdims=True)
    audio_sum = jnp.sum(up_audio.astype(F32).T * cross_audio, axis=1, keepdims=True)
    sums = jnp.concatenate(
        [jnp.broadcast_to(video_sum, (HEAD_DIM, 4)), jnp.broadcast_to(audio_sum, (HEAD_DIM, HEAD_DIM - 4))], axis=1
    ).T[0:GATE_ROWS]
    high = sums.astype(BF16)
    low = (sums - high.astype(F32)).astype(BF16)
    even = lax.broadcasted_iota(jnp.int32, sums.shape, 0) % 2 == 0
    sums = jnp.where(even, high.astype(F32), low.astype(F32)).astype(BF16)
    merged = merged.T.astype(BF16)
    grad_queries = (grad_queries.T * SCALE).astype(BF16)
    for index, array in ((0, merged), (1, grad_queries)):
        first = index * rows
        q_out[:, first : first + video_rows] = array[:video].reshape(SIDE, video_rows, HEAD_DIM)
        q_out[:, first + video_rows : first + rows] = array[video:].reshape(SIDE, audio_rows, HEAD_DIM)
    q_out[:, 2 * rows :] = jnp.broadcast_to(sums, (SIDE, *sums.shape))


def chunk_spec(array):
    shape = array.shape[:-1]
    return pl.BlockSpec((*shape, HEAD_DIM), lambda h: (0,) * len(shape) + (h,))


def head_spec(array):
    shape = array.shape[1:]
    return pl.BlockSpec((1, *shape), lambda h: (h,) + (0,) * len(shape))


def like(*shape, kind=BF16):
    return jax.ShapeDtypeStruct(shape, kind)


def cost(keys, queries, heads, products):
    return pl.CostEstimate(
        flops=2 * products * heads * keys * queries * HEAD_DIM,
        bytes_accessed=4 * heads * keys * queries,
        transcendentals=heads * keys * queries,
    )


def attention_forward(queries, keys, numbers, gates, video_rows):
    heads = gates.shape[1] // HEAD_DIM
    total = SIDE * (queries.shape[1] // 2)
    video = SIDE * video_rows
    outs = [
        like(heads, video, total),
        like(heads, total - video, total),
        like(heads, 2, HEAD_DIM, total, kind=F32),
        like(heads, 4, total, kind=F32),
    ]
    chunks = [queries, *keys]
    return pl.pallas_call(
        functools.partial(forward_kernel, video_rows),
        grid=(heads,),
        in_specs=[chunk_spec(array) for array in chunks] + [pl.BlockSpec(memory_space=pltpu.SMEM), chunk_spec(gates)],
        out_specs=[head_spec(array) for array in outs],
        out_shape=outs,
        cost_estimate=cost(total, total, heads, 2),
        compiler_params=pltpu.CompilerParams(vmem_limit_bytes=VMEM),
        name="forward",
    )(*chunks, numbers, gates)


def attention_backward(queries, keys, stats, gates, by_head, video_rows):
    width = gates.shape[1]
    heads = width // HEAD_DIM
    rows = queries.shape[1] // 2
    outs = [like(2, rows, width)] * SIDE + [like(SIDE, 2 * rows + GATE_ROWS, width)]
    chunks = [queries, *keys]
    *key_parts, query_parts = pl.pallas_call(
        functools.partial(backward_kernel, video_rows),
        grid=(heads,),
        in_specs=[chunk_spec(array) for array in chunks]
        + [head_spec(array) for array in stats]
        + [chunk_spec(gates)]
        + [head_spec(array) for array in by_head],
        out_specs=[chunk_spec(array) for array in outs],
        out_shape=outs,
        cost_estimate=cost(SIDE * rows, SIDE * rows, heads, 4),
        compiler_params=pltpu.CompilerParams(vmem_limit_bytes=VMEM),
        name="backward",
    )(*chunks, *stats, gates, *by_head)
    return key_parts, query_parts


def total_of(refs, *index):
    return sum(ref[index].astype(F32) for ref in refs)


def finish_queries_kernel(parts_ref, video_out, audio_out, video_q, audio_q, gate_ref):
    video_rows, audio_rows = video_out.shape[1], audio_out.shape[1]
    rows = video_rows + audio_rows
    parts = [parts_ref.at[place] for place in range(SIDE)]
    for index, video, audio in ((0, video_out, audio_out), (1, video_q, audio_q)):
        first = index * rows
        video[0] = total_of(parts, slice(first, first + video_rows)).astype(BF16)
        audio[0] = total_of(parts, slice(first + video_rows, first + rows)).astype(BF16)
    gates = total_of(parts, slice(2 * rows, None))
    width = gates.shape[1]
    video_gate = jnp.broadcast_to(gates[0:1] + gates[1:2], (4, width))
    audio_gate = jnp.broadcast_to(gates[4:5] + gates[5:6], (4, width))
    gate_ref[...] = jnp.concatenate([video_gate, audio_gate], axis=0)


def finish_queries(parts, video_rows, audio_rows):
    width = parts.shape[2]
    video, audio = like(1, video_rows, width), like(1, audio_rows, width)
    return pl.pallas_call(
        finish_queries_kernel,
        out_shape=[video, audio, video, audio, like(8, width, kind=F32)],
        compiler_params=pltpu.CompilerParams(vmem_limit_bytes=8 * 2**20),
        name="finish_queries",
    )(parts)


def finish_keys_kernel(*refs):
    parts, (video_k, video_v, audio_k, audio_v) = refs[:SIDE], refs[SIDE:]
    rows = video_k.shape[1]
    for index, video, audio in ((0, video_k, audio_k), (1, video_v, audio_v)):
        video[0] = total_of(parts, index, slice(0, rows)).astype(BF16)
        audio[0] = total_of(parts, index, slice(rows, None)).astype(BF16)


def finish_keys(parts, video_rows, audio_rows):
    width = parts[0].shape[2]
    video, audio = like(1, video_rows, width), like(1, audio_rows, width)
    return pl.pallas_call(
        finish_keys_kernel,
        out_shape=[video, video, audio, audio],
        compiler_params=pltpu.CompilerParams(vmem_limit_bytes=8 * 2**20),
        name="finish_keys",
    )(*parts)


def own_audio(array, vid_size, aud_size):
    pairs = [
        (v * aud_size + a, (2 * a + v % 2) * aud_size + v // 2) for v in range(vid_size) for a in range(aud_size)
    ]
    return lax.ppermute(array, ("vid", "aud"), pairs)


def fenced(holds, function, *arrays):
    outs = jax.eval_shape(function, *arrays)
    return lax.cond(
        holds, function, lambda *_: jax.tree.map(lambda out: jnp.zeros(out.shape, out.dtype), outs), *arrays
    )


def shards(
    video_q, video_k, video_v, audio_q, audio_k, audio_v, video_gate, audio_gate, audio_len, d_video_out, d_audio_out
):
    vid = lax.axis_index("vid")
    sizes = lax.axis_size("vid"), lax.axis_size("aud")
    video_rows, audio_rows = video_q.shape[1], d_audio_out.shape[1]
    holds = audio_len[0] > 0
    send_audio, video_kv, keys, queries = prepare(
        audio_q, audio_k, audio_v, video_q, video_k, video_v, d_video_out, d_audio_out
    )

    def first_chunks(send_audio, video_kv):
        return own_audio(send_audio, *sizes), along_z(video_kv, 1), along_z(video_kv, SIDE - 1)

    audio, video_1, video_3 = fenced(holds, first_chunks, send_audio, video_kv)
    audio = lax.optimization_barrier(audio)
    audio_kv = audio[1:]
    keys = lax.dynamic_update_slice(keys, audio_kv, (0, video_rows, 0))
    audio_q = jnp.broadcast_to(audio[0:1], (SIDE, *audio.shape[1:]))
    queries = lax.dynamic_update_slice(queries, audio_q, (0, 2 * video_rows + audio_rows, 0))
    audio_1, audio_3, both_2 = along_z(audio_kv, 1), along_z(audio_kv, SIDE - 1), along_z(keys, 2)
    queries = across_x(queries)
    keys = keys, video_1, audio_1, both_2, video_3, audio_3
    gates = jnp.stack([video_gate, audio_gate])
    column, row = vid // SIDE, vid % SIDE
    limits = jnp.stack([audio_len[0] - (column * SIDE + (row - p) % SIDE) * audio_rows for p in range(SIDE)])
    *by_head, stats = attention_forward(queries, keys, limits, gates, video_rows)
    key_parts, query_parts = attention_backward(
        queries, keys, gathered(stats, along_x), gates, by_head, video_rows
    )

    def query_results(parts):
        parts = across_x(parts)
        *results, gate = finish_queries(parts, video_rows, audio_rows)
        for distance in (1, 2):
            gate = gate + beside_z(gate, distance)
        return (*results, gate)

    video_out, audio_out, grad_video_q, grad_audio_q, gate = fenced(holds, query_results, query_parts)
    key_parts = returned(key_parts, along_z)
    gate = gate + lax.ppermute(gate, "pair", [(0, 1), (1, 0)])
    grad_video_k, grad_video_v, grad_audio_k, grad_audio_v = finish_keys(key_parts, video_rows, audio_rows)
    return (
        video_out,
        audio_out,
        grad_video_q,
        grad_video_k,
        grad_video_v,
        grad_audio_q,
        grad_audio_k,
        grad_audio_v,
        gate[0],
        gate[7],
    )


def solution(mesh):
    split = P("pair", "vid", "aud")
    rows = P("pair", "aud", None)
    return jax.shard_map(
        shards,
        mesh=mesh,
        in_specs=(split, split, split, rows, rows, rows, P("aud"), P("aud"), P("pair"), split, split),
        out_specs=(split,) * 8 + (P("aud"), P("aud")),
        check_vma=False,
    )
```

```python
import functools

import jax
import jax.numpy as jnp
from jax import lax
from jax.experimental import pallas as pl
from jax.experimental.pallas import tpu as pltpu
from jax.sharding import PartitionSpec as P

HEAD_DIM = 128
SCALE = HEAD_DIM ** (-0.5)
SIDE = 4
F32 = jnp.float32
BF16 = jnp.bfloat16
VIDEO, AUDIO = 0, 1
GATE_ROWS = 16
VMEM = 60 * 2**20

ALONG_X = [[x * SIDE + z for x in range(SIDE)] for z in range(SIDE)]


def along_x(array, shift):
    pairs = [(x * SIDE + z, (x + shift) % SIDE * SIDE + z) for x in range(SIDE) for z in range(SIDE)]
    return lax.ppermute(array, "vid", pairs)


def along_z(array, shift):
    pairs = [(x * SIDE + z, x * SIDE + (z + shift) % SIDE) for x in range(SIDE) for z in range(SIDE)]
    return lax.ppermute(array, "vid", pairs)


def beside_z(array, distance):
    pairs = [(x * SIDE + z, x * SIDE + (z ^ distance)) for x in range(SIDE) for z in range(SIDE)]
    return lax.ppermute(array, "vid", pairs)


def across_x(array):
    return lax.all_to_all(array, "vid", 0, 0, axis_index_groups=ALONG_X, tiled=True)


def gathered(array, along):
    return [array] + [along(array, shift) for shift in range(1, SIDE)]


def returned(parts, along):
    return [parts[0]] + [along(parts[place], SIDE - place) for place in range(1, SIDE)]


def nt(a, b):
    return lax.dot_general(a, b, (((1,), (1,)), ((), ())), preferred_element_type=F32)


def nn(a, b):
    return lax.dot_general(a, b, (((1,), (0,)), ((), ())), preferred_element_type=F32)


def gated(rows, gate_row):
    return (gate_row * rows.astype(F32)).astype(BF16)


def flat(block):
    return block.reshape(-1, block.shape[-1])


def queries_of(gathered_ref, video_rows):
    audio_rows = gathered_ref.shape[1] // 2 - video_rows
    return jnp.concatenate([flat(gathered_ref[:, :video_rows]), flat(gathered_ref[:, -audio_rows:])], axis=0)


def upstreams_of(gathered_ref, video_rows):
    audio_rows = gathered_ref.shape[1] // 2 - video_rows
    return flat(gathered_ref[:, video_rows : 2 * video_rows]), flat(gathered_ref[:, 2 * video_rows : -audio_rows])


def keys_of(refs, part, index):
    return jnp.concatenate([ref[index] for ref in refs[SIDE * part : SIDE * (part + 1)]], axis=0)


def upstream(gathered_ref, gates_ref, video_rows, part):
    video, audio = upstreams_of(gathered_ref, video_rows)
    if part == VIDEO:
        audio = gated(audio, gates_ref[1:2, :])
    else:
        video = gated(video, gates_ref[0:1, :])
    return jnp.concatenate([video, audio], axis=0)


def audio_target(vid, aud):
    x, z, y, half = vid >> 2, vid & 3, aud >> 1, aud & 1
    offset = (x - y) & 3
    to_y = (y - offset + 2 * (1 - (offset & 1))) & 3
    to_z = 2 * half + ((z + 1) & 1)
    to_half = (((z + 1) >> 1) + 1 + half) & 1
    return SIDE * y + to_z, 2 * to_y + to_half


def copy_all(pairs, sems):
    copies = [pltpu.make_async_copy(source, target, sems.at[index]) for index, (source, target) in enumerate(pairs)]
    for copy in copies:
        copy.start()
    for copy in copies:
        copy.wait()


def laid_out(kernel, name, given, shapes, count):
    return pl.pallas_call(
        kernel,
        in_specs=[pl.BlockSpec(memory_space=pl.ANY)] * len(given),
        out_specs=[pl.BlockSpec(memory_space=pltpu.VMEM)] * len(shapes),
        out_shape=[like(*shape) for shape in shapes],
        scratch_shapes=[pltpu.SemaphoreType.DMA((count,))],
        compiler_params=pltpu.CompilerParams(vmem_limit_bytes=VMEM),
        name=name,
    )(*given)


def prepare_keys_kernel(aq_ref, ak_ref, av_ref, vk_ref, vv_ref, audio, video_kv, sems):
    to_vid, to_aud = audio_target(lax.axis_index("vid"), lax.axis_index("aud"))
    rows, width = audio.shape[1:]
    taken = pl.ds(pl.multiple_of((to_vid & 1) * rows, rows), rows)
    columns = pl.ds(pl.multiple_of(to_aud * width, HEAD_DIM), width)
    pairs = [(ref.at[0, taken, columns], audio.at[index]) for index, ref in enumerate((aq_ref, ak_ref, av_ref))]
    pairs += [(ref.at[0], video_kv.at[index]) for index, ref in enumerate((vk_ref, vv_ref))]
    copy_all(pairs, sems)


def prepare_queries_kernel(vq_ref, dv_ref, da_ref, queries, sems):
    rows, audio_rows = vq_ref.shape[1], da_ref.shape[1]
    pairs = []
    for place in range(SIDE):
        pairs += [(vq_ref.at[0], queries.at[place, pl.ds(0, rows)])]
        pairs += [(dv_ref.at[0], queries.at[place, pl.ds(rows, rows)])]
        pairs += [(da_ref.at[0], queries.at[place, pl.ds(2 * rows, audio_rows)])]
    copy_all(pairs, sems)


def forward_kernel(video_rows, *refs):
    gathered_ref, k_refs, numbers_ref, gates_ref = refs[0], refs[1:9], refs[9], refs[10]
    e_refs, o_ref, stats_ref = refs[11:13], refs[13], refs[14]
    queries = queries_of(gathered_ref, video_rows)
    stats = []
    for part in (VIDEO, AUDIO):
        raw = nt(keys_of(k_refs, part, 0), queries)
        if part == AUDIO:
            rows = raw.shape[0] // SIDE
            position = lax.broadcasted_iota(jnp.int32, (rows, raw.shape[1]), 0)
            pieces = [raw[place * rows : (place + 1) * rows] for place in range(SIDE)]
            pieces = [jnp.where(position < numbers_ref[place], pieces[place], -1e30) for place in range(SIDE)]
            raw = jnp.concatenate(pieces, axis=0)
        peak = jnp.max(raw, axis=0, keepdims=True)
        expon = jnp.exp((raw - peak) * SCALE)
        total = jnp.sum(expon, axis=0, keepdims=True)
        expon = (expon * (1.0 / total)).astype(BF16)
        e_refs[part][0] = expon
        output = nn(keys_of(k_refs, part, 1).T, expon)
        o_ref[0, part] = output
        up = upstream(gathered_ref, gates_ref, video_rows, part)
        stats.append(peak * SCALE + jnp.log(total))
        stats.append(jnp.sum(up.astype(F32).T * output, axis=0, keepdims=True))
    stats_ref[0] = jnp.concatenate(stats, axis=0)


def merged_stats(refs, part):
    logs = [ref[0, 2 * part : 2 * part + 1] for ref in refs]
    peak = functools.reduce(jnp.maximum, logs)
    weights = [jnp.exp(local - peak) for local in logs]
    scale = 1.0 / sum(weights)
    delta = sum(weight * ref[0, 2 * part + 1 : 2 * part + 2] for weight, ref in zip(weights, refs)) * scale
    return weights[0] * scale, delta


def backward_keys(part, queries, up, stats_refs, k_refs, e_ref, k_outs, video_rows):
    factor, delta = merged_stats(stats_refs, part)
    probs = e_ref[0].astype(F32) * factor
    grad_values = nn(probs.astype(BF16), up).astype(BF16)
    grad_probs = nt(keys_of(k_refs, part, 1), up)
    grad_scores = (probs * (grad_probs - delta)).astype(BF16)
    grad_keys = (nn(grad_scores, queries) * SCALE).astype(BF16)
    rows, first = probs.shape[0] // SIDE, part * video_rows
    for place in range(SIDE):
        k_outs[place][0, first : first + rows] = grad_keys[place * rows : (place + 1) * rows]
        k_outs[place][1, first : first + rows] = grad_values[place * rows : (place + 1) * rows]
    return nn(keys_of(k_refs, part, 0).T, grad_scores), factor


def column_of(row):
    return jnp.broadcast_to(row, (HEAD_DIM, HEAD_DIM)).T[:, 0:1]


def backward_kernel(video_rows, *refs):
    gathered_ref, k_refs, stats_refs = refs[0], refs[1:9], refs[9:13]
    gates_ref, e_video, e_audio, o_ref = refs[13:17]
    k_outs, q_out = refs[17:21], refs[21]
    rows = gathered_ref.shape[1] // 2
    audio_rows = rows - video_rows
    video = SIDE * video_rows
    queries = queries_of(gathered_ref, video_rows)
    up = upstream(gathered_ref, gates_ref, video_rows, VIDEO)
    term_video, factor = backward_keys(VIDEO, queries, up, stats_refs, k_refs, e_video, k_outs, video_rows)
    on_video = o_ref[0, VIDEO] * factor
    up = upstream(gathered_ref, gates_ref, video_rows, AUDIO)
    term_audio, factor = backward_keys(AUDIO, queries, up, stats_refs, k_refs, e_audio, k_outs, video_rows)
    on_audio = o_ref[0, AUDIO] * factor
    grad_queries = term_video + term_audio
    cross_video, cross_audio = on_audio[:, :video], on_video[:, video:]
    merged = jnp.concatenate(
        [
            on_video[:, :video] + column_of(gates_ref[0:1, :]) * cross_video,
            on_audio[:, video:] + column_of(gates_ref[1:2, :]) * cross_audio,
        ],
        axis=1,
    )
    up_video, up_audio = upstreams_of(gathered_ref, video_rows)
    video_sum = jnp.sum(up_video.astype(F32).T * cross_video, axis=1, keepdims=True)
    audio_sum = jnp.sum(up_audio.astype(F32).T * cross_audio, axis=1, keepdims=True)
    sums = jnp.concatenate(
        [jnp.broadcast_to(video_sum, (HEAD_DIM, 4)), jnp.broadcast_to(audio_sum, (HEAD_DIM, HEAD_DIM - 4))], axis=1
    ).T[0:GATE_ROWS]
    high = sums.astype(BF16)
    low = (sums - high.astype(F32)).astype(BF16)
    even = lax.broadcasted_iota(jnp.int32, sums.shape, 0) % 2 == 0
    sums = jnp.where(even, high.astype(F32), low.astype(F32)).astype(BF16)
    merged = merged.T.astype(BF16)
    grad_queries = (grad_queries.T * SCALE).astype(BF16)
    for index, array in ((0, merged), (1, grad_queries)):
        first = index * rows
        q_out[:, first : first + video_rows] = array[:video].reshape(SIDE, video_rows, HEAD_DIM)
        q_out[:, first + video_rows : first + rows] = array[video:].reshape(SIDE, audio_rows, HEAD_DIM)
    q_out[:, 2 * rows :] = jnp.broadcast_to(sums, (SIDE, *sums.shape))


def chunk_spec(array):
    shape = array.shape[:-1]
    return pl.BlockSpec((*shape, HEAD_DIM), lambda h: (0,) * len(shape) + (h,))


def head_spec(array):
    shape = array.shape[1:]
    return pl.BlockSpec((1, *shape), lambda h: (h,) + (0,) * len(shape))


def like(*shape, kind=BF16):
    return jax.ShapeDtypeStruct(shape, kind)


def cost(keys, queries, heads, products):
    return pl.CostEstimate(
        flops=2 * products * heads * keys * queries * HEAD_DIM,
        bytes_accessed=4 * heads * keys * queries,
        transcendentals=heads * keys * queries,
    )


def attention_forward(queries, keys, numbers, gates, video_rows):
    heads = gates.shape[1] // HEAD_DIM
    total = SIDE * (queries.shape[1] // 2)
    video = SIDE * video_rows
    outs = [
        like(heads, video, total),
        like(heads, total - video, total),
        like(heads, 2, HEAD_DIM, total, kind=F32),
        like(heads, 4, total, kind=F32),
    ]
    chunks = [queries, *keys]
    return pl.pallas_call(
        functools.partial(forward_kernel, video_rows),
        grid=(heads,),
        in_specs=[chunk_spec(array) for array in chunks] + [pl.BlockSpec(memory_space=pltpu.SMEM), chunk_spec(gates)],
        out_specs=[head_spec(array) for array in outs],
        out_shape=outs,
        cost_estimate=cost(total, total, heads, 2),
        compiler_params=pltpu.CompilerParams(vmem_limit_bytes=VMEM),
        name="forward",
    )(*chunks, numbers, gates)


def attention_backward(queries, keys, stats, gates, by_head, video_rows):
    width = gates.shape[1]
    heads = width // HEAD_DIM
    rows = queries.shape[1] // 2
    outs = [like(2, rows, width)] * SIDE + [like(SIDE, 2 * rows + GATE_ROWS, width)]
    chunks = [queries, *keys]
    *key_parts, query_parts = pl.pallas_call(
        functools.partial(backward_kernel, video_rows),
        grid=(heads,),
        in_specs=[chunk_spec(array) for array in chunks]
        + [head_spec(array) for array in stats]
        + [chunk_spec(gates)]
        + [head_spec(array) for array in by_head],
        out_specs=[chunk_spec(array) for array in outs],
        out_shape=outs,
        cost_estimate=cost(SIDE * rows, SIDE * rows, heads, 4),
        compiler_params=pltpu.CompilerParams(vmem_limit_bytes=VMEM),
        name="backward",
    )(*chunks, *stats, gates, *by_head)
    return key_parts, query_parts


def total_of(refs, *index):
    return sum(ref[index].astype(F32) for ref in refs)


def finish_queries_kernel(parts_ref, video_out, audio_out, video_q, audio_q, gate_ref):
    video_rows, audio_rows = video_out.shape[1], audio_out.shape[1]
    rows = video_rows + audio_rows
    parts = [parts_ref.at[place] for place in range(SIDE)]
    for index, video, audio in ((0, video_out, audio_out), (1, video_q, audio_q)):
        first = index * rows
        video[0] = total_of(parts, slice(first, first + video_rows)).astype(BF16)
        audio[0] = total_of(parts, slice(first + video_rows, first + rows)).astype(BF16)
    gates = total_of(parts, slice(2 * rows, None))
    width = gates.shape[1]
    video_gate = jnp.broadcast_to(gates[0:1] + gates[1:2], (4, width))
    audio_gate = jnp.broadcast_to(gates[4:5] + gates[5:6], (4, width))
    gate_ref[...] = jnp.concatenate([video_gate, audio_gate], axis=0)


def finish_queries(parts, video_rows, audio_rows):
    width = parts.shape[2]
    video, audio = like(1, video_rows, width), like(1, audio_rows, width)
    return pl.pallas_call(
        finish_queries_kernel,
        out_shape=[video, audio, video, audio, like(8, width, kind=F32)],
        compiler_params=pltpu.CompilerParams(vmem_limit_bytes=8 * 2**20),
        name="finish_queries",
    )(parts)


def finish_keys_kernel(*refs):
    parts, (video_k, video_v, audio_k, audio_v) = refs[:SIDE], refs[SIDE:]
    rows = video_k.shape[1]
    for index, video, audio in ((0, video_k, audio_k), (1, video_v, audio_v)):
        video[0] = total_of(parts, index, slice(0, rows)).astype(BF16)
        audio[0] = total_of(parts, index, slice(rows, None)).astype(BF16)


def finish_keys(parts, video_rows, audio_rows):
    width = parts[0].shape[2]
    video, audio = like(1, video_rows, width), like(1, audio_rows, width)
    return pl.pallas_call(
        finish_keys_kernel,
        out_shape=[video, video, audio, audio],
        compiler_params=pltpu.CompilerParams(vmem_limit_bytes=8 * 2**20),
        name="finish_keys",
    )(*parts)


def own_audio(array):
    vid_size, aud_size = lax.axis_size("vid"), lax.axis_size("aud")
    pairs = []
    for vid in range(vid_size):
        for aud in range(aud_size):
            to_vid, to_aud = audio_target(vid, aud)
            pairs.append((vid * aud_size + aud, to_vid * aud_size + to_aud))
    return lax.ppermute(array, ("vid", "aud"), pairs)


def fenced(holds, function, *arrays):
    outs = jax.eval_shape(function, *arrays)
    return lax.cond(
        holds, function, lambda *_: jax.tree.map(lambda out: jnp.zeros(out.shape, out.dtype), outs), *arrays
    )


def shards(
    video_q, video_k, video_v, audio_q, audio_k, audio_v, video_gate, audio_gate, audio_len, d_video_out, d_audio_out
):
    vid = lax.axis_index("vid")
    video_rows, audio_rows = video_q.shape[1], d_audio_out.shape[1]
    holds = audio_len[0] > 0
    width = video_q.shape[2]
    send_audio, video_kv = laid_out(
        prepare_keys_kernel,
        "prepare_keys",
        (audio_q, audio_k, audio_v, video_k, video_v),
        [(3, audio_rows, width), (2, video_rows, width)],
        5,
    )

    def first_chunks(send_audio, video_kv, *given):
        shape = (SIDE, 2 * (video_rows + audio_rows), width)
        (queries,) = laid_out(prepare_queries_kernel, "prepare_queries", given, [shape], 3 * SIDE)
        return own_audio(send_audio), tuple(gathered(video_kv, along_z)[1:]), queries

    audio, video_keys, queries = fenced(
        holds, first_chunks, send_audio, video_kv, video_q, d_video_out, d_audio_out
    )
    audio = lax.optimization_barrier(audio)
    audio_q = jnp.broadcast_to(audio[0:1], (SIDE, *audio.shape[1:]))
    queries = lax.dynamic_update_slice(queries, audio_q, (0, 2 * video_rows + audio_rows, 0))
    audio_keys = gathered(audio[1:], along_z)
    queries = across_x(queries)
    keys = (video_kv, *video_keys, *audio_keys)
    gates = jnp.stack([video_gate, audio_gate])
    column, row = vid // SIDE, vid % SIDE
    limits = jnp.stack([audio_len[0] - (column * SIDE + (row - p) % SIDE) * audio_rows for p in range(SIDE)])
    *by_head, stats = attention_forward(queries, keys, limits, gates, video_rows)
    key_parts, query_parts = attention_backward(
        queries, keys, gathered(stats, along_x), gates, by_head, video_rows
    )

    def query_results(parts):
        parts = across_x(parts)
        *results, gate = finish_queries(parts, video_rows, audio_rows)
        for distance in (1, 2):
            gate = gate + beside_z(gate, distance)
        return (*results, gate)

    video_out, audio_out, grad_video_q, grad_audio_q, gate = fenced(holds, query_results, query_parts)
    key_parts = returned(key_parts, along_z)
    gate = gate + lax.ppermute(gate, "pair", [(0, 1), (1, 0)])
    grad_video_k, grad_video_v, grad_audio_k, grad_audio_v = finish_keys(key_parts, video_rows, audio_rows)
    return (
        video_out,
        audio_out,
        grad_video_q,
        grad_video_k,
        grad_video_v,
        grad_audio_q,
        grad_audio_k,
        grad_audio_v,
        gate[0],
        gate[7],
    )


def solution(mesh):
    split = P("pair", "vid", "aud")
    rows = P("pair", "aud", None)
    return jax.shard_map(
        shards,
        mesh=mesh,
        in_specs=(split, split, split, rows, rows, rows, P("aud"), P("aud"), P("pair"), split, split),
        out_specs=(split,) * 8 + (P("aud"), P("aud")),
        check_vma=False,
    )
```

```python
import functools

import jax
import jax.numpy as jnp
from jax import lax
from jax.experimental import pallas as pl
from jax.experimental.pallas import tpu as pltpu
from jax.sharding import PartitionSpec as P

HEAD_DIM = 128
SCALE = HEAD_DIM ** (-0.5)
SIDE = 4
F32 = jnp.float32
BF16 = jnp.bfloat16
VIDEO, AUDIO = 0, 1
GATE_ROWS = 16
VMEM = 60 * 2**20

ALONG_X = [[x * SIDE + z for x in range(SIDE)] for z in range(SIDE)]


def along_x(array, shift):
    pairs = [(x * SIDE + z, (x + shift) % SIDE * SIDE + z) for x in range(SIDE) for z in range(SIDE)]
    return lax.ppermute(array, "vid", pairs)


def along_z(array, shift):
    pairs = [(x * SIDE + z, x * SIDE + (z + shift) % SIDE) for x in range(SIDE) for z in range(SIDE)]
    return lax.ppermute(array, "vid", pairs)


def beside_z(array, distance):
    pairs = [(x * SIDE + z, x * SIDE + (z ^ distance)) for x in range(SIDE) for z in range(SIDE)]
    return lax.ppermute(array, "vid", pairs)


def all_along_x(array):
    return lax.all_gather(array, "vid", axis=0, axis_index_groups=ALONG_X)


def gathered(array, along):
    return [array] + [along(array, shift) for shift in range(1, SIDE)]


def returned(parts, along):
    return [parts[0]] + [along(parts[place], SIDE - place) for place in range(1, SIDE)]


def nt(a, b):
    return lax.dot_general(a, b, (((1,), (1,)), ((), ())), preferred_element_type=F32)


def nn(a, b):
    return lax.dot_general(a, b, (((1,), (0,)), ((), ())), preferred_element_type=F32)


def joined(refs, index):
    return jnp.concatenate([ref[index] for ref in refs], axis=0)


def gated(rows, gate_row):
    return (gate_row * rows.astype(F32)).astype(BF16)


def flat(block):
    return block.reshape(-1, block.shape[-1])


def queries_of(gathered_ref, audio_ref, video_rows):
    return jnp.concatenate([flat(gathered_ref[:, :video_rows]), flat(audio_ref[...])], axis=0)


def upstreams_of(gathered_ref, video_rows):
    return flat(gathered_ref[:, video_rows : 2 * video_rows]), flat(gathered_ref[:, 2 * video_rows :])


def upstream(gathered_ref, gates_ref, video_rows, part):
    video, audio = upstreams_of(gathered_ref, video_rows)
    if part == VIDEO:
        audio = gated(audio, gates_ref[1:2, :])
    else:
        video = gated(video, gates_ref[0:1, :])
    return jnp.concatenate([video, audio], axis=0)


def audio_target(vid, aud):
    x, z, y, half = vid >> 2, vid & 3, aud >> 1, aud & 1
    offset = (x - y) & 3
    to_y = (y - offset + 2 * (1 - (offset & 1))) & 3
    return SIDE * y + 2 * half + (z & 1), 2 * to_y + (z >> 1)


def prepare_kernel(aq_ref, ak_ref, av_ref, vq_ref, vk_ref, vv_ref, dv_ref, da_ref, audio, video_kv, queries, sems):
    to_vid, to_aud = audio_target(lax.axis_index("vid"), lax.axis_index("aud"))
    rows, width = vq_ref.shape[1:]
    audio_rows = da_ref.shape[1]
    taken = pl.ds(pl.multiple_of((to_vid & 1) * audio_rows, audio_rows), audio_rows)
    columns = pl.ds(pl.multiple_of(to_aud * width, HEAD_DIM), width)
    pairs = [(ref.at[0, taken, columns], audio.at[index]) for index, ref in enumerate((aq_ref, ak_ref, av_ref))]
    pairs += [(vk_ref.at[0], video_kv.at[0]), (vv_ref.at[0], video_kv.at[1])]
    pairs += [(vq_ref.at[0], queries.at[pl.ds(0, rows)]), (dv_ref.at[0], queries.at[pl.ds(rows, rows)])]
    pairs += [(da_ref.at[0], queries.at[pl.ds(2 * rows, audio_rows)])]
    copies = [pltpu.make_async_copy(source, target, sems.at[index]) for index, (source, target) in enumerate(pairs)]
    for copy in copies:
        copy.start()
    for copy in copies:
        copy.wait()


def prepare(audio_q, audio_k, audio_v, video_q, video_k, video_v, d_video, d_audio):
    _, video_rows, width = video_q.shape
    audio_rows = d_audio.shape[1]
    given = (audio_q, audio_k, audio_v, video_q, video_k, video_v, d_video, d_audio)
    shapes = [(3, audio_rows, width), (2, video_rows, width), (2 * video_rows + audio_rows, width)]
    return pl.pallas_call(
        prepare_kernel,
        in_specs=[pl.BlockSpec(memory_space=pl.ANY)] * len(given),
        out_specs=[pl.BlockSpec(memory_space=pltpu.VMEM)] * len(shapes),
        out_shape=[like(*shape) for shape in shapes],
        scratch_shapes=[pltpu.SemaphoreType.DMA((len(given),))],
        compiler_params=pltpu.CompilerParams(vmem_limit_bytes=VMEM),
        name="prepare",
    )(*given)


def forward_kernel(video_rows, *refs):
    gathered_ref, k_refs, audio_q, numbers_ref, gates_ref = refs[0], (refs[1:5], refs[5:9]), refs[9:13], refs[13], refs[14]
    e_refs, o_ref, stats_ref, ordered_ref = refs[15:17], refs[17], refs[18], refs[19]
    for place in range(SIDE):
        ordered_ref[lax.rem(numbers_ref[SIDE] + SIDE - place, SIDE)] = audio_q[place][...]
    queries = queries_of(gathered_ref, ordered_ref, video_rows)
    stats = []
    for part in (VIDEO, AUDIO):
        raw = nt(joined(k_refs[part], 0), queries)
        if part == AUDIO:
            rows = k_refs[part][0].shape[1]
            position = lax.broadcasted_iota(jnp.int32, (rows, raw.shape[1]), 0)
            pieces = [raw[place * rows : (place + 1) * rows] for place in range(SIDE)]
            pieces = [jnp.where(position < numbers_ref[place], pieces[place], -1e30) for place in range(SIDE)]
            raw = jnp.concatenate(pieces, axis=0)
        peak = jnp.max(raw, axis=0, keepdims=True)
        expon = jnp.exp((raw - peak) * SCALE)
        total = jnp.sum(expon, axis=0, keepdims=True)
        expon = (expon * (1.0 / total)).astype(BF16)
        e_refs[part][0] = expon
        output = nn(joined(k_refs[part], 1).T, expon)
        o_ref[0, part] = output
        up = upstream(gathered_ref, gates_ref, video_rows, part)
        stats.append(peak * SCALE + jnp.log(total))
        stats.append(jnp.sum(up.astype(F32).T * output, axis=0, keepdims=True))
    stats_ref[0] = jnp.concatenate(stats, axis=0)


def merged_stats(refs, part):
    logs = [ref[0, 2 * part : 2 * part + 1] for ref in refs]
    peak = functools.reduce(jnp.maximum, logs)
    weights = [jnp.exp(local - peak) for local in logs]
    scale = 1.0 / sum(weights)
    delta = sum(weight * ref[0, 2 * part + 1 : 2 * part + 2] for weight, ref in zip(weights, refs)) * scale
    return weights[0] * scale, delta


def backward_keys(part, queries, up, stats_refs, k_refs, e_ref, k_outs, first):
    factor, delta = merged_stats(stats_refs, part)
    probs = e_ref[0].astype(F32) * factor
    grad_values = nn(probs.astype(BF16), up).astype(BF16)
    grad_probs = nt(joined(k_refs, 1), up)
    grad_scores = (probs * (grad_probs - delta)).astype(BF16)
    grad_keys = (nn(grad_scores, queries) * SCALE).astype(BF16)
    rows = k_refs[0].shape[1]
    for place in range(SIDE):
        k_outs[place][0, first : first + rows] = grad_keys[place * rows : (place + 1) * rows]
        k_outs[place][1, first : first + rows] = grad_values[place * rows : (place + 1) * rows]
    return nn(joined(k_refs, 0).T, grad_scores), factor


def column_of(row):
    return jnp.broadcast_to(row, (HEAD_DIM, HEAD_DIM)).T[:, 0:1]


def backward_kernel(video_rows, *refs):
    gathered_ref, audio_q, k_video, k_audio, stats_refs = refs[0], refs[1], refs[2:6], refs[6:10], refs[10:14]
    gates_ref, e_video, e_audio, o_ref = refs[14:18]
    k_outs, q_out = refs[18:22], refs[22]
    audio_rows = audio_q.shape[1]
    rows = video_rows + audio_rows
    video = SIDE * video_rows
    queries = queries_of(gathered_ref, audio_q, video_rows)
    up = upstream(gathered_ref, gates_ref, video_rows, VIDEO)
    term_video, factor = backward_keys(VIDEO, queries, up, stats_refs, k_video, e_video, k_outs, 0)
    on_video = o_ref[0, VIDEO] * factor
    up = upstream(gathered_ref, gates_ref, video_rows, AUDIO)
    term_audio, factor = backward_keys(AUDIO, queries, up, stats_refs, k_audio, e_audio, k_outs, video_rows)
    on_audio = o_ref[0, AUDIO] * factor
    grad_queries = term_video + term_audio
    cross_video, cross_audio = on_audio[:, :video], on_video[:, video:]
    merged = jnp.concatenate(
        [
            on_video[:, :video] + column_of(gates_ref[0:1, :]) * cross_video,
            on_audio[:, video:] + column_of(gates_ref[1:2, :]) * cross_audio,
        ],
        axis=1,
    )
    up_video, up_audio = upstreams_of(gathered_ref, video_rows)
    video_sum = jnp.sum(up_video.astype(F32).T * cross_video, axis=1, keepdims=True)
    audio_sum = jnp.sum(up_audio.astype(F32).T * cross_audio, axis=1, keepdims=True)
    sums = jnp.concatenate(
        [jnp.broadcast_to(video_sum, (HEAD_DIM, 4)), jnp.broadcast_to(audio_sum, (HEAD_DIM, HEAD_DIM - 4))], axis=1
    ).T[0:GATE_ROWS]
    high = sums.astype(BF16)
    low = (sums - high.astype(F32)).astype(BF16)
    even = lax.broadcasted_iota(jnp.int32, sums.shape, 0) % 2 == 0
    sums = jnp.where(even, high.astype(F32), low.astype(F32)).astype(BF16)
    merged = merged.T.astype(BF16)
    grad_queries = (grad_queries.T * SCALE).astype(BF16)
    for index, array in ((0, merged), (1, grad_queries)):
        first = index * rows
        q_out[:, first : first + video_rows] = array[:video].reshape(SIDE, video_rows, HEAD_DIM)
        q_out[:, first + video_rows : first + rows] = array[video:].reshape(SIDE, audio_rows, HEAD_DIM)
    q_out[:, 2 * rows :] = jnp.broadcast_to(sums, (SIDE, *sums.shape))


def chunk_spec(array):
    shape = array.shape[:-1]
    return pl.BlockSpec((*shape, HEAD_DIM), lambda h: (0,) * len(shape) + (h,))


def head_spec(array):
    shape = array.shape[1:]
    return pl.BlockSpec((1, *shape), lambda h: (h,) + (0,) * len(shape))


def like(*shape, kind=BF16):
    return jax.ShapeDtypeStruct(shape, kind)


def cost(keys, queries, heads, products):
    return pl.CostEstimate(
        flops=2 * products * heads * keys * queries * HEAD_DIM,
        bytes_accessed=4 * heads * keys * queries,
        transcendentals=heads * keys * queries,
    )


def attention_forward(queries, audio_q, video_keys, audio_keys, numbers, gates, video_rows):
    heads = gates.shape[1] // HEAD_DIM
    audio_rows, width = audio_q[0].shape
    video, audio = SIDE * video_rows, SIDE * audio_rows
    total = video + audio
    outs = [
        like(heads, video, total),
        like(heads, audio, total),
        like(heads, 2, HEAD_DIM, total, kind=F32),
        like(heads, 4, total, kind=F32),
    ]
    ordered = like(SIDE, audio_rows, width)
    chunks = [queries, *video_keys, *audio_keys, *audio_q]
    return pl.pallas_call(
        functools.partial(forward_kernel, video_rows),
        grid=(heads,),
        in_specs=[chunk_spec(array) for array in chunks] + [pl.BlockSpec(memory_space=pltpu.SMEM), chunk_spec(gates)],
        out_specs=[head_spec(array) for array in outs] + [chunk_spec(ordered)],
        out_shape=[*outs, ordered],
        cost_estimate=cost(total, total, heads, 2),
        compiler_params=pltpu.CompilerParams(vmem_limit_bytes=VMEM),
        name="forward",
    )(*chunks, numbers, gates)


def attention_backward(queries, audio_q, video_keys, audio_keys, stats, gates, by_head, video_rows):
    width = gates.shape[1]
    heads = width // HEAD_DIM
    rows = video_rows + audio_q.shape[1]
    outs = [like(2, rows, width)] * SIDE + [like(SIDE, 2 * rows + GATE_ROWS, width)]
    chunks = [queries, audio_q, *video_keys, *audio_keys]
    *key_parts, query_parts = pl.pallas_call(
        functools.partial(backward_kernel, video_rows),
        grid=(heads,),
        in_specs=[chunk_spec(array) for array in chunks]
        + [head_spec(array) for array in stats]
        + [chunk_spec(gates)]
        + [head_spec(array) for array in by_head],
        out_specs=[chunk_spec(array) for array in outs],
        out_shape=outs,
        cost_estimate=cost(SIDE * rows, SIDE * rows, heads, 4),
        compiler_params=pltpu.CompilerParams(vmem_limit_bytes=VMEM),
        name="backward",
    )(*chunks, *stats, gates, *by_head)
    return key_parts, query_parts


def total_of(refs, *index):
    return sum(ref[index].astype(F32) for ref in refs)


def finish_queries_kernel(parts_ref, video_out, audio_out, video_q, audio_q, gate_ref):
    video_rows, audio_rows = video_out.shape[1], audio_out.shape[1]
    rows = video_rows + audio_rows
    parts = [parts_ref.at[place] for place in range(SIDE)]
    for index, video, audio in ((0, video_out, audio_out), (1, video_q, audio_q)):
        first = index * rows
        video[0] = total_of(parts, slice(first, first + video_rows)).astype(BF16)
        audio[0] = total_of(parts, slice(first + video_rows, first + rows)).astype(BF16)
    gates = total_of(parts, slice(2 * rows, None))
    width = gates.shape[1]
    video_gate = jnp.broadcast_to(gates[0:1] + gates[1:2], (4, width))
    audio_gate = jnp.broadcast_to(gates[4:5] + gates[5:6], (4, width))
    gate_ref[...] = jnp.concatenate([video_gate, audio_gate], axis=0)


def finish_queries(parts, video_rows, audio_rows):
    width = parts.shape[2]
    video, audio = like(1, video_rows, width), like(1, audio_rows, width)
    return pl.pallas_call(
        finish_queries_kernel,
        out_shape=[video, audio, video, audio, like(8, width, kind=F32)],
        compiler_params=pltpu.CompilerParams(vmem_limit_bytes=8 * 2**20),
        name="finish_queries",
    )(parts)


def finish_keys_kernel(*refs):
    parts, (video_k, video_v, audio_k, audio_v) = refs[:SIDE], refs[SIDE:]
    rows = video_k.shape[1]
    for index, video, audio in ((0, video_k, audio_k), (1, video_v, audio_v)):
        video[0] = total_of(parts, index, slice(0, rows)).astype(BF16)
        audio[0] = total_of(parts, index, slice(rows, None)).astype(BF16)


def finish_keys(parts, video_rows, audio_rows):
    width = parts[0].shape[2]
    video, audio = like(1, video_rows, width), like(1, audio_rows, width)
    return pl.pallas_call(
        finish_keys_kernel,
        out_shape=[video, video, audio, audio],
        compiler_params=pltpu.CompilerParams(vmem_limit_bytes=8 * 2**20),
        name="finish_keys",
    )(*parts)


def own_audio(array):
    vid_size, aud_size = lax.axis_size("vid"), lax.axis_size("aud")
    pairs = []
    for vid in range(vid_size):
        for aud in range(aud_size):
            to_vid, to_aud = audio_target(vid, aud)
            pairs.append((vid * aud_size + aud, to_vid * aud_size + to_aud))
    return lax.ppermute(array, ("vid", "aud"), pairs)


def fenced(holds, function, *arrays):
    outs = jax.eval_shape(function, *arrays)
    return lax.cond(
        holds, function, lambda *_: jax.tree.map(lambda out: jnp.zeros(out.shape, out.dtype), outs), *arrays
    )


def shards(
    video_q, video_k, video_v, audio_q, audio_k, audio_v, video_gate, audio_gate, audio_len, d_video_out, d_audio_out
):
    vid = lax.axis_index("vid")
    video_rows, audio_rows = video_q.shape[1], d_audio_out.shape[1]
    holds = audio_len[0] > 0
    send_audio, video_kv, queries = prepare(
        audio_q, audio_k, audio_v, video_q, video_k, video_v, d_video_out, d_audio_out
    )

    def first_chunks(send_audio, video_kv, queries):
        return own_audio(send_audio), tuple(gathered(video_kv, along_z)[1:]), all_along_x(queries)

    audio, video_keys, queries = fenced(holds, first_chunks, send_audio, video_kv, queries)
    video_keys = [video_kv, *video_keys]
    audio = lax.optimization_barrier(audio)
    audio_keys = gathered(audio[1:], along_z)
    audio_queries = gathered(audio[0], along_x)
    gates = jnp.stack([video_gate, audio_gate])
    column, row = vid // SIDE, vid % SIDE
    limits = [audio_len[0] - (column * SIDE + (row - p) % SIDE) * audio_rows for p in range(SIDE)]
    numbers = jnp.stack([*limits, column])
    *by_head, stats, audio_queries = attention_forward(
        queries, audio_queries, video_keys, audio_keys, numbers, gates, video_rows
    )
    key_parts, query_parts = attention_backward(
        queries, audio_queries, video_keys, audio_keys, gathered(stats, along_x), gates, by_head, video_rows
    )

    def query_results(parts):
        parts = lax.all_to_all(parts, "vid", 0, 0, axis_index_groups=ALONG_X, tiled=True)
        *results, gate = finish_queries(parts, video_rows, audio_rows)
        for distance in (1, 2):
            gate = gate + beside_z(gate, distance)
        return (*results, gate)

    video_out, audio_out, grad_video_q, grad_audio_q, gate = fenced(holds, query_results, query_parts)
    key_parts = returned(key_parts, along_z)
    gate = gate + lax.ppermute(gate, "pair", [(0, 1), (1, 0)])
    grad_video_k, grad_video_v, grad_audio_k, grad_audio_v = finish_keys(key_parts, video_rows, audio_rows)
    return (
        video_out,
        audio_out,
        grad_video_q,
        grad_video_k,
        grad_video_v,
        grad_audio_q,
        grad_audio_k,
        grad_audio_v,
        gate[0],
        gate[7],
    )


def solution(mesh):
    split = P("pair", "vid", "aud")
    rows = P("pair", "aud", None)
    return jax.shard_map(
        shards,
        mesh=mesh,
        in_specs=(split, split, split, rows, rows, rows, P("aud"), P("aud"), P("pair"), split, split),
        out_specs=(split,) * 8 + (P("aud"), P("aud")),
        check_vma=False,
    )
```

```python
import functools

import jax
import jax.numpy as jnp
from jax import lax
from jax.experimental import pallas as pl
from jax.experimental.pallas import tpu as pltpu
from jax.sharding import PartitionSpec as P

HEAD_DIM = 128
SCALE = HEAD_DIM ** (-0.5)
SIDE = 4
F32 = jnp.float32
BF16 = jnp.bfloat16
VIDEO, AUDIO = 0, 1
GATE_ROWS = 16
VMEM = 60 * 2**20
LOG2_E = 1.4426950408889634

ALONG_X = [[x * SIDE + z for x in range(SIDE)] for z in range(SIDE)]


def along_x(array, shift):
    pairs = [(x * SIDE + z, (x + shift) % SIDE * SIDE + z) for x in range(SIDE) for z in range(SIDE)]
    return lax.ppermute(array, "vid", pairs)


def along_z(array, shift):
    pairs = [(x * SIDE + z, x * SIDE + (z + shift) % SIDE) for x in range(SIDE) for z in range(SIDE)]
    return lax.ppermute(array, "vid", pairs)


def beside_z(array, distance):
    pairs = [(x * SIDE + z, x * SIDE + (z ^ distance)) for x in range(SIDE) for z in range(SIDE)]
    return lax.ppermute(array, "vid", pairs)


def all_along_x(array):
    return lax.all_gather(array, "vid", axis=0, axis_index_groups=ALONG_X)


def gathered(array, along):
    return [array] + [along(array, shift) for shift in range(1, SIDE)]


def returned(parts, along):
    return [parts[0]] + [along(parts[place], SIDE - place) for place in range(1, SIDE)]


def nt(a, b):
    return lax.dot_general(a, b, (((1,), (1,)), ((), ())), preferred_element_type=F32)


def nn(a, b):
    return lax.dot_general(a, b, (((1,), (0,)), ((), ())), preferred_element_type=F32)


def joined(refs, index):
    return jnp.concatenate([ref[index] for ref in refs], axis=0)


def gated(rows, gate_row):
    return (gate_row * rows.astype(F32)).astype(BF16)


def flat(block):
    return block.reshape(-1, block.shape[-1])


def queries_of(gathered_ref, audio_ref, video_rows):
    return jnp.concatenate([flat(gathered_ref[:, :video_rows]), flat(audio_ref[...])], axis=0)


def upstreams_of(gathered_ref, video_rows):
    return flat(gathered_ref[:, video_rows : 2 * video_rows]), flat(gathered_ref[:, 2 * video_rows :])


def upstream(gathered_ref, gates_ref, video_rows, part):
    video, audio = upstreams_of(gathered_ref, video_rows)
    if part == VIDEO:
        audio = gated(audio, gates_ref[1:2, :])
    else:
        video = gated(video, gates_ref[0:1, :])
    return jnp.concatenate([video, audio], axis=0)


def audio_target(vid, aud):
    x, z, y, half = vid >> 2, vid & 3, aud >> 1, aud & 1
    offset = (x - y) & 3
    to_y = (y - offset + 2 * (1 - (offset & 1))) & 3
    return SIDE * y + 2 * half + (z & 1), 2 * to_y + (z >> 1)


def prepare_kernel(aq_ref, ak_ref, av_ref, vq_ref, vk_ref, vv_ref, dv_ref, da_ref, audio, video_kv, queries, sems):
    to_vid, to_aud = audio_target(lax.axis_index("vid"), lax.axis_index("aud"))
    rows, width = vq_ref.shape[1:]
    audio_rows = da_ref.shape[1]
    taken = pl.ds(pl.multiple_of((to_vid & 1) * audio_rows, audio_rows), audio_rows)
    columns = pl.ds(pl.multiple_of(to_aud * width, HEAD_DIM), width)
    pairs = [(ref.at[0, taken, columns], audio.at[index]) for index, ref in enumerate((aq_ref, ak_ref, av_ref))]
    pairs += [(vk_ref.at[0], video_kv.at[0]), (vv_ref.at[0], video_kv.at[1])]
    pairs += [(vq_ref.at[0], queries.at[pl.ds(0, rows)]), (dv_ref.at[0], queries.at[pl.ds(rows, rows)])]
    pairs += [(da_ref.at[0], queries.at[pl.ds(2 * rows, audio_rows)])]
    copies = [pltpu.make_async_copy(source, target, sems.at[index]) for index, (source, target) in enumerate(pairs)]
    for copy in copies:
        copy.start()
    for copy in copies:
        copy.wait()


def prepare(audio_q, audio_k, audio_v, video_q, video_k, video_v, d_video, d_audio):
    _, video_rows, width = video_q.shape
    audio_rows = d_audio.shape[1]
    given = (audio_q, audio_k, audio_v, video_q, video_k, video_v, d_video, d_audio)
    shapes = [(3, audio_rows, width), (2, video_rows, width), (2 * video_rows + audio_rows, width)]
    return pl.pallas_call(
        prepare_kernel,
        in_specs=[pl.BlockSpec(memory_space=pl.ANY)] * len(given),
        out_specs=[pl.BlockSpec(memory_space=pltpu.VMEM)] * len(shapes),
        out_shape=[like(*shape) for shape in shapes],
        scratch_shapes=[pltpu.SemaphoreType.DMA((len(given),))],
        compiler_params=pltpu.CompilerParams(vmem_limit_bytes=VMEM),
        name="prepare",
    )(*given)


def scores(keys, queries, part, numbers_ref):
    raw = nt(keys, queries)
    if part == AUDIO:
        rows = raw.shape[0] // SIDE
        position = lax.broadcasted_iota(jnp.int32, (rows, raw.shape[1]), 0)
        pieces = [raw[place * rows : (place + 1) * rows] for place in range(SIDE)]
        pieces = [jnp.where(position < numbers_ref[place], pieces[place], -1e30) for place in range(SIDE)]
        raw = jnp.concatenate(pieces, axis=0)
    return raw


def attend(raw, values, up):
    peak = jnp.max(raw, axis=0, keepdims=True)
    expon = jnp.exp2((raw - peak) * (SCALE * LOG2_E))
    total = jnp.sum(expon, axis=0, keepdims=True)
    output = nn(values.T, expon.astype(BF16)) * (1.0 / total)
    delta = jnp.sum(up.T.astype(F32) * output, axis=0, keepdims=True)
    return output.astype(BF16), jnp.concatenate([peak * SCALE + jnp.log(total), delta], axis=0)


def forward_video_kernel(video_rows, *refs):
    gathered_ref, k_refs, o_ref, stats_ref = refs[0], refs[1:5], refs[5], refs[6]
    raw = scores(joined(k_refs, 0), flat(gathered_ref[:, :video_rows]), VIDEO, None)
    o_ref[0], stats_ref[0] = attend(raw, joined(k_refs, 1), upstreams_of(gathered_ref, video_rows)[0])


def forward_kernel(video_rows, *refs):
    gathered_ref, k_refs, audio_q, numbers_ref, gates_ref = refs[0], (refs[1:5], refs[5:9]), refs[9:13], refs[13], refs[14]
    o_video_ref, stats_video_ref, o_ref, stats_ref, ordered_ref = refs[15:20]
    for place in range(SIDE):
        ordered_ref[lax.rem(numbers_ref[SIDE] + SIDE - place, SIDE)] = audio_q[place][...]
    up_audio = gated(upstreams_of(gathered_ref, video_rows)[1], gates_ref[1:2, :])
    raw = scores(joined(k_refs[VIDEO], 0), flat(ordered_ref[...]), VIDEO, None)
    output, stats = attend(raw, joined(k_refs[VIDEO], 1), up_audio)
    o_ref[0, VIDEO] = jnp.concatenate([o_video_ref[0], output], axis=1)
    stats_video = jnp.concatenate([stats_video_ref[0], stats], axis=1)
    raw = scores(joined(k_refs[AUDIO], 0), queries_of(gathered_ref, ordered_ref, video_rows), AUDIO, numbers_ref)
    up = upstream(gathered_ref, gates_ref, video_rows, AUDIO)
    o_ref[0, AUDIO], stats = attend(raw, joined(k_refs[AUDIO], 1), up)
    stats_ref[0] = jnp.concatenate([stats_video, stats], axis=0)


def merged_stats(refs, part):
    logs = [ref[0, 2 * part : 2 * part + 1] for ref in refs]
    peak = functools.reduce(jnp.maximum, logs)
    weights = [jnp.exp(local - peak) for local in logs]
    total = sum(weights)
    scale = 1.0 / total
    delta = sum(weight * ref[0, 2 * part + 1 : 2 * part + 2] for weight, ref in zip(weights, refs)) * scale
    return peak + jnp.log(total), delta, weights[0] * scale


def backward_keys(part, queries, up, stats_refs, k_refs, numbers_ref, k_outs, first):
    log_total, delta, factor = merged_stats(stats_refs, part)
    raw = scores(joined(k_refs, 0), queries, part, numbers_ref)
    probs = jnp.exp2(raw * (SCALE * LOG2_E) - log_total * LOG2_E)
    grad_values = nn(probs.astype(BF16), up).astype(BF16)
    grad_probs = nt(joined(k_refs, 1), up)
    grad_scores = (probs * (grad_probs - delta)).astype(BF16)
    grad_keys = (nn(grad_scores, queries) * SCALE).astype(BF16)
    rows = k_refs[0].shape[1]
    for place in range(SIDE):
        k_outs[place][0, first : first + rows] = grad_keys[place * rows : (place + 1) * rows]
        k_outs[place][1, first : first + rows] = grad_values[place * rows : (place + 1) * rows]
    return nn(joined(k_refs, 0).T, grad_scores), factor


def column_of(row):
    return jnp.broadcast_to(row, (HEAD_DIM, HEAD_DIM)).T[:, 0:1]


def backward_kernel(video_rows, *refs):
    gathered_ref, audio_q, k_video, k_audio, stats_refs = refs[0], refs[1], refs[2:6], refs[6:10], refs[10:14]
    gates_ref, numbers_ref, o_ref = refs[14:17]
    k_outs, q_out = refs[17:21], refs[21]
    audio_rows = audio_q.shape[1]
    rows = video_rows + audio_rows
    video = SIDE * video_rows
    queries = queries_of(gathered_ref, audio_q, video_rows)
    up = upstream(gathered_ref, gates_ref, video_rows, VIDEO)
    term_video, factor = backward_keys(VIDEO, queries, up, stats_refs, k_video, numbers_ref, k_outs, 0)
    on_video = o_ref[0, VIDEO].astype(F32) * factor
    up = upstream(gathered_ref, gates_ref, video_rows, AUDIO)
    term_audio, factor = backward_keys(AUDIO, queries, up, stats_refs, k_audio, numbers_ref, k_outs, video_rows)
    on_audio = o_ref[0, AUDIO].astype(F32) * factor
    grad_queries = term_video + term_audio
    cross_video, cross_audio = on_audio[:, :video], on_video[:, video:]
    merged = jnp.concatenate(
        [
            on_video[:, :video] + column_of(gates_ref[0:1, :]) * cross_video,
            on_audio[:, video:] + column_of(gates_ref[1:2, :]) * cross_audio,
        ],
        axis=1,
    )
    up_video, up_audio = upstreams_of(gathered_ref, video_rows)
    video_sum = jnp.sum(up_video.T.astype(F32) * cross_video, axis=1, keepdims=True)
    audio_sum = jnp.sum(up_audio.T.astype(F32) * cross_audio, axis=1, keepdims=True)
    sums = jnp.concatenate(
        [jnp.broadcast_to(video_sum, (HEAD_DIM, 4)), jnp.broadcast_to(audio_sum, (HEAD_DIM, HEAD_DIM - 4))], axis=1
    ).T[0:GATE_ROWS]
    high = sums.astype(BF16)
    low = (sums - high.astype(F32)).astype(BF16)
    even = lax.broadcasted_iota(jnp.int32, sums.shape, 0) % 2 == 0
    sums = jnp.where(even, high.astype(F32), low.astype(F32)).astype(BF16)
    merged = merged.astype(BF16).T
    grad_queries = (grad_queries * SCALE).astype(BF16).T
    for index, array in ((0, merged), (1, grad_queries)):
        first = index * rows
        q_out[:, first : first + video_rows] = array[:video].reshape(SIDE, video_rows, HEAD_DIM)
        q_out[:, first + video_rows : first + rows] = array[video:].reshape(SIDE, audio_rows, HEAD_DIM)
    q_out[:, 2 * rows :] = jnp.broadcast_to(sums, (SIDE, *sums.shape))


def chunk_spec(array):
    shape = array.shape[:-1]
    return pl.BlockSpec((*shape, HEAD_DIM), lambda h: (0,) * len(shape) + (h,))


def head_spec(array):
    shape = array.shape[1:]
    return pl.BlockSpec((1, *shape), lambda h: (h,) + (0,) * len(shape))


def like(*shape, kind=BF16):
    return jax.ShapeDtypeStruct(shape, kind)


def cost(keys, queries, heads, products):
    return pl.CostEstimate(
        flops=2 * products * heads * keys * queries * HEAD_DIM,
        bytes_accessed=4 * heads * keys * queries,
        transcendentals=heads * keys * queries,
    )


def attention_forward_video(queries, video_keys, video_rows):
    heads = queries.shape[2] // HEAD_DIM
    video = SIDE * video_rows
    outs = [like(heads, HEAD_DIM, video), like(heads, 2, video, kind=F32)]
    chunks = [queries, *video_keys]
    return pl.pallas_call(
        functools.partial(forward_video_kernel, video_rows),
        grid=(heads,),
        in_specs=[chunk_spec(array) for array in chunks],
        out_specs=[head_spec(array) for array in outs],
        out_shape=outs,
        cost_estimate=cost(video, video, heads, 2),
        compiler_params=pltpu.CompilerParams(vmem_limit_bytes=VMEM),
        name="forward_video",
    )(*chunks)


def attention_forward(queries, audio_q, video_keys, audio_keys, numbers, gates, earlier, video_rows):
    heads = gates.shape[1] // HEAD_DIM
    audio_rows, width = audio_q[0].shape
    total = SIDE * (video_rows + audio_rows)
    outs = [like(heads, 2, HEAD_DIM, total), like(heads, 4, total, kind=F32)]
    ordered = like(SIDE, audio_rows, width)
    chunks = [queries, *video_keys, *audio_keys, *audio_q]
    return pl.pallas_call(
        functools.partial(forward_kernel, video_rows),
        grid=(heads,),
        in_specs=[chunk_spec(array) for array in chunks]
        + [pl.BlockSpec(memory_space=pltpu.SMEM), chunk_spec(gates)]
        + [head_spec(array) for array in earlier],
        out_specs=[head_spec(array) for array in outs] + [chunk_spec(ordered)],
        out_shape=[*outs, ordered],
        cost_estimate=cost(total, total, heads, 1),
        compiler_params=pltpu.CompilerParams(vmem_limit_bytes=VMEM),
        name="forward",
    )(*chunks, numbers, gates, *earlier)


def attention_backward(queries, audio_q, video_keys, audio_keys, stats, gates, numbers, outputs, video_rows):
    width = gates.shape[1]
    heads = width // HEAD_DIM
    rows = video_rows + audio_q.shape[1]
    outs = [like(2, rows, width)] * SIDE + [like(SIDE, 2 * rows + GATE_ROWS, width)]
    chunks = [queries, audio_q, *video_keys, *audio_keys]
    *key_parts, query_parts = pl.pallas_call(
        functools.partial(backward_kernel, video_rows),
        grid=(heads,),
        in_specs=[chunk_spec(array) for array in chunks]
        + [head_spec(array) for array in stats]
        + [chunk_spec(gates), pl.BlockSpec(memory_space=pltpu.SMEM), head_spec(outputs)],
        out_specs=[chunk_spec(array) for array in outs],
        out_shape=outs,
        cost_estimate=cost(SIDE * rows, SIDE * rows, heads, 4),
        compiler_params=pltpu.CompilerParams(vmem_limit_bytes=VMEM),
        name="backward",
    )(*chunks, *stats, gates, numbers, outputs)
    return key_parts, query_parts


def total_of(refs, *index):
    return sum(ref[index].astype(F32) for ref in refs)


def finish_queries_kernel(parts_ref, video_out, audio_out, video_q, audio_q, gate_ref):
    video_rows, audio_rows = video_out.shape[1], audio_out.shape[1]
    rows = video_rows + audio_rows
    parts = [parts_ref.at[place] for place in range(SIDE)]
    for index, video, audio in ((0, video_out, audio_out), (1, video_q, audio_q)):
        first = index * rows
        video[0] = total_of(parts, slice(first, first + video_rows)).astype(BF16)
        audio[0] = total_of(parts, slice(first + video_rows, first + rows)).astype(BF16)
    gates = total_of(parts, slice(2 * rows, None))
    width = gates.shape[1]
    video_gate = jnp.broadcast_to(gates[0:1] + gates[1:2], (4, width))
    audio_gate = jnp.broadcast_to(gates[4:5] + gates[5:6], (4, width))
    gate_ref[...] = jnp.concatenate([video_gate, audio_gate], axis=0)


def finish_queries(parts, video_rows, audio_rows):
    width = parts.shape[2]
    video, audio = like(1, video_rows, width), like(1, audio_rows, width)
    return pl.pallas_call(
        finish_queries_kernel,
        out_shape=[video, audio, video, audio, like(8, width, kind=F32)],
        compiler_params=pltpu.CompilerParams(vmem_limit_bytes=8 * 2**20),
        name="finish_queries",
    )(parts)


def finish_keys_kernel(*refs):
    parts, (video_k, video_v, audio_k, audio_v) = refs[:SIDE], refs[SIDE:]
    rows = video_k.shape[1]
    for index, video, audio in ((0, video_k, audio_k), (1, video_v, audio_v)):
        video[0] = total_of(parts, index, slice(0, rows)).astype(BF16)
        audio[0] = total_of(parts, index, slice(rows, None)).astype(BF16)


def finish_keys(parts, video_rows, audio_rows):
    width = parts[0].shape[2]
    video, audio = like(1, video_rows, width), like(1, audio_rows, width)
    return pl.pallas_call(
        finish_keys_kernel,
        out_shape=[video, video, audio, audio],
        compiler_params=pltpu.CompilerParams(vmem_limit_bytes=8 * 2**20),
        name="finish_keys",
    )(*parts)


def own_audio(array):
    vid_size, aud_size = lax.axis_size("vid"), lax.axis_size("aud")
    pairs = []
    for vid in range(vid_size):
        for aud in range(aud_size):
            to_vid, to_aud = audio_target(vid, aud)
            pairs.append((vid * aud_size + aud, to_vid * aud_size + to_aud))
    return lax.ppermute(array, ("vid", "aud"), pairs)


def fenced(holds, function, *arrays):
    outs = jax.eval_shape(function, *arrays)
    return lax.cond(
        holds, function, lambda *_: jax.tree.map(lambda out: jnp.zeros(out.shape, out.dtype), outs), *arrays
    )


def shards(
    video_q, video_k, video_v, audio_q, audio_k, audio_v, video_gate, audio_gate, audio_len, d_video_out, d_audio_out
):
    vid = lax.axis_index("vid")
    video_rows, audio_rows = video_q.shape[1], d_audio_out.shape[1]
    holds = audio_len[0] > 0
    send_audio, video_kv, queries = prepare(
        audio_q, audio_k, audio_v, video_q, video_k, video_v, d_video_out, d_audio_out
    )

    def first_chunks(send_audio, video_kv, queries):
        return own_audio(send_audio), tuple(gathered(video_kv, along_z)[1:]), all_along_x(queries)

    audio, video_keys, queries = fenced(holds, first_chunks, send_audio, video_kv, queries)
    video_keys = [video_kv, *video_keys]
    audio = lax.optimization_barrier(audio)
    audio_keys = gathered(audio[1:], along_z)
    audio_queries = gathered(audio[0], along_x)
    gates = jnp.stack([video_gate, audio_gate])
    column, row = vid // SIDE, vid % SIDE
    limits = [audio_len[0] - (column * SIDE + (row - p) % SIDE) * audio_rows for p in range(SIDE)]
    numbers = jnp.stack([*limits, column])
    earlier = attention_forward_video(queries, video_keys, video_rows)
    outputs, stats, audio_queries = attention_forward(
        queries, audio_queries, video_keys, audio_keys, numbers, gates, earlier, video_rows
    )
    key_parts, query_parts = attention_backward(
        queries, audio_queries, video_keys, audio_keys, gathered(stats, along_x), gates, numbers, outputs, video_rows
    )

    def query_results(parts):
        parts = lax.all_to_all(parts, "vid", 0, 0, axis_index_groups=ALONG_X, tiled=True)
        *results, gate = finish_queries(parts, video_rows, audio_rows)
        for distance in (1, 2):
            gate = gate + beside_z(gate, distance)
        return (*results, gate)

    video_out, audio_out, grad_video_q, grad_audio_q, gate = fenced(holds, query_results, query_parts)
    key_parts = returned(key_parts, along_z)
    gate = gate + lax.ppermute(gate, "pair", [(0, 1), (1, 0)])
    grad_video_k, grad_video_v, grad_audio_k, grad_audio_v = finish_keys(key_parts, video_rows, audio_rows)
    return (
        video_out,
        audio_out,
        grad_video_q,
        grad_video_k,
        grad_video_v,
        grad_audio_q,
        grad_audio_k,
        grad_audio_v,
        gate[0],
        gate[7],
    )


def solution(mesh):
    split = P("pair", "vid", "aud")
    rows = P("pair", "aud", None)
    return jax.shard_map(
        shards,
        mesh=mesh,
        in_specs=(split, split, split, rows, rows, rows, P("aud"), P("aud"), P("pair"), split, split),
        out_specs=(split,) * 8 + (P("aud"), P("aud")),
        check_vma=False,
    )
```

```python
import functools

import jax
import jax.numpy as jnp
from jax import lax
from jax.experimental import pallas as pl
from jax.experimental.pallas import tpu as pltpu
from jax.sharding import PartitionSpec as P

HEAD_DIM = 128
SCALE = HEAD_DIM ** (-0.5)
SIDE = 4
F32 = jnp.float32
BF16 = jnp.bfloat16
VIDEO, AUDIO = 0, 1
GATE_ROWS = 16
VMEM = 60 * 2**20
LOG2_E = 1.4426950408889634

ALONG_X = [[x * SIDE + z for x in range(SIDE)] for z in range(SIDE)]


def along_x(array, distance):
    pairs = [(x * SIDE + z, (x ^ distance) * SIDE + z) for x in range(SIDE) for z in range(SIDE)]
    return lax.ppermute(array, "vid", pairs)


def along_z(array, distance):
    pairs = [(x * SIDE + z, x * SIDE + (z ^ distance)) for x in range(SIDE) for z in range(SIDE)]
    return lax.ppermute(array, "vid", pairs)


def all_along_x(array):
    return lax.all_gather(array, "vid", axis=0, axis_index_groups=ALONG_X)


def gathered(array, along):
    return [array] + [along(array, distance) for distance in range(1, SIDE)]


def returned(parts, along):
    return [parts[0]] + [along(parts[place], place) for place in range(1, SIDE)]


def nt(a, b):
    return lax.dot_general(a, b, (((1,), (1,)), ((), ())), preferred_element_type=F32)


def nn(a, b):
    return lax.dot_general(a, b, (((1,), (0,)), ((), ())), preferred_element_type=F32)


def joined(refs, index):
    return jnp.concatenate([ref[index] for ref in refs], axis=0)


def gated(rows, gate_row):
    return (gate_row * rows.astype(F32)).astype(BF16)


def flat(block):
    return block.reshape(-1, block.shape[-1])


def queries_of(gathered_ref, audio_ref, video_rows):
    return jnp.concatenate([flat(gathered_ref[:, :video_rows]), flat(audio_ref[...])], axis=0)


def upstreams_of(gathered_ref, video_rows):
    return flat(gathered_ref[:, video_rows : 2 * video_rows]), flat(gathered_ref[:, 2 * video_rows :])


def upstream(gathered_ref, gates_ref, video_rows, part):
    video, audio = upstreams_of(gathered_ref, video_rows)
    if part == VIDEO:
        audio = gated(audio, gates_ref[1:2, :])
    else:
        video = gated(video, gates_ref[0:1, :])
    return jnp.concatenate([video, audio], axis=0)


def split_audio_kernel(audio_ref, queries_ref, keys_ref):
    queries_ref[...] = audio_ref[0]
    keys_ref[0] = audio_ref[1]
    keys_ref[1] = audio_ref[2]


def split_audio(audio):
    _, rows, width = audio.shape
    return pl.pallas_call(
        split_audio_kernel,
        out_shape=[like(rows, width), like(2, rows, width)],
        compiler_params=pltpu.CompilerParams(vmem_limit_bytes=8 * 2**20),
        name="split_audio",
    )(audio)


def audio_target(vid, aud):
    x, z, y, half = vid >> 2, vid & 3, aud >> 1, aud & 1
    offset = (x - y) & 3
    to_y = (y - offset + 2 * (1 - (offset & 1))) & 3
    return SIDE * y + 2 * half + (z & 1), 2 * to_y + (z >> 1)


def prepare_kernel(aq_ref, ak_ref, av_ref, vq_ref, vk_ref, vv_ref, dv_ref, da_ref, audio, video_kv, queries, sems):
    to_vid, to_aud = audio_target(lax.axis_index("vid"), lax.axis_index("aud"))
    rows, width = vq_ref.shape[1:]
    audio_rows = da_ref.shape[1]
    taken = pl.ds(pl.multiple_of((to_vid & 1) * audio_rows, audio_rows), audio_rows)
    columns = pl.ds(pl.multiple_of(to_aud * width, HEAD_DIM), width)
    pairs = [(ref.at[0, taken, columns], audio.at[index]) for index, ref in enumerate((aq_ref, ak_ref, av_ref))]
    pairs += [(vk_ref.at[0], video_kv.at[0]), (vv_ref.at[0], video_kv.at[1])]
    pairs += [(vq_ref.at[0], queries.at[pl.ds(0, rows)]), (dv_ref.at[0], queries.at[pl.ds(rows, rows)])]
    pairs += [(da_ref.at[0], queries.at[pl.ds(2 * rows, audio_rows)])]
    copies = [pltpu.make_async_copy(source, target, sems.at[index]) for index, (source, target) in enumerate(pairs)]
    for copy in copies:
        copy.start()
    for copy in copies:
        copy.wait()


def prepare(audio_q, audio_k, audio_v, video_q, video_k, video_v, d_video, d_audio):
    _, video_rows, width = video_q.shape
    audio_rows = d_audio.shape[1]
    given = (audio_q, audio_k, audio_v, video_q, video_k, video_v, d_video, d_audio)
    shapes = [(3, audio_rows, width), (2, video_rows, width), (2 * video_rows + audio_rows, width)]
    return pl.pallas_call(
        prepare_kernel,
        in_specs=[pl.BlockSpec(memory_space=pl.ANY)] * len(given),
        out_specs=[pl.BlockSpec(memory_space=pltpu.VMEM)] * len(shapes),
        out_shape=[like(*shape) for shape in shapes],
        scratch_shapes=[pltpu.SemaphoreType.DMA((len(given),))],
        compiler_params=pltpu.CompilerParams(vmem_limit_bytes=VMEM),
        name="prepare",
    )(*given)


def scores(keys, queries, part, numbers_ref):
    raw = nt(keys, queries)
    if part == AUDIO:
        rows = raw.shape[0] // SIDE
        position = lax.broadcasted_iota(jnp.int32, (rows, raw.shape[1]), 0)
        pieces = [raw[place * rows : (place + 1) * rows] for place in range(SIDE)]
        pieces = [jnp.where(position < numbers_ref[place], pieces[place], -1e30) for place in range(SIDE)]
        raw = jnp.concatenate(pieces, axis=0)
    return raw


def attend(raw, values, up):
    peak = jnp.max(raw, axis=0, keepdims=True)
    expon = jnp.exp2((raw - peak) * (SCALE * LOG2_E))
    total = jnp.sum(expon, axis=0, keepdims=True)
    output = nn(values.T, expon.astype(BF16)) * (1.0 / total)
    delta = jnp.sum(up.T.astype(F32) * output, axis=0, keepdims=True)
    return output.astype(BF16), jnp.concatenate([peak * SCALE + jnp.log(total), delta], axis=0)


def forward_video_kernel(video_rows, *refs):
    gathered_ref, k_refs, o_ref, stats_ref = refs[0], refs[1:5], refs[5], refs[6]
    raw = scores(joined(k_refs, 0), flat(gathered_ref[:, :video_rows]), VIDEO, None)
    o_ref[0], stats_ref[0] = attend(raw, joined(k_refs, 1), upstreams_of(gathered_ref, video_rows)[0])


def forward_kernel(video_rows, *refs):
    gathered_ref, k_refs, audio_q, numbers_ref, gates_ref = refs[0], (refs[1:5], refs[5:9]), refs[9:13], refs[13], refs[14]
    o_video_ref, stats_video_ref, o_ref, stats_ref, ordered_ref = refs[15:20]
    for place in range(SIDE):
        ordered_ref[numbers_ref[SIDE] ^ place] = audio_q[place][...]
    up_audio = gated(upstreams_of(gathered_ref, video_rows)[1], gates_ref[1:2, :])
    raw = scores(joined(k_refs[VIDEO], 0), flat(ordered_ref[...]), VIDEO, None)
    output, stats = attend(raw, joined(k_refs[VIDEO], 1), up_audio)
    o_ref[0, VIDEO] = jnp.concatenate([o_video_ref[0], output], axis=1)
    stats_video = jnp.concatenate([stats_video_ref[0], stats], axis=1)
    raw = scores(joined(k_refs[AUDIO], 0), queries_of(gathered_ref, ordered_ref, video_rows), AUDIO, numbers_ref)
    up = upstream(gathered_ref, gates_ref, video_rows, AUDIO)
    o_ref[0, AUDIO], stats = attend(raw, joined(k_refs[AUDIO], 1), up)
    stats_ref[0] = jnp.concatenate([stats_video, stats], axis=0)


def merged_stats(refs, part):
    logs = [ref[0, 2 * part : 2 * part + 1] for ref in refs]
    peak = functools.reduce(jnp.maximum, logs)
    weights = [jnp.exp(local - peak) for local in logs]
    total = sum(weights)
    scale = 1.0 / total
    delta = sum(weight * ref[0, 2 * part + 1 : 2 * part + 2] for weight, ref in zip(weights, refs)) * scale
    return peak + jnp.log(total), delta, weights[0] * scale


def backward_keys(part, queries, up, stats_refs, k_refs, numbers_ref, k_outs, first):
    log_total, delta, factor = merged_stats(stats_refs, part)
    raw = scores(joined(k_refs, 0), queries, part, numbers_ref)
    probs = jnp.exp2(raw * (SCALE * LOG2_E) - log_total * LOG2_E)
    grad_values = nn(probs.astype(BF16), up).astype(BF16)
    grad_probs = nt(joined(k_refs, 1), up)
    grad_scores = (probs * (grad_probs - delta)).astype(BF16)
    grad_keys = (nn(grad_scores, queries) * SCALE).astype(BF16)
    rows = k_refs[0].shape[1]
    for place in range(SIDE):
        k_outs[place][0, first : first + rows] = grad_keys[place * rows : (place + 1) * rows]
        k_outs[place][1, first : first + rows] = grad_values[place * rows : (place + 1) * rows]
    return nn(joined(k_refs, 0).T, grad_scores), factor


def column_of(row):
    return jnp.broadcast_to(row, (HEAD_DIM, HEAD_DIM)).T[:, 0:1]


def backward_kernel(video_rows, *refs):
    gathered_ref, audio_q, k_video, k_audio, stats_refs = refs[0], refs[1], refs[2:6], refs[6:10], refs[10:14]
    gates_ref, numbers_ref, o_ref = refs[14:17]
    k_outs, q_out = refs[17:21], refs[21]
    audio_rows = audio_q.shape[1]
    rows = video_rows + audio_rows
    video = SIDE * video_rows
    queries = queries_of(gathered_ref, audio_q, video_rows)
    up = upstream(gathered_ref, gates_ref, video_rows, VIDEO)
    term_video, factor = backward_keys(VIDEO, queries, up, stats_refs, k_video, numbers_ref, k_outs, 0)
    on_video = o_ref[0, VIDEO].astype(F32) * factor
    up = upstream(gathered_ref, gates_ref, video_rows, AUDIO)
    term_audio, factor = backward_keys(AUDIO, queries, up, stats_refs, k_audio, numbers_ref, k_outs, video_rows)
    on_audio = o_ref[0, AUDIO].astype(F32) * factor
    grad_queries = term_video + term_audio
    cross_video, cross_audio = on_audio[:, :video], on_video[:, video:]
    merged = jnp.concatenate(
        [
            on_video[:, :video] + column_of(gates_ref[0:1, :]) * cross_video,
            on_audio[:, video:] + column_of(gates_ref[1:2, :]) * cross_audio,
        ],
        axis=1,
    )
    up_video, up_audio = upstreams_of(gathered_ref, video_rows)
    video_sum = jnp.sum(up_video.T.astype(F32) * cross_video, axis=1, keepdims=True)
    audio_sum = jnp.sum(up_audio.T.astype(F32) * cross_audio, axis=1, keepdims=True)
    sums = jnp.concatenate(
        [jnp.broadcast_to(video_sum, (HEAD_DIM, 4)), jnp.broadcast_to(audio_sum, (HEAD_DIM, HEAD_DIM - 4))], axis=1
    ).T[0:GATE_ROWS]
    high = sums.astype(BF16)
    low = (sums - high.astype(F32)).astype(BF16)
    even = lax.broadcasted_iota(jnp.int32, sums.shape, 0) % 2 == 0
    sums = jnp.where(even, high.astype(F32), low.astype(F32)).astype(BF16)
    merged = merged.astype(BF16).T
    grad_queries = (grad_queries * SCALE).astype(BF16).T
    for index, array in ((0, merged), (1, grad_queries)):
        first = index * rows
        q_out[:, first : first + video_rows] = array[:video].reshape(SIDE, video_rows, HEAD_DIM)
        q_out[:, first + video_rows : first + rows] = array[video:].reshape(SIDE, audio_rows, HEAD_DIM)
    q_out[:, 2 * rows :] = jnp.broadcast_to(sums, (SIDE, *sums.shape))


def chunk_spec(array):
    shape = array.shape[:-1]
    return pl.BlockSpec((*shape, HEAD_DIM), lambda h: (0,) * len(shape) + (h,))


def head_spec(array):
    shape = array.shape[1:]
    return pl.BlockSpec((1, *shape), lambda h: (h,) + (0,) * len(shape))


def like(*shape, kind=BF16):
    return jax.ShapeDtypeStruct(shape, kind)


def cost(keys, queries, heads, products):
    return pl.CostEstimate(
        flops=2 * products * heads * keys * queries * HEAD_DIM,
        bytes_accessed=4 * heads * keys * queries,
        transcendentals=heads * keys * queries,
    )


def attention_forward_video(queries, video_keys, video_rows):
    heads = queries.shape[2] // HEAD_DIM
    video = SIDE * video_rows
    outs = [like(heads, HEAD_DIM, video), like(heads, 2, video, kind=F32)]
    chunks = [queries, *video_keys]
    return pl.pallas_call(
        functools.partial(forward_video_kernel, video_rows),
        grid=(heads,),
        in_specs=[chunk_spec(array) for array in chunks],
        out_specs=[head_spec(array) for array in outs],
        out_shape=outs,
        cost_estimate=cost(video, video, heads, 2),
        compiler_params=pltpu.CompilerParams(vmem_limit_bytes=VMEM),
        name="forward_video",
    )(*chunks)


def attention_forward(queries, audio_q, video_keys, audio_keys, numbers, gates, earlier, video_rows):
    heads = gates.shape[1] // HEAD_DIM
    audio_rows, width = audio_q[0].shape
    total = SIDE * (video_rows + audio_rows)
    outs = [like(heads, 2, HEAD_DIM, total), like(heads, 4, total, kind=F32)]
    ordered = like(SIDE, audio_rows, width)
    chunks = [queries, *video_keys, *audio_keys, *audio_q]
    return pl.pallas_call(
        functools.partial(forward_kernel, video_rows),
        grid=(heads,),
        in_specs=[chunk_spec(array) for array in chunks]
        + [pl.BlockSpec(memory_space=pltpu.SMEM), chunk_spec(gates)]
        + [head_spec(array) for array in earlier],
        out_specs=[head_spec(array) for array in outs] + [chunk_spec(ordered)],
        out_shape=[*outs, ordered],
        cost_estimate=cost(total, total, heads, 1),
        compiler_params=pltpu.CompilerParams(vmem_limit_bytes=VMEM),
        name="forward",
    )(*chunks, numbers, gates, *earlier)


def attention_backward(queries, audio_q, video_keys, audio_keys, stats, gates, numbers, outputs, video_rows):
    width = gates.shape[1]
    heads = width // HEAD_DIM
    rows = video_rows + audio_q.shape[1]
    outs = [like(2, rows, width)] * SIDE + [like(SIDE, 2 * rows + GATE_ROWS, width)]
    chunks = [queries, audio_q, *video_keys, *audio_keys]
    *key_parts, query_parts = pl.pallas_call(
        functools.partial(backward_kernel, video_rows),
        grid=(heads,),
        in_specs=[chunk_spec(array) for array in chunks]
        + [head_spec(array) for array in stats]
        + [chunk_spec(gates), pl.BlockSpec(memory_space=pltpu.SMEM), head_spec(outputs)],
        out_specs=[chunk_spec(array) for array in outs],
        out_shape=outs,
        cost_estimate=cost(SIDE * rows, SIDE * rows, heads, 4),
        compiler_params=pltpu.CompilerParams(vmem_limit_bytes=VMEM),
        name="backward",
    )(*chunks, *stats, gates, numbers, outputs)
    return key_parts, query_parts


def total_of(refs, *index):
    return sum(ref[index].astype(F32) for ref in refs)


def finish_queries_kernel(parts_ref, video_out, audio_out, video_q, audio_q, gate_ref):
    video_rows, audio_rows = video_out.shape[1], audio_out.shape[1]
    rows = video_rows + audio_rows
    parts = [parts_ref.at[place] for place in range(SIDE)]
    for index, video, audio in ((0, video_out, audio_out), (1, video_q, audio_q)):
        first = index * rows
        video[0] = total_of(parts, slice(first, first + video_rows)).astype(BF16)
        audio[0] = total_of(parts, slice(first + video_rows, first + rows)).astype(BF16)
    gates = total_of(parts, slice(2 * rows, None))
    width = gates.shape[1]
    video_gate = jnp.broadcast_to(gates[0:1] + gates[1:2], (4, width))
    audio_gate = jnp.broadcast_to(gates[4:5] + gates[5:6], (4, width))
    gate_ref[...] = jnp.concatenate([video_gate, audio_gate], axis=0)


def finish_queries(parts, video_rows, audio_rows):
    width = parts.shape[2]
    video, audio = like(1, video_rows, width), like(1, audio_rows, width)
    return pl.pallas_call(
        finish_queries_kernel,
        out_shape=[video, audio, video, audio, like(8, width, kind=F32)],
        compiler_params=pltpu.CompilerParams(vmem_limit_bytes=8 * 2**20),
        name="finish_queries",
    )(parts)


def finish_keys_kernel(*refs):
    parts, (video_k, video_v, audio_k, audio_v) = refs[:SIDE], refs[SIDE:]
    rows = video_k.shape[1]
    for index, video, audio in ((0, video_k, audio_k), (1, video_v, audio_v)):
        video[0] = total_of(parts, index, slice(0, rows)).astype(BF16)
        audio[0] = total_of(parts, index, slice(rows, None)).astype(BF16)


def finish_keys(parts, video_rows, audio_rows):
    width = parts[0].shape[2]
    video, audio = like(1, video_rows, width), like(1, audio_rows, width)
    return pl.pallas_call(
        finish_keys_kernel,
        out_shape=[video, video, audio, audio],
        compiler_params=pltpu.CompilerParams(vmem_limit_bytes=8 * 2**20),
        name="finish_keys",
    )(*parts)


def own_audio(array):
    vid_size, aud_size = lax.axis_size("vid"), lax.axis_size("aud")
    pairs = []
    for vid in range(vid_size):
        for aud in range(aud_size):
            to_vid, to_aud = audio_target(vid, aud)
            pairs.append((vid * aud_size + aud, to_vid * aud_size + to_aud))
    return lax.ppermute(array, ("vid", "aud"), pairs)


def fenced(holds, function, *arrays):
    outs = jax.eval_shape(function, *arrays)
    return lax.cond(
        holds, function, lambda *_: jax.tree.map(lambda out: jnp.zeros(out.shape, out.dtype), outs), *arrays
    )


def shards(
    video_q, video_k, video_v, audio_q, audio_k, audio_v, video_gate, audio_gate, audio_len, d_video_out, d_audio_out
):
    vid = lax.axis_index("vid")
    video_rows, audio_rows = video_q.shape[1], d_audio_out.shape[1]
    holds = audio_len[0] > 0
    send_audio, video_kv, queries = prepare(
        audio_q, audio_k, audio_v, video_q, video_k, video_v, d_video_out, d_audio_out
    )

    def first_chunks(send_audio, video_kv, queries):
        return own_audio(send_audio), tuple(gathered(video_kv, along_z)[1:]), all_along_x(queries)

    audio, video_keys, queries = fenced(holds, first_chunks, send_audio, video_kv, queries)
    video_keys = [video_kv, *video_keys]
    audio_queries, audio_keys = split_audio(audio)
    audio_keys = gathered(audio_keys, along_z)
    audio_queries = gathered(audio_queries, along_x)
    gates = jnp.stack([video_gate, audio_gate])
    column, row = vid // SIDE, vid % SIDE
    limits = [audio_len[0] - (column * SIDE + (row ^ p)) * audio_rows for p in range(SIDE)]
    numbers = jnp.stack([*limits, column])
    earlier = attention_forward_video(queries, video_keys, video_rows)
    outputs, stats, audio_queries = attention_forward(
        queries, audio_queries, video_keys, audio_keys, numbers, gates, earlier, video_rows
    )
    key_parts, query_parts = attention_backward(
        queries, audio_queries, video_keys, audio_keys, gathered(stats, along_x), gates, numbers, outputs, video_rows
    )

    def query_results(parts):
        parts = lax.all_to_all(parts, "vid", 0, 0, axis_index_groups=ALONG_X, tiled=True)
        *results, gate = finish_queries(parts, video_rows, audio_rows)
        for distance in (1, 2):
            gate = gate + along_z(gate, distance)
        return (*results, gate)

    video_out, audio_out, grad_video_q, grad_audio_q, gate = fenced(holds, query_results, query_parts)
    key_parts = returned(key_parts, along_z)
    other = lax.ppermute(gate, "pair", [(0, 1), (1, 0)])
    key_grads = finish_keys(key_parts, video_rows, audio_rows)
    other, (grad_video_k, grad_video_v, grad_audio_k, grad_audio_v) = lax.optimization_barrier((other, key_grads))
    gate = gate + other
    return (
        video_out,
        audio_out,
        grad_video_q,
        grad_video_k,
        grad_video_v,
        grad_audio_q,
        grad_audio_k,
        grad_audio_v,
        gate[0],
        gate[7],
    )


def solution(mesh):
    split = P("pair", "vid", "aud")
    rows = P("pair", "aud", None)
    return jax.shard_map(
        shards,
        mesh=mesh,
        in_specs=(split, split, split, rows, rows, rows, P("aud"), P("aud"), P("pair"), split, split),
        out_specs=(split,) * 8 + (P("aud"), P("aud")),
        check_vma=False,
    )
```

```python
import functools

import jax
import jax.numpy as jnp
from jax import lax
from jax.experimental import pallas as pl
from jax.experimental.pallas import tpu as pltpu
from jax.sharding import PartitionSpec as P

HEAD_DIM = 128
SCALE = HEAD_DIM ** (-0.5)
SIDE = 4
F32 = jnp.float32
BF16 = jnp.bfloat16
VIDEO, AUDIO = 0, 1
GATE_ROWS = 16
VMEM = 60 * 2**20
LOG2_E = 1.4426950408889634

ALONG_X = [[x * SIDE + z for x in range(SIDE)] for z in range(SIDE)]


def along_x(array, distance):
    pairs = [(x * SIDE + z, (x ^ distance) * SIDE + z) for x in range(SIDE) for z in range(SIDE)]
    return lax.ppermute(array, "vid", pairs)


def along_z(array, distance):
    pairs = [(x * SIDE + z, x * SIDE + (z ^ distance)) for x in range(SIDE) for z in range(SIDE)]
    return lax.ppermute(array, "vid", pairs)


def all_along_x(array):
    return lax.all_gather(array, "vid", axis=0, axis_index_groups=ALONG_X)


def gathered(array, along):
    return [array] + [along(array, distance) for distance in range(1, SIDE)]


def returned(parts, along):
    return [parts[0]] + [along(parts[place], place) for place in range(1, SIDE)]


def nt(a, b):
    return lax.dot_general(a, b, (((1,), (1,)), ((), ())), preferred_element_type=F32)


def nn(a, b):
    return lax.dot_general(a, b, (((1,), (0,)), ((), ())), preferred_element_type=F32)


def joined(refs, index):
    return jnp.concatenate([ref[index] for ref in refs], axis=0)


def gated(rows, gate_row):
    return (gate_row * rows.astype(F32)).astype(BF16)


def flat(block):
    return block.reshape(-1, block.shape[-1])


def queries_of(gathered_ref, audio_ref, video_rows):
    return jnp.concatenate([flat(gathered_ref[:, :video_rows]), flat(audio_ref[:, 0])], axis=0)


def upstreams_of(gathered_ref, audio_ref, video_rows):
    return flat(gathered_ref[:, video_rows:]), flat(audio_ref[:, 1])


def upstream(gathered_ref, audio_ref, gates_ref, video_rows, part):
    video, audio = upstreams_of(gathered_ref, audio_ref, video_rows)
    if part == VIDEO:
        audio = gated(audio, gates_ref[1:2, :])
    else:
        video = gated(video, gates_ref[0:1, :])
    return jnp.concatenate([video, audio], axis=0)


def split_audio_kernel(audio_ref, up_ref, queries_ref, keys_ref):
    queries_ref[0] = audio_ref[0]
    queries_ref[1] = up_ref[0]
    keys_ref[0] = audio_ref[1]
    keys_ref[1] = audio_ref[2]


def split_audio(audio, d_audio):
    _, rows, width = audio.shape
    return pl.pallas_call(
        split_audio_kernel,
        out_shape=[like(2, rows, width)] * 2,
        compiler_params=pltpu.CompilerParams(vmem_limit_bytes=8 * 2**20),
        name="split_audio",
    )(audio, d_audio)


def audio_target(vid, aud):
    x, z, y, half = vid >> 2, vid & 3, aud >> 1, aud & 1
    offset = (x - y) & 3
    to_y = (y - offset + 2 * (1 - (offset & 1))) & 3
    return SIDE * y + 2 * half + (z & 1), 2 * to_y + (z >> 1)


def prepare_kernel(aq_ref, ak_ref, av_ref, vq_ref, vk_ref, vv_ref, dv_ref, vg_ref, ag_ref, *outs):
    audio, video_kv, queries, gates, sems = outs
    to_vid, to_aud = audio_target(lax.axis_index("vid"), lax.axis_index("aud"))
    rows, width = vq_ref.shape[1:]
    audio_rows = audio.shape[1]
    taken = pl.ds(pl.multiple_of((to_vid & 1) * audio_rows, audio_rows), audio_rows)
    columns = pl.ds(pl.multiple_of(to_aud * width, HEAD_DIM), width)
    pairs = [(ref.at[0, taken, columns], audio.at[index]) for index, ref in enumerate((aq_ref, ak_ref, av_ref))]
    pairs += [(vk_ref.at[0], video_kv.at[0]), (vv_ref.at[0], video_kv.at[1])]
    pairs += [(vq_ref.at[0], queries.at[pl.ds(0, rows)]), (dv_ref.at[0], queries.at[pl.ds(rows, rows)])]
    copies = [pltpu.make_async_copy(source, target, sems.at[index]) for index, (source, target) in enumerate(pairs)]
    for copy in copies:
        copy.start()
    gates[...] = jnp.concatenate([vg_ref[...].reshape(1, width), ag_ref[...].reshape(1, width)], axis=0)
    for copy in copies:
        copy.wait()


def prepare(audio_rows, *given):
    _, video_rows, width = given[3].shape
    outs = [like(3, audio_rows, width), like(2, video_rows, width), like(2 * video_rows, width)]
    return pl.pallas_call(
        prepare_kernel,
        in_specs=[pl.BlockSpec(memory_space=pl.ANY)] * 7 + [pl.BlockSpec(memory_space=pltpu.VMEM)] * 2,
        out_specs=[pl.BlockSpec(memory_space=pltpu.VMEM)] * 4,
        out_shape=[*outs, like(2, width, kind=F32)],
        scratch_shapes=[pltpu.SemaphoreType.DMA((7,))],
        compiler_params=pltpu.CompilerParams(vmem_limit_bytes=VMEM),
        name="prepare",
    )(*given)


def scores(keys, queries, part, length_ref):
    raw = nt(keys, queries)
    if part == AUDIO:
        rows = raw.shape[0] // SIDE
        position = lax.broadcasted_iota(jnp.int32, (rows, raw.shape[1]), 0)
        pieces = [raw[place * rows : (place + 1) * rows] for place in range(SIDE)]
        vid = lax.axis_index("vid")
        for place in range(SIDE):
            chunk = (vid & ~(SIDE - 1)) + ((vid & (SIDE - 1)) ^ place)
            pieces[place] = jnp.where(position < length_ref[0] - chunk * rows, pieces[place], -1e30)
        raw = jnp.concatenate(pieces, axis=0)
    return raw


def attend(raw, values, up):
    peak = jnp.max(raw, axis=0, keepdims=True)
    expon = jnp.exp2((raw - peak) * (SCALE * LOG2_E))
    total = jnp.sum(expon, axis=0, keepdims=True)
    output = nn(values.T, expon.astype(BF16)) * (1.0 / total)
    delta = jnp.sum(up.T.astype(F32) * output, axis=0, keepdims=True)
    return output.astype(BF16), jnp.concatenate([peak * SCALE + jnp.log(total), delta], axis=0)


def forward_video_kernel(video_rows, *refs):
    gathered_ref, k_refs, o_ref, stats_ref = refs[0], refs[1:5], refs[5], refs[6]
    raw = scores(joined(k_refs, 0), flat(gathered_ref[:, :video_rows]), VIDEO, None)
    o_ref[0], stats_ref[0] = attend(raw, joined(k_refs, 1), flat(gathered_ref[:, video_rows:]))


def forward_kernel(video_rows, *refs):
    gathered_ref, k_refs, audio_q, length_ref, gates_ref = refs[0], (refs[1:5], refs[5:9]), refs[9:13], refs[13], refs[14]
    o_video_ref, stats_video_ref, o_ref, stats_ref, ordered_ref = refs[15:20]
    for place in range(SIDE):
        ordered_ref[(lax.axis_index("vid") >> 2) ^ place] = audio_q[place][...]
    up_audio = gated(flat(ordered_ref[:, 1]), gates_ref[1:2, :])
    raw = scores(joined(k_refs[VIDEO], 0), flat(ordered_ref[:, 0]), VIDEO, None)
    output, stats = attend(raw, joined(k_refs[VIDEO], 1), up_audio)
    o_ref[0, VIDEO] = jnp.concatenate([o_video_ref[0], output], axis=1)
    stats_video = jnp.concatenate([stats_video_ref[0], stats], axis=1)
    raw = scores(joined(k_refs[AUDIO], 0), queries_of(gathered_ref, ordered_ref, video_rows), AUDIO, length_ref)
    up = upstream(gathered_ref, ordered_ref, gates_ref, video_rows, AUDIO)
    o_ref[0, AUDIO], stats = attend(raw, joined(k_refs[AUDIO], 1), up)
    stats_ref[0] = jnp.concatenate([stats_video, stats], axis=0)


def merged_stats(refs, part):
    logs = [ref[0, 2 * part : 2 * part + 1] for ref in refs]
    peak = functools.reduce(jnp.maximum, logs)
    weights = [jnp.exp(local - peak) for local in logs]
    total = sum(weights)
    scale = 1.0 / total
    delta = sum(weight * ref[0, 2 * part + 1 : 2 * part + 2] for weight, ref in zip(weights, refs)) * scale
    return peak + jnp.log(total), delta, weights[0] * scale


def backward_keys(part, queries, up, stats_refs, k_refs, length_ref, k_outs, first):
    log_total, delta, factor = merged_stats(stats_refs, part)
    raw = scores(joined(k_refs, 0), queries, part, length_ref)
    probs = jnp.exp2(raw * (SCALE * LOG2_E) - log_total * LOG2_E)
    grad_values = nn(probs.astype(BF16), up).astype(BF16)
    grad_probs = nt(joined(k_refs, 1), up)
    grad_scores = (probs * (grad_probs - delta)).astype(BF16)
    grad_keys = (nn(grad_scores, queries) * SCALE).astype(BF16)
    rows = k_refs[0].shape[1]
    for place in range(SIDE):
        k_outs[place][0, first : first + rows] = grad_keys[place * rows : (place + 1) * rows]
        k_outs[place][1, first : first + rows] = grad_values[place * rows : (place + 1) * rows]
    return nn(joined(k_refs, 0).T, grad_scores), factor


def column_of(row):
    return jnp.broadcast_to(row, (HEAD_DIM, HEAD_DIM)).T[:, 0:1]


def backward_kernel(video_rows, *refs):
    gathered_ref, audio_q, k_video, k_audio, stats_refs = refs[0], refs[1], refs[2:6], refs[6:10], refs[10:14]
    gates_ref, length_ref, o_ref = refs[14:17]
    k_outs, q_out = refs[17:21], refs[21]
    audio_rows = audio_q.shape[2]
    rows = video_rows + audio_rows
    video = SIDE * video_rows
    queries = queries_of(gathered_ref, audio_q, video_rows)
    up = upstream(gathered_ref, audio_q, gates_ref, video_rows, VIDEO)
    term_video, factor = backward_keys(VIDEO, queries, up, stats_refs, k_video, length_ref, k_outs, 0)
    on_video = o_ref[0, VIDEO].astype(F32) * factor
    up = upstream(gathered_ref, audio_q, gates_ref, video_rows, AUDIO)
    term_audio, factor = backward_keys(AUDIO, queries, up, stats_refs, k_audio, length_ref, k_outs, video_rows)
    on_audio = o_ref[0, AUDIO].astype(F32) * factor
    grad_queries = term_video + term_audio
    cross_video, cross_audio = on_audio[:, :video], on_video[:, video:]
    merged = jnp.concatenate(
        [
            on_video[:, :video] + column_of(gates_ref[0:1, :]) * cross_video,
            on_audio[:, video:] + column_of(gates_ref[1:2, :]) * cross_audio,
        ],
        axis=1,
    )
    up_video, up_audio = upstreams_of(gathered_ref, audio_q, video_rows)
    video_sum = jnp.sum(up_video.T.astype(F32) * cross_video, axis=1, keepdims=True)
    audio_sum = jnp.sum(up_audio.T.astype(F32) * cross_audio, axis=1, keepdims=True)
    sums = jnp.concatenate(
        [jnp.broadcast_to(video_sum, (HEAD_DIM, 4)), jnp.broadcast_to(audio_sum, (HEAD_DIM, HEAD_DIM - 4))], axis=1
    ).T[0:GATE_ROWS]
    high = sums.astype(BF16)
    low = (sums - high.astype(F32)).astype(BF16)
    even = lax.broadcasted_iota(jnp.int32, sums.shape, 0) % 2 == 0
    sums = jnp.where(even, high.astype(F32), low.astype(F32)).astype(BF16)
    merged = merged.astype(BF16).T
    grad_queries = (grad_queries * SCALE).astype(BF16).T
    for index, array in ((0, merged), (1, grad_queries)):
        first = index * rows
        q_out[:, first : first + video_rows] = array[:video].reshape(SIDE, video_rows, HEAD_DIM)
        q_out[:, first + video_rows : first + rows] = array[video:].reshape(SIDE, audio_rows, HEAD_DIM)
    q_out[:, 2 * rows :] = jnp.broadcast_to(sums, (SIDE, *sums.shape))


def chunk_spec(array):
    shape = array.shape[:-1]
    return pl.BlockSpec((*shape, HEAD_DIM), lambda h: (0,) * len(shape) + (h,))


def head_spec(array):
    shape = array.shape[1:]
    return pl.BlockSpec((1, *shape), lambda h: (h,) + (0,) * len(shape))


def like(*shape, kind=BF16):
    return jax.ShapeDtypeStruct(shape, kind)


def cost(keys, queries, heads, products):
    return pl.CostEstimate(
        flops=2 * products * heads * keys * queries * HEAD_DIM,
        bytes_accessed=4 * heads * keys * queries,
        transcendentals=heads * keys * queries,
    )


def attention_forward_video(queries, video_keys, video_rows):
    heads = queries.shape[2] // HEAD_DIM
    video = SIDE * video_rows
    outs = [like(heads, HEAD_DIM, video), like(heads, 2, video, kind=F32)]
    chunks = [queries, *video_keys]
    return pl.pallas_call(
        functools.partial(forward_video_kernel, video_rows),
        grid=(heads,),
        in_specs=[chunk_spec(array) for array in chunks],
        out_specs=[head_spec(array) for array in outs],
        out_shape=outs,
        cost_estimate=cost(video, video, heads, 2),
        compiler_params=pltpu.CompilerParams(vmem_limit_bytes=VMEM),
        name="forward_video",
    )(*chunks)


def attention_forward(queries, audio_q, video_keys, audio_keys, audio_len, gates, earlier, video_rows):
    heads = gates.shape[1] // HEAD_DIM
    _, audio_rows, width = audio_q[0].shape
    total = SIDE * (video_rows + audio_rows)
    outs = [like(heads, 2, HEAD_DIM, total), like(heads, 4, total, kind=F32)]
    ordered = like(SIDE, 2, audio_rows, width)
    chunks = [queries, *video_keys, *audio_keys, *audio_q]
    return pl.pallas_call(
        functools.partial(forward_kernel, video_rows),
        grid=(heads,),
        in_specs=[chunk_spec(array) for array in chunks]
        + [pl.BlockSpec(memory_space=pltpu.SMEM), chunk_spec(gates)]
        + [head_spec(array) for array in earlier],
        out_specs=[head_spec(array) for array in outs] + [chunk_spec(ordered)],
        out_shape=[*outs, ordered],
        cost_estimate=cost(total, total, heads, 1),
        compiler_params=pltpu.CompilerParams(vmem_limit_bytes=VMEM),
        name="forward",
    )(*chunks, audio_len, gates, *earlier)


def attention_backward(queries, audio_q, video_keys, audio_keys, stats, gates, audio_len, outputs, video_rows):
    width = gates.shape[1]
    heads = width // HEAD_DIM
    rows = video_rows + audio_q.shape[2]
    outs = [like(2, rows, width)] * SIDE + [like(SIDE, 2 * rows + GATE_ROWS, width)]
    chunks = [queries, audio_q, *video_keys, *audio_keys]
    *key_parts, query_parts = pl.pallas_call(
        functools.partial(backward_kernel, video_rows),
        grid=(heads,),
        in_specs=[chunk_spec(array) for array in chunks]
        + [head_spec(array) for array in stats]
        + [chunk_spec(gates), pl.BlockSpec(memory_space=pltpu.SMEM), head_spec(outputs)],
        out_specs=[chunk_spec(array) for array in outs],
        out_shape=outs,
        cost_estimate=cost(SIDE * rows, SIDE * rows, heads, 4),
        compiler_params=pltpu.CompilerParams(vmem_limit_bytes=VMEM),
        name="backward",
    )(*chunks, *stats, gates, audio_len, outputs)
    return key_parts, query_parts


def total_of(refs, *index):
    return sum(ref[index].astype(F32) for ref in refs)


def finish_queries_kernel(parts_ref, video_out, audio_out, video_q, audio_q, gate_ref):
    video_rows, audio_rows = video_out.shape[1], audio_out.shape[1]
    rows = video_rows + audio_rows
    parts = [parts_ref.at[place] for place in range(SIDE)]
    for index, video, audio in ((0, video_out, audio_out), (1, video_q, audio_q)):
        first = index * rows
        video[0] = total_of(parts, slice(first, first + video_rows)).astype(BF16)
        audio[0] = total_of(parts, slice(first + video_rows, first + rows)).astype(BF16)
    gates = total_of(parts, slice(2 * rows, None))
    width = gates.shape[1]
    video_gate = jnp.broadcast_to(gates[0:1] + gates[1:2], (4, width))
    audio_gate = jnp.broadcast_to(gates[4:5] + gates[5:6], (4, width))
    gate_ref[...] = jnp.concatenate([video_gate, audio_gate], axis=0)


def finish_queries(parts, video_rows, audio_rows):
    width = parts.shape[2]
    video, audio = like(1, video_rows, width), like(1, audio_rows, width)
    return pl.pallas_call(
        finish_queries_kernel,
        out_shape=[video, audio, video, audio, like(8, width, kind=F32)],
        compiler_params=pltpu.CompilerParams(vmem_limit_bytes=8 * 2**20),
        name="finish_queries",
    )(parts)


def finish_keys_kernel(*refs):
    parts, (video_k, video_v, audio_k, audio_v) = refs[:SIDE], refs[SIDE:]
    rows = video_k.shape[1]
    for index, video, audio in ((0, video_k, audio_k), (1, video_v, audio_v)):
        video[0] = total_of(parts, index, slice(0, rows)).astype(BF16)
        audio[0] = total_of(parts, index, slice(rows, None)).astype(BF16)


def finish_keys(parts, video_rows, audio_rows):
    width = parts[0].shape[2]
    video, audio = like(1, video_rows, width), like(1, audio_rows, width)
    return pl.pallas_call(
        finish_keys_kernel,
        out_shape=[video, video, audio, audio],
        compiler_params=pltpu.CompilerParams(vmem_limit_bytes=8 * 2**20),
        name="finish_keys",
    )(*parts)


def own_audio(array):
    vid_size, aud_size = lax.axis_size("vid"), lax.axis_size("aud")
    pairs = []
    for vid in range(vid_size):
        for aud in range(aud_size):
            to_vid, to_aud = audio_target(vid, aud)
            pairs.append((vid * aud_size + aud, to_vid * aud_size + to_aud))
    return lax.ppermute(array, ("vid", "aud"), pairs)


def fenced(holds, function, *arrays):
    outs = jax.eval_shape(function, *arrays)
    return lax.cond(
        holds, function, lambda *_: jax.tree.map(lambda out: jnp.zeros(out.shape, out.dtype), outs), *arrays
    )


def shards(
    video_q, video_k, video_v, audio_q, audio_k, audio_v, video_gate, audio_gate, audio_len, d_video_out, d_audio_out
):
    vid = lax.axis_index("vid")
    video_rows, audio_rows = video_q.shape[1], d_audio_out.shape[1]
    holds = audio_len[0] > 0
    send_audio, video_kv, queries, gates = prepare(
        audio_rows, audio_q, audio_k, audio_v, video_q, video_k, video_v, d_video_out, video_gate, audio_gate
    )

    def first_chunks(send_audio, video_kv, queries):
        return own_audio(send_audio), tuple(gathered(video_kv, along_z)[1:]), all_along_x(queries)

    audio, video_keys, queries = fenced(holds, first_chunks, send_audio, video_kv, queries)
    video_keys = [video_kv, *video_keys]
    audio_queries, audio_keys = split_audio(audio, d_audio_out)
    audio_keys = gathered(audio_keys, along_z)
    audio_queries = gathered(audio_queries, along_x)
    earlier = attention_forward_video(queries, video_keys, video_rows)
    outputs, stats, audio_queries = attention_forward(
        queries, audio_queries, video_keys, audio_keys, audio_len, gates, earlier, video_rows
    )
    key_parts, query_parts = attention_backward(
        queries, audio_queries, video_keys, audio_keys, gathered(stats, along_x), gates, audio_len, outputs, video_rows
    )

    def query_results(parts):
        parts = lax.all_to_all(parts, "vid", 0, 0, axis_index_groups=ALONG_X, tiled=True)
        *results, gate = finish_queries(parts, video_rows, audio_rows)
        for distance in (1, 2):
            gate = gate + along_z(gate, distance)
        return (*results, gate)

    video_out, audio_out, grad_video_q, grad_audio_q, gate = fenced(holds, query_results, query_parts)
    key_parts = returned(key_parts, along_z)
    other = lax.ppermute(gate, "pair", [(0, 1), (1, 0)])
    key_grads = finish_keys(key_parts, video_rows, audio_rows)
    other, (grad_video_k, grad_video_v, grad_audio_k, grad_audio_v) = lax.optimization_barrier((other, key_grads))
    gate = gate + other
    return (
        video_out,
        audio_out,
        grad_video_q,
        grad_video_k,
        grad_video_v,
        grad_audio_q,
        grad_audio_k,
        grad_audio_v,
        gate[0],
        gate[7],
    )


def solution(mesh):
    split = P("pair", "vid", "aud")
    rows = P("pair", "aud", None)
    return jax.shard_map(
        shards,
        mesh=mesh,
        in_specs=(split, split, split, rows, rows, rows, P("aud"), P("aud"), P("pair"), split, split),
        out_specs=(split,) * 8 + (P("aud"), P("aud")),
        check_vma=False,
    )
```

```python
import functools

import jax
import jax.numpy as jnp
from jax import lax
from jax.experimental import pallas as pl
from jax.experimental.pallas import tpu as pltpu
from jax.sharding import PartitionSpec as P

HEAD_DIM = 128
SCALE = HEAD_DIM ** (-0.5)
SIDE = 4
F32 = jnp.float32
BF16 = jnp.bfloat16
VIDEO, AUDIO = 0, 1
GATE_ROWS = 16
VMEM = 60 * 2**20
LOG2_E = 1.4426950408889634

ALONG_X = [[x * SIDE + z for x in range(SIDE)] for z in range(SIDE)]


def along_x(array, distance):
    pairs = [(x * SIDE + z, (x ^ distance) * SIDE + z) for x in range(SIDE) for z in range(SIDE)]
    return lax.ppermute(array, "vid", pairs)


def along_z(array, distance):
    pairs = [(x * SIDE + z, x * SIDE + (z ^ distance)) for x in range(SIDE) for z in range(SIDE)]
    return lax.ppermute(array, "vid", pairs)


def all_along_x(array):
    return lax.all_gather(array, "vid", axis=0, axis_index_groups=ALONG_X)


def gathered(array, along):
    return [array] + [along(array, distance) for distance in range(1, SIDE)]


def returned(parts, along):
    return [parts[0]] + [along(parts[place], place) for place in range(1, SIDE)]


def nt(a, b):
    return lax.dot_general(a, b, (((1,), (1,)), ((), ())), preferred_element_type=F32)


def nn(a, b):
    return lax.dot_general(a, b, (((1,), (0,)), ((), ())), preferred_element_type=F32)


def joined(refs, index):
    return jnp.concatenate([ref[index] for ref in refs], axis=0)


def gated(rows, gate_row):
    return (gate_row * rows.astype(F32)).astype(BF16)


def flat(block):
    return block.reshape(-1, block.shape[-1])


def queries_of(gathered_ref, audio_ref, video_rows):
    return jnp.concatenate([flat(gathered_ref[:, :video_rows]), flat(audio_ref[:, 0])], axis=0)


def upstreams_of(gathered_ref, audio_ref, video_rows):
    return flat(gathered_ref[:, video_rows:]), flat(audio_ref[:, 1])


def head_row(ref):
    first = pl.multiple_of(pl.program_id(0) * HEAD_DIM, HEAD_DIM)
    return ref[pl.ds(first, HEAD_DIM)].reshape(1, HEAD_DIM)


def upstream(gathered_ref, audio_ref, gate_rows, video_rows, part):
    video, audio = upstreams_of(gathered_ref, audio_ref, video_rows)
    if part == VIDEO:
        audio = gated(audio, gate_rows[AUDIO])
    else:
        video = gated(video, gate_rows[VIDEO])
    return jnp.concatenate([video, audio], axis=0)


def split_audio_kernel(audio_ref, up_ref, queries_ref, keys_ref):
    queries_ref[0] = audio_ref[0]
    queries_ref[1] = up_ref[0]
    keys_ref[0] = audio_ref[1]
    keys_ref[1] = audio_ref[2]


def split_audio(audio, d_audio):
    _, rows, width = audio.shape
    return pl.pallas_call(
        split_audio_kernel,
        out_shape=[like(2, rows, width)] * 2,
        compiler_params=pltpu.CompilerParams(vmem_limit_bytes=8 * 2**20),
        name="split_audio",
    )(audio, d_audio)


def audio_target(vid, aud):
    x, z, y, half = vid >> 2, vid & 3, aud >> 1, aud & 1
    offset = (x - y) & 3
    to_y = (y - offset + 2 * (1 - (offset & 1))) & 3
    return SIDE * y + 2 * half + (z & 1), 2 * to_y + (z >> 1)


def prepare_kernel(aq_ref, ak_ref, av_ref, vq_ref, vk_ref, vv_ref, dv_ref, audio, video_kv, queries, sems):
    to_vid, to_aud = audio_target(lax.axis_index("vid"), lax.axis_index("aud"))
    rows, width = vq_ref.shape[1:]
    audio_rows = audio.shape[1]
    taken = pl.ds(pl.multiple_of((to_vid & 1) * audio_rows, audio_rows), audio_rows)
    columns = pl.ds(pl.multiple_of(to_aud * width, HEAD_DIM), width)
    pairs = [(ref.at[0, taken, columns], audio.at[index]) for index, ref in enumerate((aq_ref, ak_ref, av_ref))]
    pairs += [(vk_ref.at[0], video_kv.at[0]), (vv_ref.at[0], video_kv.at[1])]
    pairs += [(vq_ref.at[0], queries.at[pl.ds(0, rows)]), (dv_ref.at[0], queries.at[pl.ds(rows, rows)])]
    copies = [pltpu.make_async_copy(source, target, sems.at[index]) for index, (source, target) in enumerate(pairs)]
    for copy in copies:
        copy.start()
    for copy in copies:
        copy.wait()


def prepare(audio_rows, *given):
    _, video_rows, width = given[3].shape
    outs = [like(3, audio_rows, width), like(2, video_rows, width), like(2 * video_rows, width)]
    return pl.pallas_call(
        prepare_kernel,
        in_specs=[pl.BlockSpec(memory_space=pl.ANY)] * 7,
        out_specs=[pl.BlockSpec(memory_space=pltpu.VMEM)] * 3,
        out_shape=outs,
        scratch_shapes=[pltpu.SemaphoreType.DMA((7,))],
        compiler_params=pltpu.CompilerParams(vmem_limit_bytes=VMEM),
        name="prepare",
    )(*given)


def scores(keys, queries, part, length_ref):
    raw = nt(keys, queries)
    if part == AUDIO:
        rows = raw.shape[0] // SIDE
        position = lax.broadcasted_iota(jnp.int32, (rows, raw.shape[1]), 0)
        pieces = [raw[place * rows : (place + 1) * rows] for place in range(SIDE)]
        vid = lax.axis_index("vid")
        for place in range(SIDE):
            chunk = (vid & ~(SIDE - 1)) + ((vid & (SIDE - 1)) ^ place)
            pieces[place] = jnp.where(position < length_ref[0] - chunk * rows, pieces[place], -1e30)
        raw = jnp.concatenate(pieces, axis=0)
    return raw


def attend(raw, values, up):
    peak = jnp.max(raw, axis=0, keepdims=True)
    expon = jnp.exp2((raw - peak) * (SCALE * LOG2_E))
    total = jnp.sum(expon, axis=0, keepdims=True)
    output = nn(values.T, expon.astype(BF16)) * (1.0 / total)
    delta = jnp.sum(up.T.astype(F32) * output, axis=0, keepdims=True)
    return output.astype(BF16), jnp.concatenate([peak * SCALE + jnp.log(total), delta], axis=0)


def forward_video_kernel(video_rows, *refs):
    gathered_ref, k_refs, o_ref, stats_ref = refs[0], refs[1:5], refs[5], refs[6]
    raw = scores(joined(k_refs, 0), flat(gathered_ref[:, :video_rows]), VIDEO, None)
    o_ref[0], stats_ref[0] = attend(raw, joined(k_refs, 1), flat(gathered_ref[:, video_rows:]))


def forward_kernel(video_rows, *refs):
    gathered_ref, k_refs, audio_q, length_ref = refs[0], (refs[1:5], refs[5:9]), refs[9:13], refs[13]
    gate_rows = head_row(refs[14]), head_row(refs[15])
    o_video_ref, stats_video_ref, o_ref, stats_ref, ordered_ref = refs[16:21]
    for place in range(SIDE):
        ordered_ref[(lax.axis_index("vid") >> 2) ^ place] = audio_q[place][...]
    up_audio = gated(flat(ordered_ref[:, 1]), gate_rows[AUDIO])
    raw = scores(joined(k_refs[VIDEO], 0), flat(ordered_ref[:, 0]), VIDEO, None)
    output, stats = attend(raw, joined(k_refs[VIDEO], 1), up_audio)
    o_ref[0, VIDEO] = jnp.concatenate([o_video_ref[0], output], axis=1)
    stats_video = jnp.concatenate([stats_video_ref[0], stats], axis=1)
    raw = scores(joined(k_refs[AUDIO], 0), queries_of(gathered_ref, ordered_ref, video_rows), AUDIO, length_ref)
    up = upstream(gathered_ref, ordered_ref, gate_rows, video_rows, AUDIO)
    o_ref[0, AUDIO], stats = attend(raw, joined(k_refs[AUDIO], 1), up)
    stats_ref[0] = jnp.concatenate([stats_video, stats], axis=0)


def merged_stats(refs, part):
    logs = [ref[0, 2 * part : 2 * part + 1] for ref in refs]
    peak = functools.reduce(jnp.maximum, logs)
    weights = [jnp.exp(local - peak) for local in logs]
    total = sum(weights)
    scale = 1.0 / total
    delta = sum(weight * ref[0, 2 * part + 1 : 2 * part + 2] for weight, ref in zip(weights, refs)) * scale
    return peak + jnp.log(total), delta, weights[0] * scale


def backward_keys(part, queries, up, stats_refs, k_refs, length_ref, k_outs, first):
    log_total, delta, factor = merged_stats(stats_refs, part)
    raw = scores(joined(k_refs, 0), queries, part, length_ref)
    probs = jnp.exp2(raw * (SCALE * LOG2_E) - log_total * LOG2_E)
    grad_values = nn(probs.astype(BF16), up).astype(BF16)
    grad_probs = nt(joined(k_refs, 1), up)
    grad_scores = (probs * (grad_probs - delta)).astype(BF16)
    grad_keys = (nn(grad_scores, queries) * SCALE).astype(BF16)
    rows = k_refs[0].shape[1]
    for place in range(SIDE):
        k_outs[place][0, first : first + rows] = grad_keys[place * rows : (place + 1) * rows]
        k_outs[place][1, first : first + rows] = grad_values[place * rows : (place + 1) * rows]
    return nn(joined(k_refs, 0).T, grad_scores), factor


def column_of(row):
    return jnp.broadcast_to(row, (HEAD_DIM, HEAD_DIM)).T[:, 0:1]


def backward_kernel(video_rows, *refs):
    gathered_ref, audio_q, k_video, k_audio, stats_refs = refs[0], refs[1], refs[2:6], refs[6:10], refs[10:14]
    gate_rows, length_ref, o_ref = (head_row(refs[14]), head_row(refs[15])), refs[16], refs[17]
    k_outs, q_out = refs[18:22], refs[22]
    audio_rows = audio_q.shape[2]
    rows = video_rows + audio_rows
    video = SIDE * video_rows
    queries = queries_of(gathered_ref, audio_q, video_rows)
    up = upstream(gathered_ref, audio_q, gate_rows, video_rows, VIDEO)
    term_video, factor = backward_keys(VIDEO, queries, up, stats_refs, k_video, length_ref, k_outs, 0)
    on_video = o_ref[0, VIDEO].astype(F32) * factor
    up = upstream(gathered_ref, audio_q, gate_rows, video_rows, AUDIO)
    term_audio, factor = backward_keys(AUDIO, queries, up, stats_refs, k_audio, length_ref, k_outs, video_rows)
    on_audio = o_ref[0, AUDIO].astype(F32) * factor
    grad_queries = term_video + term_audio
    cross_video, cross_audio = on_audio[:, :video], on_video[:, video:]
    merged = jnp.concatenate(
        [
            on_video[:, :video] + column_of(gate_rows[VIDEO]) * cross_video,
            on_audio[:, video:] + column_of(gate_rows[AUDIO]) * cross_audio,
        ],
        axis=1,
    )
    up_video, up_audio = upstreams_of(gathered_ref, audio_q, video_rows)
    video_sum = jnp.sum(up_video.T.astype(F32) * cross_video, axis=1, keepdims=True)
    audio_sum = jnp.sum(up_audio.T.astype(F32) * cross_audio, axis=1, keepdims=True)
    sums = jnp.concatenate(
        [jnp.broadcast_to(video_sum, (HEAD_DIM, 4)), jnp.broadcast_to(audio_sum, (HEAD_DIM, HEAD_DIM - 4))], axis=1
    ).T[0:GATE_ROWS]
    high = sums.astype(BF16)
    low = (sums - high.astype(F32)).astype(BF16)
    even = lax.broadcasted_iota(jnp.int32, sums.shape, 0) % 2 == 0
    sums = jnp.where(even, high.astype(F32), low.astype(F32)).astype(BF16)
    merged = merged.astype(BF16).T
    grad_queries = (grad_queries * SCALE).astype(BF16).T
    for index, array in ((0, merged), (1, grad_queries)):
        first = index * rows
        q_out[:, first : first + video_rows] = array[:video].reshape(SIDE, video_rows, HEAD_DIM)
        q_out[:, first + video_rows : first + rows] = array[video:].reshape(SIDE, audio_rows, HEAD_DIM)
    q_out[:, 2 * rows :] = jnp.broadcast_to(sums, (SIDE, *sums.shape))


def chunk_spec(array):
    shape = array.shape[:-1]
    return pl.BlockSpec((*shape, HEAD_DIM), lambda h: (0,) * len(shape) + (h,))


def head_spec(array):
    shape = array.shape[1:]
    return pl.BlockSpec((1, *shape), lambda h: (h,) + (0,) * len(shape))


def like(*shape, kind=BF16):
    return jax.ShapeDtypeStruct(shape, kind)


def cost(keys, queries, heads, products):
    return pl.CostEstimate(
        flops=2 * products * heads * keys * queries * HEAD_DIM,
        bytes_accessed=4 * heads * keys * queries,
        transcendentals=heads * keys * queries,
    )


def attention_forward_video(queries, video_keys, video_rows):
    heads = queries.shape[2] // HEAD_DIM
    video = SIDE * video_rows
    outs = [like(heads, HEAD_DIM, video), like(heads, 2, video, kind=F32)]
    chunks = [queries, *video_keys]
    return pl.pallas_call(
        functools.partial(forward_video_kernel, video_rows),
        grid=(heads,),
        in_specs=[chunk_spec(array) for array in chunks],
        out_specs=[head_spec(array) for array in outs],
        out_shape=outs,
        cost_estimate=cost(video, video, heads, 2),
        compiler_params=pltpu.CompilerParams(vmem_limit_bytes=VMEM),
        name="forward_video",
    )(*chunks)


def attention_forward(queries, audio_q, video_keys, audio_keys, audio_len, gates, earlier, video_rows):
    _, audio_rows, width = audio_q[0].shape
    heads = width // HEAD_DIM
    total = SIDE * (video_rows + audio_rows)
    outs = [like(heads, 2, HEAD_DIM, total), like(heads, 4, total, kind=F32)]
    ordered = like(SIDE, 2, audio_rows, width)
    chunks = [queries, *video_keys, *audio_keys, *audio_q]
    return pl.pallas_call(
        functools.partial(forward_kernel, video_rows),
        grid=(heads,),
        in_specs=[chunk_spec(array) for array in chunks]
        + [pl.BlockSpec(memory_space=pltpu.SMEM)]
        + [pl.BlockSpec(gate.shape, lambda h: (0,)) for gate in gates]
        + [head_spec(array) for array in earlier],
        out_specs=[head_spec(array) for array in outs] + [chunk_spec(ordered)],
        out_shape=[*outs, ordered],
        cost_estimate=cost(total, total, heads, 1),
        compiler_params=pltpu.CompilerParams(vmem_limit_bytes=VMEM),
        name="forward",
    )(*chunks, audio_len, *gates, *earlier)


def attention_backward(queries, audio_q, video_keys, audio_keys, stats, gates, audio_len, outputs, video_rows):
    width = queries.shape[2]
    heads = width // HEAD_DIM
    rows = video_rows + audio_q.shape[2]
    outs = [like(2, rows, width)] * SIDE + [like(SIDE, 2 * rows + GATE_ROWS, width)]
    chunks = [queries, audio_q, *video_keys, *audio_keys]
    *key_parts, query_parts = pl.pallas_call(
        functools.partial(backward_kernel, video_rows),
        grid=(heads,),
        in_specs=[chunk_spec(array) for array in chunks]
        + [head_spec(array) for array in stats]
        + [pl.BlockSpec(gate.shape, lambda h: (0,)) for gate in gates]
        + [pl.BlockSpec(memory_space=pltpu.SMEM), head_spec(outputs)],
        out_specs=[chunk_spec(array) for array in outs],
        out_shape=outs,
        cost_estimate=cost(SIDE * rows, SIDE * rows, heads, 4),
        compiler_params=pltpu.CompilerParams(vmem_limit_bytes=VMEM),
        name="backward",
    )(*chunks, *stats, *gates, audio_len, outputs)
    return key_parts, query_parts


def total_of(refs, *index):
    return sum(ref[index].astype(F32) for ref in refs)


def finish_queries_kernel(parts_ref, video_out, audio_out, video_q, audio_q, gate_ref):
    video_rows, audio_rows = video_out.shape[1], audio_out.shape[1]
    rows = video_rows + audio_rows
    parts = [parts_ref.at[place] for place in range(SIDE)]
    for index, video, audio in ((0, video_out, audio_out), (1, video_q, audio_q)):
        first = index * rows
        video[0] = total_of(parts, slice(first, first + video_rows)).astype(BF16)
        audio[0] = total_of(parts, slice(first + video_rows, first + rows)).astype(BF16)
    gates = total_of(parts, slice(2 * rows, None))
    width = gates.shape[1]
    video_gate = jnp.broadcast_to(gates[0:1] + gates[1:2], (4, width))
    audio_gate = jnp.broadcast_to(gates[4:5] + gates[5:6], (4, width))
    gate_ref[...] = jnp.concatenate([video_gate, audio_gate], axis=0)


def finish_queries(parts, video_rows, audio_rows):
    width = parts.shape[2]
    video, audio = like(1, video_rows, width), like(1, audio_rows, width)
    return pl.pallas_call(
        finish_queries_kernel,
        out_shape=[video, audio, video, audio, like(8, width, kind=F32)],
        compiler_params=pltpu.CompilerParams(vmem_limit_bytes=8 * 2**20),
        name="finish_queries",
    )(parts)


def finish_keys_kernel(*refs):
    parts, (video_k, video_v, audio_k, audio_v) = refs[:SIDE], refs[SIDE:]
    rows = video_k.shape[1]
    for index, video, audio in ((0, video_k, audio_k), (1, video_v, audio_v)):
        video[0] = total_of(parts, index, slice(0, rows)).astype(BF16)
        audio[0] = total_of(parts, index, slice(rows, None)).astype(BF16)


def finish_keys(parts, video_rows, audio_rows):
    width = parts[0].shape[2]
    video, audio = like(1, video_rows, width), like(1, audio_rows, width)
    return pl.pallas_call(
        finish_keys_kernel,
        out_shape=[video, video, audio, audio],
        compiler_params=pltpu.CompilerParams(vmem_limit_bytes=8 * 2**20),
        name="finish_keys",
    )(*parts)


def own_audio(array):
    vid_size, aud_size = lax.axis_size("vid"), lax.axis_size("aud")
    pairs = []
    for vid in range(vid_size):
        for aud in range(aud_size):
            to_vid, to_aud = audio_target(vid, aud)
            pairs.append((vid * aud_size + aud, to_vid * aud_size + to_aud))
    return lax.ppermute(array, ("vid", "aud"), pairs)


def fenced(holds, function, *arrays):
    outs = jax.eval_shape(function, *arrays)
    return lax.cond(
        holds, function, lambda *_: jax.tree.map(lambda out: jnp.zeros(out.shape, out.dtype), outs), *arrays
    )


def shards(
    video_q, video_k, video_v, audio_q, audio_k, audio_v, video_gate, audio_gate, audio_len, d_video_out, d_audio_out
):
    vid = lax.axis_index("vid")
    video_rows, audio_rows = video_q.shape[1], d_audio_out.shape[1]
    holds = audio_len[0] > 0
    send_audio, video_kv, queries = prepare(
        audio_rows, audio_q, audio_k, audio_v, video_q, video_k, video_v, d_video_out
    )
    gates = video_gate, audio_gate

    def first_chunks(send_audio, video_kv, queries):
        return own_audio(send_audio), tuple(gathered(video_kv, along_z)[1:]), all_along_x(queries)

    audio, video_keys, queries = fenced(holds, first_chunks, send_audio, video_kv, queries)
    video_keys = [video_kv, *video_keys]
    audio_queries, audio_keys = split_audio(audio, d_audio_out)
    audio_keys = gathered(audio_keys, along_z)
    audio_queries = gathered(audio_queries, along_x)
    earlier = attention_forward_video(queries, video_keys, video_rows)
    outputs, stats, audio_queries = attention_forward(
        queries, audio_queries, video_keys, audio_keys, audio_len, gates, earlier, video_rows
    )
    key_parts, query_parts = attention_backward(
        queries, audio_queries, video_keys, audio_keys, gathered(stats, along_x), gates, audio_len, outputs, video_rows
    )

    def query_results(parts):
        parts = lax.all_to_all(parts, "vid", 0, 0, axis_index_groups=ALONG_X, tiled=True)
        *results, gate = finish_queries(parts, video_rows, audio_rows)
        for distance in (1, 2):
            gate = gate + along_z(gate, distance)
        return (*results, gate)

    video_out, audio_out, grad_video_q, grad_audio_q, gate = fenced(holds, query_results, query_parts)
    key_parts = returned(key_parts, along_z)
    other = lax.ppermute(gate, "pair", [(0, 1), (1, 0)])
    key_grads = finish_keys(key_parts, video_rows, audio_rows)
    other, (grad_video_k, grad_video_v, grad_audio_k, grad_audio_v) = lax.optimization_barrier((other, key_grads))
    gate = gate + other
    return (
        video_out,
        audio_out,
        grad_video_q,
        grad_video_k,
        grad_video_v,
        grad_audio_q,
        grad_audio_k,
        grad_audio_v,
        gate[0],
        gate[7],
    )


def solution(mesh):
    split = P("pair", "vid", "aud")
    rows = P("pair", "aud", None)
    return jax.shard_map(
        shards,
        mesh=mesh,
        in_specs=(split, split, split, rows, rows, rows, P("aud"), P("aud"), P("pair"), split, split),
        out_specs=(split,) * 8 + (P("aud"), P("aud")),
        check_vma=False,
    )
```

```python
import functools

import jax
import jax.numpy as jnp
from jax import lax
from jax.experimental import pallas as pl
from jax.experimental.pallas import tpu as pltpu
from jax.sharding import PartitionSpec as P

HEAD_DIM = 128
SCALE = HEAD_DIM ** (-0.5)
SIDE = 4
F32 = jnp.float32
BF16 = jnp.bfloat16
VIDEO, AUDIO = 0, 1
GATE_ROWS = 16
VMEM = 60 * 2**20
LOG2_E = 1.4426950408889634

ALONG_X = [[x * SIDE + z for x in range(SIDE)] for z in range(SIDE)]


def along_x(array, distance):
    pairs = [(x * SIDE + z, (x ^ distance) * SIDE + z) for x in range(SIDE) for z in range(SIDE)]
    return lax.ppermute(array, "vid", pairs)


def along_z(array, distance):
    pairs = [(x * SIDE + z, x * SIDE + (z ^ distance)) for x in range(SIDE) for z in range(SIDE)]
    return lax.ppermute(array, "vid", pairs)


def all_along_x(array):
    return lax.all_gather(array, "vid", axis=0, axis_index_groups=ALONG_X)


def gathered(array, along):
    return [array] + [along(array, distance) for distance in range(1, SIDE)]


def returned(parts, along):
    return [parts[0]] + [along(parts[place], place) for place in range(1, SIDE)]


def nt(a, b):
    return lax.dot_general(a, b, (((1,), (1,)), ((), ())), preferred_element_type=F32)


def nn(a, b):
    return lax.dot_general(a, b, (((1,), (0,)), ((), ())), preferred_element_type=F32)


def joined(refs, index):
    return jnp.concatenate([ref[index] for ref in refs], axis=0)


def gated(rows, gate_row):
    return (gate_row * rows.astype(F32)).astype(BF16)


def flat(block):
    return block.reshape(-1, block.shape[-1])


def queries_of(gathered_ref, audio_ref, video_rows):
    return jnp.concatenate([flat(gathered_ref[:, :video_rows]), flat(audio_ref[:, 0])], axis=0)


def upstreams_of(gathered_ref, audio_ref, video_rows):
    return flat(gathered_ref[:, video_rows:]), flat(audio_ref[:, 1])


def head_row(ref):
    first = pl.multiple_of(pl.program_id(0) * HEAD_DIM, HEAD_DIM)
    return ref[pl.ds(first, HEAD_DIM)].reshape(1, HEAD_DIM)


def upstream(gathered_ref, audio_ref, gate_rows, video_rows, part):
    video, audio = upstreams_of(gathered_ref, audio_ref, video_rows)
    if part == VIDEO:
        audio = gated(audio, gate_rows[AUDIO])
    else:
        video = gated(video, gate_rows[VIDEO])
    return jnp.concatenate([video, audio], axis=0)


def split_audio_kernel(audio_ref, up_ref, queries_ref, keys_ref):
    queries_ref[0] = audio_ref[0]
    queries_ref[1] = up_ref[0]
    keys_ref[0] = audio_ref[1]
    keys_ref[1] = audio_ref[2]


def split_audio(audio, d_audio):
    _, rows, width = audio.shape
    return pl.pallas_call(
        split_audio_kernel,
        out_shape=[like(2, rows, width)] * 2,
        compiler_params=pltpu.CompilerParams(vmem_limit_bytes=8 * 2**20),
        name="split_audio",
    )(audio, d_audio)


def audio_target(vid, aud):
    x, z, y, half = vid >> 2, vid & 3, aud >> 1, aud & 1
    offset = (x - y) & 3
    to_y = (y - offset + 2 * (1 - (offset & 1))) & 3
    return SIDE * y + 2 * half + (z & 1), 2 * to_y + (z >> 1)


def prepare_kernel(aq_ref, ak_ref, av_ref, vq_ref, vk_ref, vv_ref, dv_ref, audio, video_kv, queries, sems):
    to_vid, to_aud = audio_target(lax.axis_index("vid"), lax.axis_index("aud"))
    rows, width = vq_ref.shape[1:]
    audio_rows = audio.shape[1]
    taken = pl.ds(pl.multiple_of((to_vid & 1) * audio_rows, audio_rows), audio_rows)
    columns = pl.ds(pl.multiple_of(to_aud * width, HEAD_DIM), width)
    pairs = [(ref.at[0, taken, columns], audio.at[index]) for index, ref in enumerate((aq_ref, ak_ref, av_ref))]
    pairs += [(vk_ref.at[0], video_kv.at[0]), (vv_ref.at[0], video_kv.at[1])]
    pairs += [(vq_ref.at[0], queries.at[pl.ds(0, rows)]), (dv_ref.at[0], queries.at[pl.ds(rows, rows)])]
    copies = [pltpu.make_async_copy(source, target, sems.at[index]) for index, (source, target) in enumerate(pairs)]
    for copy in copies:
        copy.start()
    for copy in copies:
        copy.wait()


def prepare(audio_rows, *given):
    _, video_rows, width = given[3].shape
    outs = [like(3, audio_rows, width), like(2, video_rows, width), like(2 * video_rows, width)]
    return pl.pallas_call(
        prepare_kernel,
        in_specs=[pl.BlockSpec(memory_space=pl.ANY)] * 7,
        out_specs=[pl.BlockSpec(memory_space=pltpu.VMEM)] * 3,
        out_shape=outs,
        scratch_shapes=[pltpu.SemaphoreType.DMA((7,))],
        compiler_params=pltpu.CompilerParams(vmem_limit_bytes=VMEM),
        name="prepare",
    )(*given)


def scores(keys, queries, part, length_ref):
    raw = nt(keys, queries)
    if part == AUDIO:
        rows = raw.shape[0] // SIDE
        position = lax.broadcasted_iota(jnp.int32, (rows, raw.shape[1]), 0)
        pieces = [raw[place * rows : (place + 1) * rows] for place in range(SIDE)]
        vid = lax.axis_index("vid")
        for place in range(SIDE):
            chunk = (vid & ~(SIDE - 1)) + ((vid & (SIDE - 1)) ^ place)
            pieces[place] = jnp.where(position < length_ref[0] - chunk * rows, pieces[place], -1e30)
        raw = jnp.concatenate(pieces, axis=0)
    return raw


def attend(raw, values, up):
    peak = jnp.max(raw, axis=0, keepdims=True)
    expon = jnp.exp2((raw - peak) * (SCALE * LOG2_E))
    total = jnp.sum(expon, axis=0, keepdims=True)
    output = nn(values.T, expon.astype(BF16)) * (1.0 / total)
    delta = jnp.sum(up.T.astype(F32) * output, axis=0, keepdims=True)
    return output.astype(BF16), jnp.concatenate([peak * SCALE + jnp.log(total), delta], axis=0)


def forward_video_kernel(video_rows, *refs):
    gathered_ref, k_refs, o_ref, stats_ref = refs[0], refs[1:5], refs[5], refs[6]
    raw = scores(joined(k_refs, 0), flat(gathered_ref[:, :video_rows]), VIDEO, None)
    o_ref[0], stats_ref[0] = attend(raw, joined(k_refs, 1), flat(gathered_ref[:, video_rows:]))


def forward_kernel(video_rows, *refs):
    gathered_ref, k_refs, audio_q, length_ref = refs[0], (refs[1:5], refs[5:9]), refs[9:13], refs[13]
    gate_rows = head_row(refs[14]), head_row(refs[15])
    o_video_ref, stats_video_ref, o_ref, stats_ref, ordered_ref = refs[16:21]
    for place in range(SIDE):
        ordered_ref[(lax.axis_index("vid") >> 2) ^ place] = audio_q[place][...]
    up_audio = gated(flat(ordered_ref[:, 1]), gate_rows[AUDIO])
    raw = scores(joined(k_refs[VIDEO], 0), flat(ordered_ref[:, 0]), VIDEO, None)
    output, stats = attend(raw, joined(k_refs[VIDEO], 1), up_audio)
    o_ref[0, VIDEO] = jnp.concatenate([o_video_ref[0], output], axis=1)
    stats_video = jnp.concatenate([stats_video_ref[0], stats], axis=1)
    raw = scores(joined(k_refs[AUDIO], 0), queries_of(gathered_ref, ordered_ref, video_rows), AUDIO, length_ref)
    up = upstream(gathered_ref, ordered_ref, gate_rows, video_rows, AUDIO)
    o_ref[0, AUDIO], stats = attend(raw, joined(k_refs[AUDIO], 1), up)
    stats_ref[0] = jnp.concatenate([stats_video, stats], axis=0)


def merged_stats(refs, part):
    logs = [ref[0, 2 * part : 2 * part + 1] for ref in refs]
    peak = functools.reduce(jnp.maximum, logs)
    weights = [jnp.exp(local - peak) for local in logs]
    total = sum(weights)
    scale = 1.0 / total
    delta = sum(weight * ref[0, 2 * part + 1 : 2 * part + 2] for weight, ref in zip(weights, refs)) * scale
    return peak + jnp.log(total), delta, weights[0] * scale


def backward_keys(part, queries, up, stats_refs, k_refs, length_ref, k_outs, first):
    log_total, delta, factor = merged_stats(stats_refs, part)
    raw = scores(joined(k_refs, 0), queries, part, length_ref)
    probs = jnp.exp2(raw * (SCALE * LOG2_E) - log_total * LOG2_E)
    grad_values = nn(probs.astype(BF16), up).astype(BF16)
    grad_probs = nt(joined(k_refs, 1), up)
    grad_scores = (probs * (grad_probs - delta)).astype(BF16)
    grad_keys = (nn(grad_scores, queries) * SCALE).astype(BF16)
    rows = k_refs[0].shape[1]
    for place in range(SIDE):
        k_outs[place][0, first : first + rows] = grad_keys[place * rows : (place + 1) * rows]
        k_outs[place][1, first : first + rows] = grad_values[place * rows : (place + 1) * rows]
    return nn(joined(k_refs, 0).T, grad_scores), factor


def column_of(row):
    return jnp.broadcast_to(row, (HEAD_DIM, HEAD_DIM)).T[:, 0:1]


def backward_kernel(video_rows, *refs):
    gathered_ref, audio_q, k_video, k_audio, stats_refs = refs[0], refs[1], refs[2:6], refs[6:10], refs[10:14]
    gate_rows, length_ref, o_ref = (head_row(refs[14]), head_row(refs[15])), refs[16], refs[17]
    k_outs, q_out = refs[18:22], refs[22]
    audio_rows = audio_q.shape[2]
    rows = video_rows + audio_rows
    video = SIDE * video_rows
    queries = queries_of(gathered_ref, audio_q, video_rows)
    up = upstream(gathered_ref, audio_q, gate_rows, video_rows, VIDEO)
    term_video, factor = backward_keys(VIDEO, queries, up, stats_refs, k_video, length_ref, k_outs, 0)
    on_video = o_ref[0, VIDEO].astype(F32) * factor
    up = upstream(gathered_ref, audio_q, gate_rows, video_rows, AUDIO)
    term_audio, factor = backward_keys(AUDIO, queries, up, stats_refs, k_audio, length_ref, k_outs, video_rows)
    on_audio = o_ref[0, AUDIO].astype(F32) * factor
    grad_queries = term_video + term_audio
    cross_video, cross_audio = on_audio[:, :video], on_video[:, video:]
    merged = jnp.concatenate(
        [
            on_video[:, :video] + column_of(gate_rows[VIDEO]) * cross_video,
            on_audio[:, video:] + column_of(gate_rows[AUDIO]) * cross_audio,
        ],
        axis=1,
    )
    up_video, up_audio = upstreams_of(gathered_ref, audio_q, video_rows)
    video_sum = jnp.sum(up_video.T.astype(F32) * cross_video, axis=1, keepdims=True)
    audio_sum = jnp.sum(up_audio.T.astype(F32) * cross_audio, axis=1, keepdims=True)
    sums = jnp.concatenate(
        [jnp.broadcast_to(video_sum, (HEAD_DIM, 4)), jnp.broadcast_to(audio_sum, (HEAD_DIM, HEAD_DIM - 4))], axis=1
    ).T[0:GATE_ROWS]
    high = sums.astype(BF16)
    low = (sums - high.astype(F32)).astype(BF16)
    even = lax.broadcasted_iota(jnp.int32, sums.shape, 0) % 2 == 0
    sums = jnp.where(even, high.astype(F32), low.astype(F32)).astype(BF16)
    merged = merged.astype(BF16).T
    grad_queries = (grad_queries * SCALE).astype(BF16).T
    for index, array in ((0, merged), (1, grad_queries)):
        first = index * rows
        q_out[:, first : first + video_rows] = array[:video].reshape(SIDE, video_rows, HEAD_DIM)
        q_out[:, first + video_rows : first + rows] = array[video:].reshape(SIDE, audio_rows, HEAD_DIM)
    q_out[:, 2 * rows :] = jnp.broadcast_to(sums, (SIDE, *sums.shape))


def chunk_spec(array):
    shape = array.shape[:-1]
    return pl.BlockSpec((*shape, HEAD_DIM), lambda h: (0,) * len(shape) + (h,))


def head_spec(array):
    shape = array.shape[1:]
    return pl.BlockSpec((1, *shape), lambda h: (h,) + (0,) * len(shape))


def like(*shape, kind=BF16):
    return jax.ShapeDtypeStruct(shape, kind)


def cost(keys, queries, heads, products):
    return pl.CostEstimate(
        flops=2 * products * heads * keys * queries * HEAD_DIM,
        bytes_accessed=4 * heads * keys * queries,
        transcendentals=heads * keys * queries,
    )


def attention_forward_video(queries, video_keys, video_rows):
    heads = queries.shape[2] // HEAD_DIM
    video = SIDE * video_rows
    outs = [like(heads, HEAD_DIM, video), like(heads, 2, video, kind=F32)]
    chunks = [queries, *video_keys]
    return pl.pallas_call(
        functools.partial(forward_video_kernel, video_rows),
        grid=(heads,),
        in_specs=[chunk_spec(array) for array in chunks],
        out_specs=[head_spec(array) for array in outs],
        out_shape=outs,
        cost_estimate=cost(video, video, heads, 2),
        compiler_params=pltpu.CompilerParams(vmem_limit_bytes=VMEM),
        name="forward_video",
    )(*chunks)


def attention_forward(queries, audio_q, video_keys, audio_keys, audio_len, gates, earlier, video_rows):
    _, audio_rows, width = audio_q[0].shape
    heads = width // HEAD_DIM
    total = SIDE * (video_rows + audio_rows)
    outs = [like(heads, 2, HEAD_DIM, total), like(heads, 4, total, kind=F32)]
    ordered = like(SIDE, 2, audio_rows, width)
    chunks = [queries, *video_keys, *audio_keys, *audio_q]
    return pl.pallas_call(
        functools.partial(forward_kernel, video_rows),
        grid=(heads,),
        in_specs=[chunk_spec(array) for array in chunks]
        + [pl.BlockSpec(memory_space=pltpu.SMEM)]
        + [pl.BlockSpec(gate.shape, lambda h: (0,)) for gate in gates]
        + [head_spec(array) for array in earlier],
        out_specs=[head_spec(array) for array in outs] + [chunk_spec(ordered)],
        out_shape=[*outs, ordered],
        cost_estimate=cost(total, total, heads, 1),
        compiler_params=pltpu.CompilerParams(vmem_limit_bytes=VMEM),
        name="forward",
    )(*chunks, audio_len, *gates, *earlier)


def attention_backward(queries, audio_q, video_keys, audio_keys, stats, gates, audio_len, outputs, video_rows):
    width = queries.shape[2]
    heads = width // HEAD_DIM
    rows = video_rows + audio_q.shape[2]
    outs = [like(2, rows, width)] * SIDE + [like(SIDE, 2 * rows + GATE_ROWS, width)]
    chunks = [queries, audio_q, *video_keys, *audio_keys]
    *key_parts, query_parts = pl.pallas_call(
        functools.partial(backward_kernel, video_rows),
        grid=(heads,),
        in_specs=[chunk_spec(array) for array in chunks]
        + [head_spec(array) for array in stats]
        + [pl.BlockSpec(gate.shape, lambda h: (0,)) for gate in gates]
        + [pl.BlockSpec(memory_space=pltpu.SMEM), head_spec(outputs)],
        out_specs=[chunk_spec(array) for array in outs],
        out_shape=outs,
        cost_estimate=cost(SIDE * rows, SIDE * rows, heads, 4),
        compiler_params=pltpu.CompilerParams(vmem_limit_bytes=VMEM),
        name="backward",
    )(*chunks, *stats, *gates, audio_len, outputs)
    return key_parts, query_parts


def total_of(refs, *index):
    return sum(ref[index].astype(F32) for ref in refs)


def finish_queries_kernel(parts_ref, video_out, audio_out, video_q, audio_q, gate_ref):
    video_rows, audio_rows = video_out.shape[1], audio_out.shape[1]
    rows = video_rows + audio_rows
    parts = [parts_ref.at[place] for place in range(SIDE)]
    for index, video, audio in ((0, video_out, audio_out), (1, video_q, audio_q)):
        first = index * rows
        video[0] = total_of(parts, slice(first, first + video_rows)).astype(BF16)
        audio[0] = total_of(parts, slice(first + video_rows, first + rows)).astype(BF16)
    gates = total_of(parts, slice(2 * rows, None))
    width = gates.shape[1]
    video_gate = jnp.broadcast_to(gates[0:1] + gates[1:2], (4, width))
    audio_gate = jnp.broadcast_to(gates[4:5] + gates[5:6], (4, width))
    gate_ref[...] = jnp.concatenate([video_gate, audio_gate], axis=0)


def finish_queries(parts, video_rows, audio_rows):
    width = parts.shape[2]
    video, audio = like(1, video_rows, width), like(1, audio_rows, width)
    return pl.pallas_call(
        finish_queries_kernel,
        out_shape=[video, audio, video, audio, like(8, width, kind=F32)],
        compiler_params=pltpu.CompilerParams(vmem_limit_bytes=8 * 2**20),
        name="finish_queries",
    )(parts)


def finish_keys_kernel(*refs):
    parts, (video_k, video_v, audio_k, audio_v) = refs[:SIDE], refs[SIDE:]
    rows = video_k.shape[1]
    for index, video, audio in ((0, video_k, audio_k), (1, video_v, audio_v)):
        video[0] = total_of(parts, index, slice(0, rows)).astype(BF16)
        audio[0] = total_of(parts, index, slice(rows, None)).astype(BF16)


def finish_keys(parts, video_rows, audio_rows):
    width = parts[0].shape[2]
    video, audio = like(1, video_rows, width), like(1, audio_rows, width)
    return pl.pallas_call(
        finish_keys_kernel,
        out_shape=[video, video, audio, audio],
        compiler_params=pltpu.CompilerParams(vmem_limit_bytes=8 * 2**20),
        name="finish_keys",
    )(*parts)


def own_audio(array):
    vid_size, aud_size = lax.axis_size("vid"), lax.axis_size("aud")
    pairs = []
    for vid in range(vid_size):
        for aud in range(aud_size):
            to_vid, to_aud = audio_target(vid, aud)
            pairs.append((vid * aud_size + aud, to_vid * aud_size + to_aud))
    return lax.ppermute(array, ("vid", "aud"), pairs)


def fenced(holds, function, *arrays):
    outs = jax.eval_shape(function, *arrays)
    return lax.cond(
        holds, function, lambda *_: jax.tree.map(lambda out: jnp.zeros(out.shape, out.dtype), outs), *arrays
    )


def shards(
    video_q, video_k, video_v, audio_q, audio_k, audio_v, video_gate, audio_gate, audio_len, d_video_out, d_audio_out
):
    vid = lax.axis_index("vid")
    video_rows, audio_rows = video_q.shape[1], d_audio_out.shape[1]
    holds = audio_len[0] > 0
    send_audio, video_kv, queries = prepare(
        audio_rows, audio_q, audio_k, audio_v, video_q, video_k, video_v, d_video_out
    )
    gates = video_gate, audio_gate

    def first_chunks(send_audio, video_kv, queries):
        return own_audio(send_audio), tuple(gathered(video_kv, along_z)[1:]), all_along_x(queries)

    audio, video_keys, queries = fenced(holds, first_chunks, send_audio, video_kv, queries)
    video_keys = [video_kv, *video_keys]
    audio_queries, audio_keys = split_audio(audio, d_audio_out)
    audio_keys = gathered(audio_keys, along_z)
    audio_queries = gathered(audio_queries, along_x)
    earlier = attention_forward_video(queries, video_keys, video_rows)
    outputs, stats, audio_queries = attention_forward(
        queries, audio_queries, video_keys, audio_keys, audio_len, gates, earlier, video_rows
    )
    key_parts, query_parts = attention_backward(
        queries, audio_queries, video_keys, audio_keys, gathered(stats, along_x), gates, audio_len, outputs, video_rows
    )

    def query_results(parts):
        parts = lax.all_to_all(parts, "vid", 0, 0, axis_index_groups=ALONG_X, tiled=True)
        return tuple(finish_queries(parts, video_rows, audio_rows))

    video_out, audio_out, grad_video_q, grad_audio_q, gate = fenced(holds, query_results, query_parts)
    key_parts = returned(key_parts, along_z)
    gate, key_parts[1] = lax.optimization_barrier((gate, key_parts[1]))
    gate = sum(gathered(gate, along_z))
    other = lax.ppermute(gate, "pair", [(0, 1), (1, 0)])
    key_grads = finish_keys(key_parts, video_rows, audio_rows)
    other, (grad_video_k, grad_video_v, grad_audio_k, grad_audio_v) = lax.optimization_barrier((other, key_grads))
    gate = gate + other
    return (
        video_out,
        audio_out,
        grad_video_q,
        grad_video_k,
        grad_video_v,
        grad_audio_q,
        grad_audio_k,
        grad_audio_v,
        gate[0],
        gate[7],
    )


def solution(mesh):
    split = P("pair", "vid", "aud")
    rows = P("pair", "aud", None)
    return jax.shard_map(
        shards,
        mesh=mesh,
        in_specs=(split, split, split, rows, rows, rows, P("aud"), P("aud"), P("pair"), split, split),
        out_specs=(split,) * 8 + (P("aud"), P("aud")),
        check_vma=False,
    )
```

```python
import functools

import jax
import jax.numpy as jnp
from jax import lax
from jax.experimental import pallas as pl
from jax.experimental.pallas import tpu as pltpu
from jax.sharding import PartitionSpec as P

HEAD_DIM = 128
SCALE = HEAD_DIM ** (-0.5)
SIDE = 4
F32 = jnp.float32
BF16 = jnp.bfloat16
VIDEO, AUDIO = 0, 1
GATE_ROWS = 16
VMEM = 60 * 2**20
LOG2_E = 1.4426950408889634

ALONG_X = [[x * SIDE + z for x in range(SIDE)] for z in range(SIDE)]


def along_x(array, distance):
    pairs = [(x * SIDE + z, (x ^ distance) * SIDE + z) for x in range(SIDE) for z in range(SIDE)]
    return lax.ppermute(array, "vid", pairs)


def along_z(array, distance):
    pairs = [(x * SIDE + z, x * SIDE + (z ^ distance)) for x in range(SIDE) for z in range(SIDE)]
    return lax.ppermute(array, "vid", pairs)


def all_along_x(array):
    return lax.all_gather(array, "vid", axis=0, axis_index_groups=ALONG_X)


def gathered(array, along):
    return [array] + [along(array, distance) for distance in range(1, SIDE)]


def returned(parts, along):
    return [parts[0]] + [along(parts[place], place) for place in range(1, SIDE)]


def nt(a, b):
    return lax.dot_general(a, b, (((1,), (1,)), ((), ())), preferred_element_type=F32)


def nn(a, b):
    return lax.dot_general(a, b, (((1,), (0,)), ((), ())), preferred_element_type=F32)


def joined(refs, index):
    return jnp.concatenate([ref[index] for ref in refs], axis=0)


def gated(rows, gate_row):
    return (gate_row * rows.astype(F32)).astype(BF16)


def flat(block):
    return block.reshape(-1, block.shape[-1])


def queries_of(gathered_ref, audio_ref, audio_rows):
    return jnp.concatenate([flat(gathered_ref[...]), flat(audio_ref[:, :audio_rows])], axis=0)


def upstreams_of(audio_ref, audio_rows):
    return flat(audio_ref[:, 2 * audio_rows :]), flat(audio_ref[:, audio_rows : 2 * audio_rows])


def head_row(ref):
    first = pl.multiple_of(pl.program_id(0) * HEAD_DIM, HEAD_DIM)
    return ref[pl.ds(first, HEAD_DIM)].reshape(1, HEAD_DIM)


def upstream(audio_ref, gate_rows, audio_rows, part):
    video, audio = upstreams_of(audio_ref, audio_rows)
    if part == VIDEO:
        audio = gated(audio, gate_rows[AUDIO])
    else:
        video = gated(video, gate_rows[VIDEO])
    return jnp.concatenate([video, audio], axis=0)


def split_audio_kernel(audio_ref, up_audio_ref, up_video_ref, queries_ref, keys_ref):
    rows = audio_ref.shape[1]
    queries_ref[:rows] = audio_ref[0]
    queries_ref[rows : 2 * rows] = up_audio_ref[0]
    queries_ref[2 * rows :] = up_video_ref[0]
    keys_ref[0] = audio_ref[1]
    keys_ref[1] = audio_ref[2]


def split_audio(audio, d_audio, d_video):
    _, rows, width = audio.shape
    return pl.pallas_call(
        split_audio_kernel,
        out_shape=[like(2 * rows + d_video.shape[1], width), like(2, rows, width)],
        compiler_params=pltpu.CompilerParams(vmem_limit_bytes=8 * 2**20),
        name="split_audio",
    )(audio, d_audio, d_video)


def audio_target(vid, aud):
    x, z, y, half = vid >> 2, vid & 3, aud >> 1, aud & 1
    offset = (x - y) & 3
    to_y = (y - offset + 2 * (1 - (offset & 1))) & 3
    return SIDE * y + 2 * half + (z & 1), 2 * to_y + (z >> 1)


def prepare_kernel(aq_ref, ak_ref, av_ref, vq_ref, vk_ref, vv_ref, audio, video_kv, queries, sems):
    to_vid, to_aud = audio_target(lax.axis_index("vid"), lax.axis_index("aud"))
    audio_rows, width = audio.shape[1:]
    taken = pl.ds(pl.multiple_of((to_vid & 1) * audio_rows, audio_rows), audio_rows)
    columns = pl.ds(pl.multiple_of(to_aud * width, HEAD_DIM), width)
    pairs = [(ref.at[0, taken, columns], audio.at[index]) for index, ref in enumerate((aq_ref, ak_ref, av_ref))]
    pairs += [(vk_ref.at[0], video_kv.at[0]), (vv_ref.at[0], video_kv.at[1])]
    pairs += [(vq_ref.at[0], queries)]
    copies = [pltpu.make_async_copy(source, target, sems.at[index]) for index, (source, target) in enumerate(pairs)]
    for copy in copies:
        copy.start()
    for copy in copies:
        copy.wait()


def prepare(audio_rows, *given):
    _, video_rows, width = given[3].shape
    outs = [like(3, audio_rows, width), like(2, video_rows, width), like(video_rows, width)]
    return pl.pallas_call(
        prepare_kernel,
        in_specs=[pl.BlockSpec(memory_space=pl.ANY)] * 6,
        out_specs=[pl.BlockSpec(memory_space=pltpu.VMEM)] * 3,
        out_shape=outs,
        scratch_shapes=[pltpu.SemaphoreType.DMA((6,))],
        compiler_params=pltpu.CompilerParams(vmem_limit_bytes=VMEM),
        name="prepare",
    )(*given)


def scores(keys, queries, part, length_ref):
    raw = nt(keys, queries)
    if part == AUDIO:
        rows = raw.shape[0] // SIDE
        position = lax.broadcasted_iota(jnp.int32, (rows, raw.shape[1]), 0)
        pieces = [raw[place * rows : (place + 1) * rows] for place in range(SIDE)]
        vid = lax.axis_index("vid")
        for place in range(SIDE):
            chunk = (vid & ~(SIDE - 1)) + ((vid & (SIDE - 1)) ^ place)
            pieces[place] = jnp.where(position < length_ref[0] - chunk * rows, pieces[place], -1e30)
        raw = jnp.concatenate(pieces, axis=0)
    return raw


def row_delta(up, output):
    return jnp.sum(up.T.astype(F32) * output, axis=0, keepdims=True)


def attend(raw, values, up):
    peak = jnp.max(raw, axis=0, keepdims=True)
    expon = jnp.exp2((raw - peak) * (SCALE * LOG2_E))
    total = jnp.sum(expon, axis=0, keepdims=True)
    output = nn(values.T, expon.astype(BF16)) * (1.0 / total)
    log_total = peak * SCALE + jnp.log(total)
    delta = log_total if up is None else row_delta(up, output)
    return output.astype(BF16), jnp.concatenate([log_total, delta], axis=0)


def forward_video_kernel(*refs):
    gathered_ref, k_refs, o_ref, stats_ref = refs[0], refs[1:5], refs[5], refs[6]
    raw = scores(joined(k_refs, 0), flat(gathered_ref[...]), VIDEO, None)
    o_ref[0], stats_ref[0] = attend(raw, joined(k_refs, 1), None)


def forward_kernel(video_rows, *refs):
    gathered_ref, k_refs, audio_q, length_ref = refs[0], (refs[1:5], refs[5:9]), refs[9:13], refs[13]
    gate_rows = head_row(refs[14]), head_row(refs[15])
    o_video_ref, stats_video_ref, o_ref, stats_ref, ordered_ref = refs[16:21]
    for place in range(SIDE):
        ordered_ref[(lax.axis_index("vid") >> 2) ^ place] = audio_q[place][...]
    audio_rows = (ordered_ref.shape[1] - video_rows) // 2
    up_video, up_audio = upstreams_of(ordered_ref, audio_rows)
    raw = scores(joined(k_refs[VIDEO], 0), flat(ordered_ref[:, :audio_rows]), VIDEO, None)
    output, stats = attend(raw, joined(k_refs[VIDEO], 1), gated(up_audio, gate_rows[AUDIO]))
    o_ref[0, VIDEO] = jnp.concatenate([o_video_ref[0], output], axis=1)
    delta = row_delta(up_video, o_video_ref[0].astype(F32))
    stats_video = jnp.concatenate([stats_video_ref[0, 0:1], delta], axis=0)
    stats_video = jnp.concatenate([stats_video, stats], axis=1)
    raw = scores(joined(k_refs[AUDIO], 0), queries_of(gathered_ref, ordered_ref, audio_rows), AUDIO, length_ref)
    up = upstream(ordered_ref, gate_rows, audio_rows, AUDIO)
    o_ref[0, AUDIO], stats = attend(raw, joined(k_refs[AUDIO], 1), up)
    stats_ref[0] = jnp.concatenate([stats_video, stats], axis=0)


def merged_stats(refs, part):
    logs = [ref[0, 2 * part : 2 * part + 1] for ref in refs]
    peak = functools.reduce(jnp.maximum, logs)
    weights = [jnp.exp(local - peak) for local in logs]
    total = sum(weights)
    scale = 1.0 / total
    delta = sum(weight * ref[0, 2 * part + 1 : 2 * part + 2] for weight, ref in zip(weights, refs)) * scale
    return peak + jnp.log(total), delta, weights[0] * scale


def backward_keys(part, queries, up, stats_refs, k_refs, length_ref, k_outs, first):
    log_total, delta, factor = merged_stats(stats_refs, part)
    raw = scores(joined(k_refs, 0), queries, part, length_ref)
    probs = jnp.exp2(raw * (SCALE * LOG2_E) - log_total * LOG2_E)
    grad_values = nn(probs.astype(BF16), up).astype(BF16)
    grad_probs = nt(joined(k_refs, 1), up)
    grad_scores = (probs * (grad_probs - delta)).astype(BF16)
    grad_keys = (nn(grad_scores, queries) * SCALE).astype(BF16)
    rows = k_refs[0].shape[1]
    for place in range(SIDE):
        k_outs[place][0, first : first + rows] = grad_keys[place * rows : (place + 1) * rows]
        k_outs[place][1, first : first + rows] = grad_values[place * rows : (place + 1) * rows]
    return nn(joined(k_refs, 0).T, grad_scores), factor


def column_of(row):
    return jnp.broadcast_to(row, (HEAD_DIM, HEAD_DIM)).T[:, 0:1]


def backward_kernel(video_rows, *refs):
    gathered_ref, audio_q, k_video, k_audio, stats_refs = refs[0], refs[1], refs[2:6], refs[6:10], refs[10:14]
    gate_rows, length_ref, o_ref = (head_row(refs[14]), head_row(refs[15])), refs[16], refs[17]
    k_outs, q_out = refs[18:22], refs[22]
    audio_rows = (audio_q.shape[1] - video_rows) // 2
    rows = video_rows + audio_rows
    video = SIDE * video_rows
    queries = queries_of(gathered_ref, audio_q, audio_rows)
    up = upstream(audio_q, gate_rows, audio_rows, VIDEO)
    term_video, factor = backward_keys(VIDEO, queries, up, stats_refs, k_video, length_ref, k_outs, 0)
    on_video = o_ref[0, VIDEO].astype(F32) * factor
    up = upstream(audio_q, gate_rows, audio_rows, AUDIO)
    term_audio, factor = backward_keys(AUDIO, queries, up, stats_refs, k_audio, length_ref, k_outs, video_rows)
    on_audio = o_ref[0, AUDIO].astype(F32) * factor
    grad_queries = term_video + term_audio
    cross_video, cross_audio = on_audio[:, :video], on_video[:, video:]
    merged = jnp.concatenate(
        [
            on_video[:, :video] + column_of(gate_rows[VIDEO]) * cross_video,
            on_audio[:, video:] + column_of(gate_rows[AUDIO]) * cross_audio,
        ],
        axis=1,
    )
    up_video, up_audio = upstreams_of(audio_q, audio_rows)
    video_sum = jnp.sum(up_video.T.astype(F32) * cross_video, axis=1, keepdims=True)
    audio_sum = jnp.sum(up_audio.T.astype(F32) * cross_audio, axis=1, keepdims=True)
    sums = jnp.concatenate(
        [jnp.broadcast_to(video_sum, (HEAD_DIM, 4)), jnp.broadcast_to(audio_sum, (HEAD_DIM, HEAD_DIM - 4))], axis=1
    ).T[0:GATE_ROWS]
    high = sums.astype(BF16)
    low = (sums - high.astype(F32)).astype(BF16)
    even = lax.broadcasted_iota(jnp.int32, sums.shape, 0) % 2 == 0
    sums = jnp.where(even, high.astype(F32), low.astype(F32)).astype(BF16)
    merged = merged.astype(BF16).T
    grad_queries = (grad_queries * SCALE).astype(BF16).T
    for index, array in ((0, merged), (1, grad_queries)):
        first = index * rows
        q_out[:, first : first + video_rows] = array[:video].reshape(SIDE, video_rows, HEAD_DIM)
        q_out[:, first + video_rows : first + rows] = array[video:].reshape(SIDE, audio_rows, HEAD_DIM)
    q_out[:, 2 * rows :] = jnp.broadcast_to(sums, (SIDE, *sums.shape))


def chunk_spec(array):
    shape = array.shape[:-1]
    return pl.BlockSpec((*shape, HEAD_DIM), lambda h: (0,) * len(shape) + (h,))


def head_spec(array):
    shape = array.shape[1:]
    return pl.BlockSpec((1, *shape), lambda h: (h,) + (0,) * len(shape))


def like(*shape, kind=BF16):
    return jax.ShapeDtypeStruct(shape, kind)


def cost(keys, queries, heads, products):
    return pl.CostEstimate(
        flops=2 * products * heads * keys * queries * HEAD_DIM,
        bytes_accessed=4 * heads * keys * queries,
        transcendentals=heads * keys * queries,
    )


def attention_forward_video(queries, video_keys, video_rows):
    heads = queries.shape[2] // HEAD_DIM
    video = SIDE * video_rows
    outs = [like(heads, HEAD_DIM, video), like(heads, 2, video, kind=F32)]
    chunks = [queries, *video_keys]
    return pl.pallas_call(
        forward_video_kernel,
        grid=(heads,),
        in_specs=[chunk_spec(array) for array in chunks],
        out_specs=[head_spec(array) for array in outs],
        out_shape=outs,
        cost_estimate=cost(video, video, heads, 2),
        compiler_params=pltpu.CompilerParams(vmem_limit_bytes=VMEM),
        name="forward_video",
    )(*chunks)


def attention_forward(queries, audio_q, video_keys, audio_keys, audio_len, gates, earlier, video_rows):
    audio_rows, width = audio_keys[0].shape[1:]
    heads = width // HEAD_DIM
    total = SIDE * (video_rows + audio_rows)
    outs = [like(heads, 2, HEAD_DIM, total), like(heads, 4, total, kind=F32)]
    ordered = like(SIDE, *audio_q[0].shape)
    chunks = [queries, *video_keys, *audio_keys, *audio_q]
    return pl.pallas_call(
        functools.partial(forward_kernel, video_rows),
        grid=(heads,),
        in_specs=[chunk_spec(array) for array in chunks]
        + [pl.BlockSpec(memory_space=pltpu.SMEM)]
        + [pl.BlockSpec(gate.shape, lambda h: (0,)) for gate in gates]
        + [head_spec(array) for array in earlier],
        out_specs=[head_spec(array) for array in outs] + [chunk_spec(ordered)],
        out_shape=[*outs, ordered],
        cost_estimate=cost(total, total, heads, 1),
        compiler_params=pltpu.CompilerParams(vmem_limit_bytes=VMEM),
        name="forward",
    )(*chunks, audio_len, *gates, *earlier)


def attention_backward(queries, audio_q, video_keys, audio_keys, stats, gates, audio_len, outputs, video_rows):
    width = queries.shape[2]
    heads = width // HEAD_DIM
    rows = video_rows + audio_keys[0].shape[1]
    outs = [like(2, rows, width)] * SIDE + [like(SIDE, 2 * rows + GATE_ROWS, width)]
    chunks = [queries, audio_q, *video_keys, *audio_keys]
    *key_parts, query_parts = pl.pallas_call(
        functools.partial(backward_kernel, video_rows),
        grid=(heads,),
        in_specs=[chunk_spec(array) for array in chunks]
        + [head_spec(array) for array in stats]
        + [pl.BlockSpec(gate.shape, lambda h: (0,)) for gate in gates]
        + [pl.BlockSpec(memory_space=pltpu.SMEM), head_spec(outputs)],
        out_specs=[chunk_spec(array) for array in outs],
        out_shape=outs,
        cost_estimate=cost(SIDE * rows, SIDE * rows, heads, 4),
        compiler_params=pltpu.CompilerParams(vmem_limit_bytes=VMEM),
        name="backward",
    )(*chunks, *stats, *gates, audio_len, outputs)
    return key_parts, query_parts


def total_of(refs, *index):
    return sum(ref[index].astype(F32) for ref in refs)


def finish_queries_kernel(parts_ref, video_out, audio_out, video_q, audio_q, gate_ref):
    video_rows, audio_rows = video_out.shape[1], audio_out.shape[1]
    rows = video_rows + audio_rows
    parts = [parts_ref.at[place] for place in range(SIDE)]
    for index, video, audio in ((0, video_out, audio_out), (1, video_q, audio_q)):
        first = index * rows
        video[0] = total_of(parts, slice(first, first + video_rows)).astype(BF16)
        audio[0] = total_of(parts, slice(first + video_rows, first + rows)).astype(BF16)
    gates = total_of(parts, slice(2 * rows, None))
    width = gates.shape[1]
    video_gate = jnp.broadcast_to(gates[0:1] + gates[1:2], (4, width))
    audio_gate = jnp.broadcast_to(gates[4:5] + gates[5:6], (4, width))
    gate_ref[...] = jnp.concatenate([video_gate, audio_gate], axis=0)


def finish_queries(parts, video_rows, audio_rows):
    width = parts.shape[2]
    video, audio = like(1, video_rows, width), like(1, audio_rows, width)
    return pl.pallas_call(
        finish_queries_kernel,
        out_shape=[video, audio, video, audio, like(8, width, kind=F32)],
        compiler_params=pltpu.CompilerParams(vmem_limit_bytes=8 * 2**20),
        name="finish_queries",
    )(parts)


def finish_keys_kernel(*refs):
    parts, (video_k, video_v, audio_k, audio_v) = refs[:SIDE], refs[SIDE:]
    rows = video_k.shape[1]
    for index, video, audio in ((0, video_k, audio_k), (1, video_v, audio_v)):
        video[0] = total_of(parts, index, slice(0, rows)).astype(BF16)
        audio[0] = total_of(parts, index, slice(rows, None)).astype(BF16)


def finish_keys(parts, video_rows, audio_rows):
    width = parts[0].shape[2]
    video, audio = like(1, video_rows, width), like(1, audio_rows, width)
    return pl.pallas_call(
        finish_keys_kernel,
        out_shape=[video, video, audio, audio],
        compiler_params=pltpu.CompilerParams(vmem_limit_bytes=8 * 2**20),
        name="finish_keys",
    )(*parts)


def own_audio(array):
    vid_size, aud_size = lax.axis_size("vid"), lax.axis_size("aud")
    pairs = []
    for vid in range(vid_size):
        for aud in range(aud_size):
            to_vid, to_aud = audio_target(vid, aud)
            pairs.append((vid * aud_size + aud, to_vid * aud_size + to_aud))
    return lax.ppermute(array, ("vid", "aud"), pairs)


def fenced(holds, function, *arrays):
    outs = jax.eval_shape(function, *arrays)
    return lax.cond(
        holds, function, lambda *_: jax.tree.map(lambda out: jnp.zeros(out.shape, out.dtype), outs), *arrays
    )


def shards(
    video_q, video_k, video_v, audio_q, audio_k, audio_v, video_gate, audio_gate, audio_len, d_video_out, d_audio_out
):
    vid = lax.axis_index("vid")
    video_rows, audio_rows = video_q.shape[1], d_audio_out.shape[1]
    holds = audio_len[0] > 0
    send_audio, video_kv, queries = prepare(
        audio_rows, audio_q, audio_k, audio_v, video_q, video_k, video_v
    )
    gates = video_gate, audio_gate

    def first_chunks(send_audio, video_kv, queries):
        return own_audio(send_audio), tuple(gathered(video_kv, along_z)[1:]), all_along_x(queries)

    audio, video_keys, queries = fenced(holds, first_chunks, send_audio, video_kv, queries)
    video_keys = [video_kv, *video_keys]
    audio_queries, audio_keys = split_audio(audio, d_audio_out, d_video_out)
    audio_keys = gathered(audio_keys, along_z)
    audio_queries = gathered(audio_queries, along_x)
    earlier = attention_forward_video(queries, video_keys, video_rows)
    outputs, stats, audio_queries = attention_forward(
        queries, audio_queries, video_keys, audio_keys, audio_len, gates, earlier, video_rows
    )
    key_parts, query_parts = attention_backward(
        queries, audio_queries, video_keys, audio_keys, gathered(stats, along_x), gates, audio_len, outputs, video_rows
    )

    def query_results(parts):
        parts = lax.all_to_all(parts, "vid", 0, 0, axis_index_groups=ALONG_X, tiled=True)
        return tuple(finish_queries(parts, video_rows, audio_rows))

    video_out, audio_out, grad_video_q, grad_audio_q, gate = fenced(holds, query_results, query_parts)
    key_parts = returned(key_parts, along_z)
    gate, key_parts[1] = lax.optimization_barrier((gate, key_parts[1]))
    gate = sum(gathered(gate, along_z))
    other = lax.ppermute(gate, "pair", [(0, 1), (1, 0)])
    key_grads = finish_keys(key_parts, video_rows, audio_rows)
    other, (grad_video_k, grad_video_v, grad_audio_k, grad_audio_v) = lax.optimization_barrier((other, key_grads))
    gate = gate + other
    return (
        video_out,
        audio_out,
        grad_video_q,
        grad_video_k,
        grad_video_v,
        grad_audio_q,
        grad_audio_k,
        grad_audio_v,
        gate[0],
        gate[7],
    )


def solution(mesh):
    split = P("pair", "vid", "aud")
    rows = P("pair", "aud", None)
    return jax.shard_map(
        shards,
        mesh=mesh,
        in_specs=(split, split, split, rows, rows, rows, P("aud"), P("aud"), P("pair"), split, split),
        out_specs=(split,) * 8 + (P("aud"), P("aud")),
        check_vma=False,
    )
```

```python
import functools

import jax
import jax.numpy as jnp
from jax import lax
from jax.experimental import pallas as pl
from jax.experimental.pallas import tpu as pltpu
from jax.sharding import PartitionSpec as P

HEAD_DIM = 128
SCALE = HEAD_DIM ** (-0.5)
SIDE = 4
F32 = jnp.float32
BF16 = jnp.bfloat16
VIDEO, AUDIO = 0, 1
GATE_ROWS = 16
VMEM = 60 * 2**20
LOG2_E = 1.4426950408889634

ALONG_X = [[x * SIDE + z for x in range(SIDE)] for z in range(SIDE)]


def along_x(array, distance):
    pairs = [(x * SIDE + z, (x ^ distance) * SIDE + z) for x in range(SIDE) for z in range(SIDE)]
    return lax.ppermute(array, "vid", pairs)


def along_z(array, distance):
    pairs = [(x * SIDE + z, x * SIDE + (z ^ distance)) for x in range(SIDE) for z in range(SIDE)]
    return lax.ppermute(array, "vid", pairs)


def all_along_x(array):
    return lax.all_gather(array, "vid", axis=0, axis_index_groups=ALONG_X)


def gathered(array, along):
    return [array] + [along(array, distance) for distance in range(1, SIDE)]


def returned(parts, along):
    return [parts[0]] + [along(parts[place], place) for place in range(1, SIDE)]


def nt(a, b):
    return lax.dot_general(a, b, (((1,), (1,)), ((), ())), preferred_element_type=F32)


def nn(a, b):
    return lax.dot_general(a, b, (((1,), (0,)), ((), ())), preferred_element_type=F32)


def joined(refs, index):
    return jnp.concatenate([ref[index] for ref in refs], axis=0)


def gated(rows, gate_row):
    return (gate_row * rows.astype(F32)).astype(BF16)


def flat(block):
    return block.reshape(-1, block.shape[-1])


def queries_of(gathered_ref, audio_ref, video_rows):
    return jnp.concatenate([flat(gathered_ref[:, :video_rows]), flat(audio_ref[:, 0])], axis=0)


def upstreams_of(gathered_ref, audio_ref, video_rows):
    return flat(gathered_ref[:, video_rows:]), flat(audio_ref[:, 1])


def head_row(ref):
    first = pl.multiple_of(pl.program_id(0) * HEAD_DIM, HEAD_DIM)
    return ref[pl.ds(first, HEAD_DIM)].reshape(1, HEAD_DIM)


def upstream(gathered_ref, audio_ref, gate_rows, video_rows, part):
    video, audio = upstreams_of(gathered_ref, audio_ref, video_rows)
    if part == VIDEO:
        audio = gated(audio, gate_rows[AUDIO])
    else:
        video = gated(video, gate_rows[VIDEO])
    return jnp.concatenate([video, audio], axis=0)


def split_audio_kernel(audio_ref, up_ref, queries_ref, keys_ref):
    queries_ref[0] = audio_ref[0]
    queries_ref[1] = up_ref[0]
    keys_ref[0] = audio_ref[1]
    keys_ref[1] = audio_ref[2]


def split_audio(audio, d_audio):
    _, rows, width = audio.shape
    return pl.pallas_call(
        split_audio_kernel,
        out_shape=[like(2, rows, width)] * 2,
        compiler_params=pltpu.CompilerParams(vmem_limit_bytes=8 * 2**20),
        name="split_audio",
    )(audio, d_audio)


def audio_target(vid, aud):
    x, z, y, half = vid >> 2, vid & 3, aud >> 1, aud & 1
    offset = (x - y) & 3
    to_y = (y - offset + 2 * (1 - (offset & 1))) & 3
    return SIDE * y + 2 * half + (z & 1), 2 * to_y + (z >> 1)


def prepare_kernel(aq_ref, ak_ref, av_ref, vq_ref, vk_ref, vv_ref, dv_ref, audio, video_kv, queries, sems):
    to_vid, to_aud = audio_target(lax.axis_index("vid"), lax.axis_index("aud"))
    rows, width = vq_ref.shape[1:]
    audio_rows = audio.shape[1]
    taken = pl.ds(pl.multiple_of((to_vid & 1) * audio_rows, audio_rows), audio_rows)
    columns = pl.ds(pl.multiple_of(to_aud * width, HEAD_DIM), width)
    pairs = [(ref.at[0, taken, columns], audio.at[index]) for index, ref in enumerate((aq_ref, ak_ref, av_ref))]
    pairs += [(vk_ref.at[0], video_kv.at[0]), (vv_ref.at[0], video_kv.at[1])]
    pairs += [(vq_ref.at[0], queries.at[pl.ds(0, rows)]), (dv_ref.at[0], queries.at[pl.ds(rows, rows)])]
    copies = [pltpu.make_async_copy(source, target, sems.at[index]) for index, (source, target) in enumerate(pairs)]
    for copy in copies:
        copy.start()
    for copy in copies:
        copy.wait()


def prepare(audio_rows, *given):
    _, video_rows, width = given[3].shape
    outs = [like(3, audio_rows, width), like(2, video_rows, width), like(2 * video_rows, width)]
    return pl.pallas_call(
        prepare_kernel,
        in_specs=[pl.BlockSpec(memory_space=pl.ANY)] * 7,
        out_specs=[pl.BlockSpec(memory_space=pltpu.VMEM)] * 3,
        out_shape=outs,
        scratch_shapes=[pltpu.SemaphoreType.DMA((7,))],
        compiler_params=pltpu.CompilerParams(vmem_limit_bytes=VMEM),
        name="prepare",
    )(*given)


def scores(keys, queries, part, length_ref):
    raw = nt(keys, queries)
    if part == AUDIO:
        rows = raw.shape[0] // SIDE
        position = lax.broadcasted_iota(jnp.int32, (rows, raw.shape[1]), 0)
        pieces = [raw[place * rows : (place + 1) * rows] for place in range(SIDE)]
        vid = lax.axis_index("vid")
        for place in range(SIDE):
            chunk = (vid & ~(SIDE - 1)) + ((vid & (SIDE - 1)) ^ place)
            pieces[place] = jnp.where(position < length_ref[0] - chunk * rows, pieces[place], -1e30)
        raw = jnp.concatenate(pieces, axis=0)
    return raw


def attend(raw, values, up):
    peak = jnp.max(raw, axis=0, keepdims=True)
    expon = jnp.exp2((raw - peak) * (SCALE * LOG2_E))
    total = jnp.sum(expon, axis=0, keepdims=True)
    output = nn(values.T, expon.astype(BF16)) * (1.0 / total)
    delta = jnp.sum(up.T.astype(F32) * output, axis=0, keepdims=True)
    return output.astype(BF16), jnp.concatenate([peak * SCALE + jnp.log(total), delta], axis=0)


def forward_video_kernel(video_rows, *refs):
    gathered_ref, k_refs, o_ref, stats_ref = refs[0], refs[1:5], refs[5], refs[6]
    raw = scores(joined(k_refs, 0), flat(gathered_ref[:, :video_rows]), VIDEO, None)
    o_ref[0], stats_ref[0] = attend(raw, joined(k_refs, 1), flat(gathered_ref[:, video_rows:]))


def forward_kernel(video_rows, *refs):
    gathered_ref, k_refs, audio_q, length_ref = refs[0], (refs[1:5], refs[5:9]), refs[9:13], refs[13]
    gate_rows = head_row(refs[14]), head_row(refs[15])
    o_video_ref, stats_video_ref, o_ref, stats_ref, ordered_ref = refs[16:21]
    for place in range(SIDE):
        ordered_ref[(lax.axis_index("vid") >> 2) ^ place] = audio_q[place][...]
    up_audio = gated(flat(ordered_ref[:, 1]), gate_rows[AUDIO])
    raw = scores(joined(k_refs[VIDEO], 0), flat(ordered_ref[:, 0]), VIDEO, None)
    output, stats = attend(raw, joined(k_refs[VIDEO], 1), up_audio)
    o_ref[0, VIDEO] = jnp.concatenate([o_video_ref[0], output], axis=1)
    stats_video = jnp.concatenate([stats_video_ref[0], stats], axis=1)
    raw = scores(joined(k_refs[AUDIO], 0), queries_of(gathered_ref, ordered_ref, video_rows), AUDIO, length_ref)
    up = upstream(gathered_ref, ordered_ref, gate_rows, video_rows, AUDIO)
    o_ref[0, AUDIO], stats = attend(raw, joined(k_refs[AUDIO], 1), up)
    stats_ref[0] = jnp.concatenate([stats_video, stats], axis=0)


def merged_stats(refs, part):
    logs = [ref[0, 2 * part : 2 * part + 1] for ref in refs]
    peak = functools.reduce(jnp.maximum, logs)
    weights = [jnp.exp(local - peak) for local in logs]
    total = sum(weights)
    scale = 1.0 / total
    delta = sum(weight * ref[0, 2 * part + 1 : 2 * part + 2] for weight, ref in zip(weights, refs)) * scale
    return peak + jnp.log(total), delta, weights[0] * scale


def backward_keys(part, queries, up, stats_refs, k_refs, length_ref, k_outs, first):
    log_total, delta, factor = merged_stats(stats_refs, part)
    raw = scores(joined(k_refs, 0), queries, part, length_ref)
    probs = jnp.exp2(raw * (SCALE * LOG2_E) - log_total * LOG2_E)
    grad_values = nn(probs.astype(BF16), up).astype(BF16)
    grad_probs = nt(joined(k_refs, 1), up)
    grad_scores = (probs * (grad_probs - delta)).astype(BF16)
    grad_keys = (nn(grad_scores, queries) * SCALE).astype(BF16)
    rows = k_refs[0].shape[1]
    for place in range(SIDE):
        k_outs[place][0, first : first + rows] = grad_keys[place * rows : (place + 1) * rows]
        k_outs[place][1, first : first + rows] = grad_values[place * rows : (place + 1) * rows]
    return nn(joined(k_refs, 0).T, grad_scores), factor


def column_of(row):
    return jnp.broadcast_to(row, (HEAD_DIM, HEAD_DIM)).T[:, 0:1]


def backward_kernel(video_rows, *refs):
    gathered_ref, audio_q, k_video, k_audio, stats_refs = refs[0], refs[1], refs[2:6], refs[6:10], refs[10:14]
    gate_rows, length_ref, o_ref = (head_row(refs[14]), head_row(refs[15])), refs[16], refs[17]
    k_outs, q_out = refs[18:22], refs[22]
    audio_rows = audio_q.shape[2]
    rows = video_rows + audio_rows
    video = SIDE * video_rows
    queries = queries_of(gathered_ref, audio_q, video_rows)
    up = upstream(gathered_ref, audio_q, gate_rows, video_rows, VIDEO)
    term_video, factor = backward_keys(VIDEO, queries, up, stats_refs, k_video, length_ref, k_outs, 0)
    on_video = o_ref[0, VIDEO].astype(F32) * factor
    up = upstream(gathered_ref, audio_q, gate_rows, video_rows, AUDIO)
    term_audio, factor = backward_keys(AUDIO, queries, up, stats_refs, k_audio, length_ref, k_outs, video_rows)
    on_audio = o_ref[0, AUDIO].astype(F32) * factor
    grad_queries = term_video + term_audio
    cross_video, cross_audio = on_audio[:, :video], on_video[:, video:]
    merged = jnp.concatenate(
        [
            on_video[:, :video] + column_of(gate_rows[VIDEO]) * cross_video,
            on_audio[:, video:] + column_of(gate_rows[AUDIO]) * cross_audio,
        ],
        axis=1,
    )
    up_video, up_audio = upstreams_of(gathered_ref, audio_q, video_rows)
    video_sum = jnp.sum(up_video.T.astype(F32) * cross_video, axis=1, keepdims=True)
    audio_sum = jnp.sum(up_audio.T.astype(F32) * cross_audio, axis=1, keepdims=True)
    sums = jnp.concatenate(
        [jnp.broadcast_to(video_sum, (HEAD_DIM, 4)), jnp.broadcast_to(audio_sum, (HEAD_DIM, HEAD_DIM - 4))], axis=1
    ).T[0:GATE_ROWS]
    high = sums.astype(BF16)
    low = (sums - high.astype(F32)).astype(BF16)
    even = lax.broadcasted_iota(jnp.int32, sums.shape, 0) % 2 == 0
    sums = jnp.where(even, high.astype(F32), low.astype(F32)).astype(BF16)
    merged = merged.astype(BF16).T
    grad_queries = (grad_queries * SCALE).astype(BF16).T
    for index, array in ((0, merged), (1, grad_queries)):
        first = index * rows
        q_out[:, first : first + video_rows] = array[:video].reshape(SIDE, video_rows, HEAD_DIM)
        q_out[:, first + video_rows : first + rows] = array[video:].reshape(SIDE, audio_rows, HEAD_DIM)
    q_out[:, 2 * rows :] = jnp.broadcast_to(sums, (SIDE, *sums.shape))


def chunk_spec(array):
    shape = array.shape[:-1]
    return pl.BlockSpec((*shape, HEAD_DIM), lambda h: (0,) * len(shape) + (h,))


def head_spec(array):
    shape = array.shape[1:]
    return pl.BlockSpec((1, *shape), lambda h: (h,) + (0,) * len(shape))


def like(*shape, kind=BF16):
    return jax.ShapeDtypeStruct(shape, kind)


def cost(keys, queries, heads, products):
    return pl.CostEstimate(
        flops=2 * products * heads * keys * queries * HEAD_DIM,
        bytes_accessed=4 * heads * keys * queries,
        transcendentals=heads * keys * queries,
    )


def attention_forward_video(queries, video_keys, video_rows):
    heads = queries.shape[2] // HEAD_DIM
    video = SIDE * video_rows
    outs = [like(heads, HEAD_DIM, video), like(heads, 2, video, kind=F32)]
    chunks = [queries, *video_keys]
    return pl.pallas_call(
        functools.partial(forward_video_kernel, video_rows),
        grid=(heads,),
        in_specs=[chunk_spec(array) for array in chunks],
        out_specs=[head_spec(array) for array in outs],
        out_shape=outs,
        cost_estimate=cost(video, video, heads, 2),
        compiler_params=pltpu.CompilerParams(vmem_limit_bytes=VMEM),
        name="forward_video",
    )(*chunks)


def attention_forward(queries, audio_q, video_keys, audio_keys, audio_len, gates, earlier, video_rows):
    _, audio_rows, width = audio_q[0].shape
    heads = width // HEAD_DIM
    total = SIDE * (video_rows + audio_rows)
    outs = [like(heads, 2, HEAD_DIM, total), like(heads, 4, total, kind=F32)]
    ordered = like(SIDE, 2, audio_rows, width)
    chunks = [queries, *video_keys, *audio_keys, *audio_q]
    return pl.pallas_call(
        functools.partial(forward_kernel, video_rows),
        grid=(heads,),
        in_specs=[chunk_spec(array) for array in chunks]
        + [pl.BlockSpec(memory_space=pltpu.SMEM)]
        + [pl.BlockSpec(gate.shape, lambda h: (0,)) for gate in gates]
        + [head_spec(array) for array in earlier],
        out_specs=[head_spec(array) for array in outs] + [chunk_spec(ordered)],
        out_shape=[*outs, ordered],
        cost_estimate=cost(total, total, heads, 1),
        compiler_params=pltpu.CompilerParams(vmem_limit_bytes=VMEM),
        name="forward",
    )(*chunks, audio_len, *gates, *earlier)


def attention_backward(queries, audio_q, video_keys, audio_keys, stats, gates, audio_len, outputs, video_rows):
    width = queries.shape[2]
    heads = width // HEAD_DIM
    rows = video_rows + audio_q.shape[2]
    outs = [like(2, rows, width)] * SIDE + [like(SIDE, 2 * rows + GATE_ROWS, width)]
    chunks = [queries, audio_q, *video_keys, *audio_keys]
    *key_parts, query_parts = pl.pallas_call(
        functools.partial(backward_kernel, video_rows),
        grid=(heads,),
        in_specs=[chunk_spec(array) for array in chunks]
        + [head_spec(array) for array in stats]
        + [pl.BlockSpec(gate.shape, lambda h: (0,)) for gate in gates]
        + [pl.BlockSpec(memory_space=pltpu.SMEM), head_spec(outputs)],
        out_specs=[chunk_spec(array) for array in outs],
        out_shape=outs,
        cost_estimate=cost(SIDE * rows, SIDE * rows, heads, 4),
        compiler_params=pltpu.CompilerParams(vmem_limit_bytes=VMEM),
        name="backward",
    )(*chunks, *stats, *gates, audio_len, outputs)
    return key_parts, query_parts


def total_of(refs, *index):
    return sum(ref[index].astype(F32) for ref in refs)


def finish_queries_kernel(parts_ref, video_out, audio_out, video_q, audio_q):
    video_rows, audio_rows = video_out.shape[1], audio_out.shape[1]
    rows = video_rows + audio_rows
    parts = [parts_ref.at[place] for place in range(SIDE)]
    for index, video, audio in ((0, video_out, audio_out), (1, video_q, audio_q)):
        first = index * rows
        video[0] = total_of(parts, slice(first, first + video_rows)).astype(BF16)
        audio[0] = total_of(parts, slice(first + video_rows, first + rows)).astype(BF16)


def gate_sums_kernel(parts_ref, gate_ref):
    gates = jnp.sum(parts_ref[...].astype(F32), axis=0)
    video_gate = jnp.broadcast_to(gates[0:1] + gates[1:2], (4, gates.shape[1]))
    audio_gate = jnp.broadcast_to(gates[4:5] + gates[5:6], (4, gates.shape[1]))
    gate_ref[...] = jnp.concatenate([video_gate, audio_gate], axis=0)


def gate_sums(parts):
    count, rows, width = parts.shape
    return pl.pallas_call(
        gate_sums_kernel,
        grid=(1,),
        in_specs=[pl.BlockSpec((count, GATE_ROWS, width), lambda i: (0, rows // GATE_ROWS - 1, 0))],
        out_specs=pl.BlockSpec((8, width), lambda i: (0, 0)),
        out_shape=like(8, width, kind=F32),
        compiler_params=pltpu.CompilerParams(vmem_limit_bytes=8 * 2**20),
        name="gate_sums",
    )(parts)


def finish_queries(parts, video_rows, audio_rows):
    width = parts.shape[2]
    video, audio = like(1, video_rows, width), like(1, audio_rows, width)
    return pl.pallas_call(
        finish_queries_kernel,
        out_shape=[video, audio, video, audio],
        compiler_params=pltpu.CompilerParams(vmem_limit_bytes=8 * 2**20),
        name="finish_queries",
    )(parts)


def finish_keys_kernel(*refs):
    parts, (video_k, video_v, audio_k, audio_v) = refs[:SIDE], refs[SIDE:]
    rows = video_k.shape[1]
    for index, video, audio in ((0, video_k, audio_k), (1, video_v, audio_v)):
        video[0] = total_of(parts, index, slice(0, rows)).astype(BF16)
        audio[0] = total_of(parts, index, slice(rows, None)).astype(BF16)


def finish_keys(parts, video_rows, audio_rows):
    width = parts[0].shape[2]
    video, audio = like(1, video_rows, width), like(1, audio_rows, width)
    return pl.pallas_call(
        finish_keys_kernel,
        out_shape=[video, video, audio, audio],
        compiler_params=pltpu.CompilerParams(vmem_limit_bytes=8 * 2**20),
        name="finish_keys",
    )(*parts)


def own_audio(array):
    vid_size, aud_size = lax.axis_size("vid"), lax.axis_size("aud")
    pairs = []
    for vid in range(vid_size):
        for aud in range(aud_size):
            to_vid, to_aud = audio_target(vid, aud)
            pairs.append((vid * aud_size + aud, to_vid * aud_size + to_aud))
    return lax.ppermute(array, ("vid", "aud"), pairs)


def fenced(holds, function, *arrays):
    outs = jax.eval_shape(function, *arrays)
    return lax.cond(
        holds, function, lambda *_: jax.tree.map(lambda out: jnp.zeros(out.shape, out.dtype), outs), *arrays
    )


def shards(
    video_q, video_k, video_v, audio_q, audio_k, audio_v, video_gate, audio_gate, audio_len, d_video_out, d_audio_out
):
    vid = lax.axis_index("vid")
    video_rows, audio_rows = video_q.shape[1], d_audio_out.shape[1]
    holds = audio_len[0] > 0
    send_audio, video_kv, queries = prepare(
        audio_rows, audio_q, audio_k, audio_v, video_q, video_k, video_v, d_video_out
    )
    gates = video_gate, audio_gate

    def first_chunks(send_audio, video_kv, queries):
        return own_audio(send_audio), tuple(gathered(video_kv, along_z)[1:]), all_along_x(queries)

    audio, video_keys, queries = fenced(holds, first_chunks, send_audio, video_kv, queries)
    video_keys = [video_kv, *video_keys]
    audio_queries, audio_keys = split_audio(audio, d_audio_out)
    audio_keys = gathered(audio_keys, along_z)
    audio_queries = gathered(audio_queries, along_x)
    earlier = attention_forward_video(queries, video_keys, video_rows)
    outputs, stats, audio_queries = attention_forward(
        queries, audio_queries, video_keys, audio_keys, audio_len, gates, earlier, video_rows
    )
    key_parts, query_parts = attention_backward(
        queries, audio_queries, video_keys, audio_keys, gathered(stats, along_x), gates, audio_len, outputs, video_rows
    )

    def exchanged(parts):
        return lax.all_to_all(parts, "vid", 0, 0, axis_index_groups=ALONG_X, tiled=True)

    query_parts = fenced(holds, exchanged, query_parts)
    gate = gate_sums(query_parts)
    video_out, audio_out, grad_video_q, grad_audio_q = finish_queries(query_parts, video_rows, audio_rows)
    key_parts = returned(key_parts, along_z)
    gate, key_parts[1] = lax.optimization_barrier((gate, key_parts[1]))
    gate = sum(gathered(gate, along_z))
    other = lax.ppermute(gate, "pair", [(0, 1), (1, 0)])
    key_grads = finish_keys(key_parts, video_rows, audio_rows)
    other, (grad_video_k, grad_video_v, grad_audio_k, grad_audio_v) = lax.optimization_barrier((other, key_grads))
    gate = gate + other
    return (
        video_out,
        audio_out,
        grad_video_q,
        grad_video_k,
        grad_video_v,
        grad_audio_q,
        grad_audio_k,
        grad_audio_v,
        gate[0],
        gate[7],
    )


def solution(mesh):
    split = P("pair", "vid", "aud")
    rows = P("pair", "aud", None)
    return jax.shard_map(
        shards,
        mesh=mesh,
        in_specs=(split, split, split, rows, rows, rows, P("aud"), P("aud"), P("pair"), split, split),
        out_specs=(split,) * 8 + (P("aud"), P("aud")),
        check_vma=False,
    )
```
